128 devices in a mesh: section: 2 (over z_lo), rep: 2 (over z_hi), shard: 32 (over y, x, core).
Axes of the slice: x: 4, y: 4, z: 4 (z_hi: 2, z_lo: 2; z = z_hi * 2 + z_lo), core: 2. Of those that a mesh axis runs over, the one named last changes fastest.
Arguments:
- inputs: bfloat16 [2, 2, 4096, 1024], P(None, 'rep', 'shard'), may hold values from -6 to 6
- segments: int32 [2, 2, 4096], P(None, 'rep', 'shard'), may hold values from 0 to 20, as said below
- cotangent: bfloat16 [2, 2, 4096, 1024], P(None, 'rep', 'shard'), may hold values from -6 to 6
- qkv_weight: bfloat16 [2, 1024, 3072], P('section', 'shard'), may hold values from -0.1875 to 0.1875
- qkv_bias: bfloat16 [2, 3072], P('section', 'shard'), may hold values from -0.29882812 to 0.29882812
- dense_weight: bfloat16 [2, 1024, 1024], P('section', 'shard'), may hold values from -1.5 to 1.5
- dense_bias: bfloat16 [2, 1024], P('section', 'shard'), may hold values from -1.796875 to 1.796875
- fc_in_weight: bfloat16 [2, 1024, 4096], P('section', 'shard'), may hold values from -0.1875 to 0.1875
- fc_in_bias: bfloat16 [2, 4096], P('section', 'shard'), may hold values from -1.796875 to 1.796875
- fc_out_weight: bfloat16 [2, 4096, 1024], P('section', 'shard'), may hold values from -0.09375 to 0.09375
- fc_out_bias: bfloat16 [2, 1024], P('section', 'shard'), may hold values from -1.796875 to 1.796875
- norm1_gain: bfloat16 [2, 1024], P('section', 'shard'), may hold values from 0.5 to 1.5
- norm1_bias: bfloat16 [2, 1024], P('section', 'shard'), may hold values from -1.796875 to 1.796875
- norm2_gain: bfloat16 [2, 1024], P('section', 'shard'), may hold values from 0.5 to 1.5
- norm2_bias: bfloat16 [2, 1024], P('section', 'shard'), may hold values from -1.796875 to 1.796875
Outputs:
- section_outputs: bfloat16 [2, 2, 2, 4096, 1024], P('section', None, 'rep', 'shard')
- input_grads: bfloat16 [2, 2, 2, 4096, 1024], P('section', None, 'rep', 'shard')
- qkv_weight_grad: float32 [2, 1024, 3072], P('section', 'shard')
- qkv_bias_grad: float32 [2, 2048], P('section', 'shard')
- value_bias_grad: float32 [2, 1024], P('section', 'shard')
- dense_weight_grad: float32 [2, 1024, 1024], P('section', 'shard')
- dense_bias_grad: float32 [2, 1024], P('section', 'shard')
- fc_in_weight_grad: float32 [2, 1024, 4096], P('section', 'shard')
- fc_in_bias_grad: float32 [2, 4096], P('section', 'shard')
- fc_out_weight_grad: float32 [2, 4096, 1024], P('section', 'shard')
- fc_out_bias_grad: float32 [2, 1024], P('section', 'shard')
- norm1_gain_grad: float32 [2, 1024], P('section', 'shard')
- norm1_bias_grad: float32 [2, 1024], P('section', 'shard')
- norm2_gain_grad: float32 [2, 1024], P('section', 'shard')
- norm2_bias_grad: float32 [2, 1024], P('section', 'shard')
The draws below stay inside these ranges and needn't reach their ends.
Inputs may be any that keep to these rules, and one draw needn't show every extreme that they name: `segments`: within each sequence the numbers start at 0, never fall and rise by at most one from a token to the next; each run of equal numbers is one document, each but the last of at least 204 tokens.
All inputs are finite; a program needn't handle non-finite values.
Results may differ from the reference program's by a relative error of at most 0.022.
Values may be sent and summed in bfloat16 or wider, within the bound.
No kernel may reach another device: no remote copies, remote signals or barrier semaphores. Data moves between devices by JAX's collectives and lax.ppermute only.
A program may use at most 320 MiB of HBM per device.

```python
import math
import jax
import jax.numpy as jnp
from jax import lax

D = 1024
HEADS = 16
HD = 64
FF = 4096
ROT = 16
MICRO = 2
LENGTH = 4096
DOC_MIN = 204
SEQS = 2
LAYERS = 2


def draw_segments(key, part):
    key = jax.random.fold_in(key, 11)
    shortest = DOC_MIN
    longest = max(shortest + 1, LENGTH // 2)
    doc_count = LENGTH // shortest + 1
    doc_sizes = jax.random.randint(jax.random.fold_in(key, 1), (MICRO, SEQS, doc_count), shortest, longest + 1)
    doc_ends = jnp.cumsum(doc_sizes, axis=-1)
    places = jnp.arange(LENGTH, dtype=jnp.int32)
    ragged = jnp.sum((doc_ends[..., None] <= places).astype(jnp.int32), axis=-2)
    whole_pick = jax.random.randint(jax.random.fold_in(key, 2), (1, SEQS, 1), 0, MICRO)
    even_seq = jax.random.randint(jax.random.fold_in(key, 3), (), 0, SEQS)
    micro_ids = jnp.arange(MICRO, dtype=jnp.int32)[:, None, None]
    seq_ids = jnp.arange(SEQS, dtype=jnp.int32)[None, :, None]
    even = jnp.broadcast_to(places // shortest, ragged.shape)
    mixed = jnp.where(seq_ids == even_seq, even, ragged)
    return jnp.where(micro_ids == whole_pick, jnp.zeros_like(ragged), mixed).astype(jnp.int32)


def levels(stream_key, dims, cuts, least, high):
    def one(axis_at, blocks):
        draws = jax.random.uniform(jax.random.fold_in(jax.random.fold_in(stream_key, 6), axis_at), (blocks,), jnp.float32, least / len(cuts), high / len(cuts))
        return jnp.repeat(jnp.exp(draws), dims[axis_at] // blocks).reshape((-1,) + (1,) * (len(dims) - axis_at - 1))

    gain = one(*cuts[0])
    for cut in cuts[1:]:
        gain = gain * one(*cut)
    return gain


def noise(rng, dims, spread, bound, cuts=(), held_as=jnp.bfloat16):
    result = jax.random.normal(rng, dims, jnp.float32) * spread
    if len(cuts) > 0:
        result = levels(rng, dims, cuts, -0.22, 0.18) * result
    return jnp.clip(result, min=-bound, max=bound).astype(held_as)


def setup_inputs(seed: int = 0) -> dict:
    streams_of = jax.random.split(jax.random.key(seed), 16)
    inputs = noise(streams_of[0], (MICRO, SEQS, LENGTH, D), 1.0, 6.0, ((1, 2), (2, 32)))
    segments = draw_segments(jax.random.fold_in(streams_of[15], 71), 0)
    cotangent = noise(streams_of[2], (MICRO, SEQS, LENGTH, D), 1.0, 6.0, ((1, 2), (2, 32)))
    qkv_weight = noise(streams_of[3], (LAYERS, D, 3 * D), D ** -0.5, 0.1875, ((0, 2), (1, 32)))
    qkv_bias = noise(streams_of[4], (LAYERS, 3 * D), 0.05, 0.29882812, ((0, 2), (1, 32)))
    dense_weight = noise(streams_of[5], (LAYERS, D, D), (max(1, D // 64)) ** -0.5, 1.5, ((0, 2), (1, 32)))
    dense_bias = noise(streams_of[6], (LAYERS, D), 0.3, 1.796875, ((0, 2), (1, 32)))
    fc_in_weight = noise(streams_of[7], (LAYERS, D, FF), D ** -0.5, 0.1875, ((0, 2), (1, 32)))
    fc_in_bias = noise(streams_of[8], (LAYERS, FF), 0.3, 1.796875, ((0, 2), (1, 32)))
    fc_out_weight = noise(streams_of[9], (LAYERS, FF, D), FF ** -0.5, 0.09375, ((0, 2), (1, 32)))
    fc_out_bias = noise(streams_of[10], (LAYERS, D), 0.3, 1.796875, ((0, 2), (1, 32)))
    norm1_gain = jnp.clip(1.0 + 0.1 * jax.random.normal(streams_of[11], (LAYERS, D), jnp.float32), 0.5, 1.5).astype(jnp.bfloat16)
    norm1_bias = noise(streams_of[12], (LAYERS, D), 0.3, 1.796875, ((0, 2), (1, 32)))
    norm2_gain = jnp.clip(1.0 + 0.1 * jax.random.normal(streams_of[13], (LAYERS, D), jnp.float32), 0.5, 1.5).astype(jnp.bfloat16)
    norm2_bias = noise(streams_of[14], (LAYERS, D), 0.3, 1.796875, ((0, 2), (1, 32)))
    return {"inputs": inputs, "segments": segments, "cotangent": cotangent, "qkv_weight": qkv_weight, "qkv_bias": qkv_bias, "dense_weight": dense_weight, "dense_bias": dense_bias, "fc_in_weight": fc_in_weight, "fc_in_bias": fc_in_bias, "fc_out_weight": fc_out_weight, "fc_out_bias": fc_out_bias, "norm1_gain": norm1_gain, "norm1_bias": norm1_bias, "norm2_gain": norm2_gain, "norm2_bias": norm2_bias}


@jax.custom_vjp
def low(v):
    return lax.optimization_barrier(v.astype(jnp.bfloat16)).astype(jnp.float32)

@jax.custom_vjp
def low_back(v):
    return v

def low_keep(v):
    return (low(v), None)

def low_pass(kept, grad):
    return (grad,)

def back_keep(v):
    return (v, None)

def back_low(kept, grad):
    return (low(grad),)
low.defvjp(low_keep, low_pass)
low_back.defvjp(back_keep, back_low)
epsilon = 1e-05

def product(left, right):
    return jnp.dot(left, right, precision=lax.Precision.HIGHEST, preferred_element_type=jnp.float32)

def layer_norm(values, norm_gain, norm_bias):
    average = lax.optimization_barrier(jnp.mean(values, axis=-1, keepdims=True))
    centred = values - average
    variance = lax.optimization_barrier(jnp.mean(centred * centred, axis=-1, keepdims=True))
    return centred * lax.rsqrt(variance + epsilon) * norm_gain + norm_bias

def rotary_tables(positions):
    half_rot = ROT // 2
    frequency = jnp.exp(jnp.arange(half_rot, dtype=jnp.float32) * (-2.0 * math.log(10000.0) / ROT))
    angles = positions.astype(jnp.float32)[:, None] * frequency[None, :]
    return (jnp.cos(angles)[:, None, :], jnp.sin(angles)[:, None, :])

def rotate(head_rows, cosine_table, sine_table):
    half_rot = ROT // 2
    first_half = head_rows[..., :half_rot]
    second = head_rows[..., half_rot:ROT]
    return jnp.concatenate([first_half * cosine_table - second * sine_table, second * cosine_table + first_half * sine_table, head_rows[..., ROT:]], axis=-1)

def doc_positions(segment_row):
    places = jnp.arange(LENGTH, dtype=jnp.int32)
    starts_here = jnp.concatenate([jnp.ones((1,), jnp.bool_), segment_row[1:] != segment_row[:-1]])
    doc_start = lax.cummax(jnp.where(starts_here, places, jnp.zeros_like(places)), axis=0)
    return places - doc_start

def attention(queries, keys, values, segment_row):
    query_block = math.gcd(LENGTH, 512)
    block_count = LENGTH // query_block
    places = jnp.arange(LENGTH, dtype=jnp.int32)
    score_scale = 1.0 / math.sqrt(HD)

    @jax.checkpoint
    def one_block(pieces):
        query_part, query_places, query_segs = pieces
        scores = jnp.einsum('qhd,khd->hqk', query_part, keys, precision=lax.Precision.HIGHEST) * score_scale
        scores = low_back(scores)
        allowed = (places[None, :] <= query_places[:, None]) & (segment_row[None, :] == query_segs[:, None])
        scores = jnp.where(allowed[None], scores, -1e+30)
        top_score = lax.optimization_barrier(jnp.max(scores, axis=-1, keepdims=True))
        shifted = jnp.exp(scores - top_score)
        probability = low(shifted / lax.optimization_barrier(jnp.sum(shifted, axis=-1, keepdims=True)))
        return jnp.einsum('hqk,khd->qhd', probability, values, precision=lax.Precision.HIGHEST)
    block_inputs = (queries.reshape(block_count, query_block, HEADS, HD), places.reshape(block_count, query_block), segment_row.reshape(block_count, query_block))
    return lax.map(one_block, block_inputs).reshape(LENGTH, D)

def one_layer(hidden_in, segment_row, cosine_table, sine_table, layer_weights):
    attn_matrix, attn_shift, dense_matrix, dense_shift, up_matrix, up_shift, down_matrix, down_shift, gain_first, bias_first, gain_second, bias_second = layer_weights
    normed_attn = low(layer_norm(hidden_in, gain_first, bias_first))
    normed_mlp = low(layer_norm(hidden_in, gain_second, bias_second))
    projected = low_back(product(normed_attn, attn_matrix) + attn_shift)
    queries = low(rotate(projected[:, :D].reshape(LENGTH, HEADS, HD), cosine_table, sine_table))
    keys = low(rotate(projected[:, D:2 * D].reshape(LENGTH, HEADS, HD), cosine_table, sine_table))
    values = low(projected[:, 2 * D:].reshape(LENGTH, HEADS, HD))
    mixed_heads = low(low_back(attention(queries, keys, values, segment_row)))
    upward = low_back(product(normed_mlp, up_matrix) + up_shift)
    activated = low(jax.nn.gelu(upward, approximate=False))
    return hidden_in + product(mixed_heads, dense_matrix) + dense_shift + product(activated, down_matrix) + down_shift

def reference(inputs, segments, cotangent, qkv_weight, qkv_bias, dense_weight, dense_bias, fc_in_weight, fc_in_bias, fc_out_weight, fc_out_bias, norm1_gain, norm1_bias, norm2_gain, norm2_bias):
    sequences = MICRO * SEQS
    weights_float = tuple((weight_stack.astype(jnp.float32) for weight_stack in (qkv_weight, qkv_bias, dense_weight, dense_bias, fc_in_weight, fc_in_bias, fc_out_weight, fc_out_bias, norm1_gain, norm1_bias, norm2_gain, norm2_bias)))
    segment_flat = segments.reshape(sequences, LENGTH)
    positions = jax.vmap(doc_positions)(segment_flat)
    cosine_flat, sine_flat = jax.vmap(rotary_tables)(positions)
    inputs_flat = inputs.astype(jnp.float32).reshape(sequences, LENGTH, D)
    probes = jnp.zeros((LAYERS - 1, sequences, LENGTH, D), jnp.float32)

    def whole_model(start_rows, weight_tuple, probe_rows):
        hidden = start_rows
        section_values = []
        for layer_index in range(LAYERS):
            layer_weights = tuple((weight_stack[layer_index] for weight_stack in weight_tuple))

            def run_one(pieces):
                return one_layer(pieces[0], pieces[1], pieces[2], pieces[3], layer_weights)
            hidden = lax.map(jax.checkpoint(run_one), (hidden, segment_flat, cosine_flat, sine_flat))
            if layer_index + 1 < LAYERS:
                hidden = low_back(low(hidden) + probe_rows[layer_index])
            section_values.append(hidden)
        return jnp.stack(section_values)
    outputs_float, pullback = jax.vjp(whole_model, inputs_flat, weights_float, probes)
    cotangent_flat = cotangent.astype(jnp.float32).reshape(sequences, LENGTH, D)
    seeds = jnp.zeros_like(outputs_float).at[LAYERS - 1].set(cotangent_flat)
    input_grad, weight_grads, probe_grads = pullback(seeds)
    every_input = jnp.concatenate([input_grad[None], probe_grads], axis=0)
    full_shape = (LAYERS, MICRO, SEQS, LENGTH, D)
    section_outputs = outputs_float.reshape(full_shape).astype(jnp.bfloat16)
    input_grads = every_input.reshape(full_shape).astype(jnp.bfloat16)
    bias_grads = weight_grads[1]
    return (section_outputs, input_grads, weight_grads[0], bias_grads[:, :2 * D], bias_grads[:, 2 * D:], weight_grads[2], weight_grads[3], weight_grads[4], weight_grads[5], weight_grads[6], weight_grads[7], weight_grads[8], weight_grads[9], weight_grads[10], weight_grads[11])
```

```python
import functools
import math

import jax
import jax.numpy as jnp
from jax import lax
from jax.experimental import pallas as pl
from jax.experimental.pallas import tpu as pltpu
from jax.sharding import PartitionSpec as P

D = 1024
HEADS = 16
HD = 64
FF = 4096
ROT = 16
epsilon = 1e-05

CHIPS = 16
UNITS = FF // CHIPS
WIDE = 512
TOKENS = 2048
TILE = 256
WINDOW = 512
BLOCK = 128
SIDE = 4
OFFSETS = (0, 1, -1, 2)
DOCS = 24
LOG2E = math.log2(math.e)
SCALE = 1.0 / math.sqrt(HD)
MIB = 1024 * 1024

f32 = jnp.float32
bf16 = jnp.bfloat16

SAME_CORE = [[2 * chip + core for chip in range(CHIPS)] for core in range(2)]
LAST = (((1,), (1,)), ((), ()))
FIRST = (((0,), (0,)), ((), ()))


def core_swap(value):
    return lax.ppermute(value, "shard", [(i, i ^ 1) for i in range(2 * CHIPS)])


def section_swap(value):
    return lax.ppermute(value, "section", [(0, 1), (1, 0)])


def rep_swap(value):
    return lax.ppermute(value, "rep", [(0, 1), (1, 0)])


def plane_gather(rows):
    return lax.all_gather(rows, "shard", axis=0, tiled=True, axis_index_groups=SAME_CORE)


def plane_scatter(partial):
    return lax.psum_scatter(
        partial, "shard", scatter_dimension=0, tiled=True, axis_index_groups=SAME_CORE
    )


def hop(value, second, step):
    pairs = []
    for y in range(SIDE):
        for x in range(SIDE):
            for core in range(2):
                along_x = (core == 0) != second
                to_y, to_x = ((y, (x + step) % SIDE) if along_x else ((y + step) % SIDE, x))
                pairs.append(((y * SIDE + x) * 2 + core, (to_y * SIDE + to_x) * 2 + core))
    return lax.ppermute(value, "shard", pairs)


def row_gather(own):
    return (own, hop(own, False, -1), hop(own, False, 1), hop(own, False, 2))


def ring_gather(own):
    half = own.shape[0] // 2
    after = hop(own, True, -1)
    prior = hop(own, True, 1)
    far_first = hop(prior[:half], True, 1)
    far_last = hop(after[half:], True, -1)
    return (own, after, prior, far_first, far_last)


def block_order(chip, core):
    y, x = (chip // SIDE, chip % SIDE)
    order = []
    for second in OFFSETS:
        for first in OFFSETS:
            step_y, step_x = (jnp.where(core == 0, second, first), jnp.where(core == 0, first, second))
            order.append(((y + step_y) % SIDE) * SIDE + (x + step_x) % SIDE)
    return jnp.stack(order).astype(jnp.int32)


def gather_rows(own):
    return ring_gather(jnp.concatenate(row_gather(own), axis=0))


def add(*terms):
    return sum(term.astype(f32) for term in terms)


def scatter_rows(parts, weight, order, flipped):
    quarter = SIDE * BLOCK
    half = quarter // 2
    far = blocks_product(parts, weight, order[3 * SIDE :], flipped, bf16)
    far_first = hop(far[:half], True, 1)
    far_last = hop(far[half:], True, -1)
    near = blocks_product(parts, weight, order[SIDE : 3 * SIDE], flipped, bf16)
    ahead = jnp.concatenate([add(near[:half], far_first).astype(bf16), near[half:quarter]])
    back = jnp.concatenate(
        [near[quarter : quarter + half], add(near[quarter + half :], far_last).astype(bf16)]
    )
    from_back = hop(ahead, True, 1)
    from_ahead = hop(back, True, -1)
    home = blocks_product(parts, weight, order[:SIDE], flipped, f32)
    rows = lambda at, count: add(*(v[at : at + count] for v in (home, from_back, from_ahead)))
    ahead, back, far = (rows(k * BLOCK, BLOCK).astype(bf16) for k in (1, 2, 3))
    return add(rows(0, BLOCK), hop(far, False, 2), hop(ahead, False, 1), hop(back, False, -1))


def dot(left, right, dims=None):
    if dims is None:
        return jnp.dot(left, right, preferred_element_type=f32)
    return lax.dot_general(left, right, dims, preferred_element_type=f32)


def norm_rows(rows):
    values = rows.astype(f32)
    centred = values - jnp.mean(values, axis=-1, keepdims=True)
    inverse = lax.rsqrt(jnp.mean(centred * centred, axis=-1, keepdims=True) + epsilon)
    return (centred * inverse, inverse)


def half_turn(rows):
    lane = lax.broadcasted_iota(jnp.int32, rows.shape, 1) % HD
    ahead = pltpu.roll(rows, BLOCK - ROT // 2, 1)
    behind = pltpu.roll(rows, ROT // 2, 1)
    return jnp.where(lane < ROT // 2, ahead, behind)


def fetch_blocks(order_ref, pieces, rows_ref, sems):
    copies = []
    for piece in pieces:
        for block in range(piece.shape[0] // BLOCK):
            slot = len(copies)
            place = pl.multiple_of(order_ref[slot] * BLOCK, BLOCK)
            copy = pltpu.make_async_copy(
                piece.at[pl.ds(block * BLOCK, BLOCK)], rows_ref.at[pl.ds(place, BLOCK)], sems.at[slot]
            )
            copy.start()
            copies.append(copy)
    for copy in copies:
        copy.wait()


def project_kernel(count, order_ref, *refs):
    pieces, refs = (refs[:count], refs[count:])
    w_ref, b_ref, g_ref, c_ref, s_ref, n_ref, q_ref, kv_ref, act_ref, slope_ref, rows_ref, sems = refs

    @pl.when(pl.program_id(0) == 0)
    def _():
        fetch_blocks(order_ref, pieces, rows_ref, sems)

    here = pl.ds(pl.multiple_of(pl.program_id(0) * TILE, TILE), TILE)
    normed, _ = norm_rows(rows_ref[here, :])
    n_ref[...] = normed.astype(bf16)
    first = (normed * g_ref[0:1] + g_ref[1:2]).astype(bf16)
    second = (normed * g_ref[2:3] + g_ref[3:4]).astype(bf16)
    made = dot(first, w_ref[:, : 2 * BLOCK]) + b_ref[:, : 2 * BLOCK]
    cosine, sine = (c_ref[...], s_ref[...])
    query = made[:, :BLOCK]
    query = query * cosine + half_turn(query) * sine
    q_ref[...] = (query * SCALE).astype(bf16)
    pair = made[:, BLOCK:]
    pair = pair * cosine + half_turn(pair) * sine
    kv_ref[...] = pair.astype(bf16)
    up = dot(second, w_ref[:, 2 * BLOCK :]) + b_ref[:, 2 * BLOCK :]
    normal_cdf = 0.5 * (1.0 + lax.erf(up * (1.0 / math.sqrt(2.0))))
    act_ref[...] = (up * normal_cdf).astype(bf16)
    bell = jnp.exp(-0.5 * up * up) * (1.0 / math.sqrt(2.0 * math.pi))
    slope_ref[...] = (normal_cdf + up * bell).astype(bf16)


def tile_rows(width):
    return pl.BlockSpec((TILE, width), lambda i, order: (i, 0))


def whole_of(height, width):
    return pl.BlockSpec((height, width), lambda i, order: (0, 0))


def out_rows(width):
    return jax.ShapeDtypeStruct((TOKENS, width), bf16)


def project(order, pieces, weight, shift, gains, cosine, sine):
    return pl.pallas_call(
        functools.partial(project_kernel, len(pieces)),
        grid_spec=pltpu.PrefetchScalarGridSpec(
            num_scalar_prefetch=1,
            grid=(TOKENS // TILE,),
            in_specs=[pl.BlockSpec(memory_space=pl.ANY)] * len(pieces)
            + [whole_of(D, WIDE), whole_of(1, WIDE), whole_of(4, D), tile_rows(BLOCK), tile_rows(BLOCK)],
            out_specs=[tile_rows(w) for w in (D, BLOCK, BLOCK, UNITS, UNITS)],
            scratch_shapes=[pltpu.VMEM((TOKENS, D), bf16), pltpu.SemaphoreType.DMA((CHIPS,))],
        ),
        out_shape=[out_rows(w) for w in (D, BLOCK, BLOCK, UNITS, UNITS)],
        compiler_params=pltpu.CompilerParams(vmem_limit_bytes=24 * MIB),
        cost_estimate=pl.CostEstimate(
            flops=2 * TOKENS * D * WIDE, bytes_accessed=12 * MIB, transcendentals=2 * TOKENS * UNITS
        ),
        name="project",
    )(order, *pieces, weight, shift, gains, cosine, sine)


def pull_back_kernel(count, order_ref, *refs):
    pieces, refs = (refs[:count], refs[count:])
    w_ref, slope_ref, do_ref, e_ref, g_ref, rows_ref, sems = refs

    @pl.when(pl.program_id(0) == 0)
    def _():
        fetch_blocks(order_ref, pieces, rows_ref, sems)

    here = pl.ds(pl.multiple_of(pl.program_id(0) * TILE, TILE), TILE)
    grad = rows_ref[here, :]
    g_ref[...] = grad
    back = dot(grad, w_ref[...], LAST)
    e_ref[...] = (back[:, :UNITS] * slope_ref[...].astype(f32)).astype(bf16)
    do_ref[...] = back[:, UNITS:]


def pull_back(order, pieces, weight, slope):
    return pl.pallas_call(
        functools.partial(pull_back_kernel, len(pieces)),
        grid_spec=pltpu.PrefetchScalarGridSpec(
            num_scalar_prefetch=1,
            grid=(TOKENS // TILE,),
            in_specs=[pl.BlockSpec(memory_space=pl.ANY)] * len(pieces)
            + [whole_of(UNITS + BLOCK, D), tile_rows(UNITS)],
            out_specs=[tile_rows(w) for w in (BLOCK, UNITS, D)],
            scratch_shapes=[pltpu.VMEM((TOKENS, D), bf16), pltpu.SemaphoreType.DMA((CHIPS,))],
        ),
        out_shape=[jax.ShapeDtypeStruct((TOKENS, BLOCK), f32), out_rows(UNITS), out_rows(D)],
        compiler_params=pltpu.CompilerParams(vmem_limit_bytes=24 * MIB),
        cost_estimate=pl.CostEstimate(
            flops=2 * TOKENS * D * (UNITS + BLOCK), bytes_accessed=12 * MIB, transcendentals=0
        ),
        name="pull_back",
    )(order, *pieces, weight, slope)


def blocks_product_kernel(count, flipped, order_ref, *refs):
    w_ref, out_ref = refs[-2:]
    columns = [
        jnp.concatenate([refs[part * SIDE + block][...] for block in range(SIDE)], axis=0)
        for part in range(count)
    ]
    left = jnp.concatenate(columns, axis=1)
    out_ref[...] = dot(left, w_ref[...], LAST if flipped else None).astype(out_ref.dtype)


def blocks_product(parts, weight, order, flipped, dtype):
    def block(width, which):
        return pl.BlockSpec((BLOCK, width), lambda i, order: (order[i * SIDE + which], 0))

    groups = order.shape[0] // SIDE
    depth = sum(part.shape[1] for part in parts)
    return pl.pallas_call(
        functools.partial(blocks_product_kernel, len(parts), flipped),
        grid_spec=pltpu.PrefetchScalarGridSpec(
            num_scalar_prefetch=1,
            grid=(groups,),
            in_specs=[block(part.shape[1], which) for part in parts for which in range(SIDE)]
            + [whole_of(*weight.shape)],
            out_specs=pl.BlockSpec((SIDE * BLOCK, D), lambda i, order: (i, 0)),
        ),
        out_shape=jax.ShapeDtypeStruct((groups * SIDE * BLOCK, D), dtype),
        compiler_params=pltpu.CompilerParams(vmem_limit_bytes=24 * MIB),
        cost_estimate=pl.CostEstimate(
            flops=2 * groups * SIDE * BLOCK * depth * D, bytes_accessed=2 * MIB + groups * MIB, transcendentals=0
        ),
        name="blocks_product",
    )(order, *[part for part in parts for _ in range(SIDE)], weight)


def key_places(tile, core):
    row = lax.broadcasted_iota(jnp.int32, (WINDOW, 1), 0)
    return tile * (2 * WINDOW) + (row // BLOCK) * (2 * BLOCK) + core * BLOCK + row % BLOCK


def query_places(tile, core):
    row = lax.broadcasted_iota(jnp.int32, (1, WINDOW), 1)
    return tile * (2 * WINDOW) + (row // BLOCK) * (2 * BLOCK) + core * BLOCK + row % BLOCK


def turned(rows):
    return jnp.transpose(rows.astype(f32)).astype(bf16)


def attend_kernel(
    info_ref, q_ref, start_ref, own_ref, other_ref, o_ref, wide_ref, top_ref, over_ref, vt_ref
):
    tile = pl.program_id(0)
    core = info_ref[2 * (TOKENS // WINDOW)]

    @pl.when(tile == 0)
    def _():
        for part in range(TOKENS // BLOCK):
            rows = pl.ds(part * BLOCK, BLOCK)
            for which, ref in enumerate((own_ref, other_ref)):
                pair = turned(ref[rows, :])
                vt_ref[which, :, rows] = jnp.concatenate([pair[HD:], jnp.ones((16, BLOCK), bf16)], axis=0)

    query = q_ref[...]
    starts = start_ref[...]
    places = query_places(tile, core)

    def step(index, carry, masked):
        top, mixed = carry
        rows = pl.ds(pl.multiple_of(index * WINDOW, WINDOW), WINDOW)
        scores = [dot(ref[rows, :], query, LAST) * LOG2E for ref in (own_ref, other_ref)]
        if masked:
            allowed = []
            for which in range(2):
                keys = key_places(index, core if which == 0 else 1 - core)
                allowed.append((keys >= starts) & (keys <= places))
            scores = [jnp.where(a, s, -1e30) for a, s in zip(allowed, scores)]
        highest = jnp.max(jnp.maximum(scores[0], scores[1]), axis=0, keepdims=True)
        raised = jnp.maximum(top, jnp.ceil(highest))
        parts = [jnp.exp2(s - raised) for s in scores]
        if masked:
            parts = [jnp.where(a, p, 0.0) for a, p in zip(allowed, parts)]
        mixed = mixed * jnp.exp2(top - raised)
        for which in range(2):
            mixed = mixed + dot(vt_ref[which, :, rows], parts[which].astype(bf16))
        return (raised, mixed)

    carry = (jnp.full((1, WINDOW), -1e30, f32), jnp.zeros((HD + 16, WINDOW), f32))
    low, clear = (info_ref[tile], info_ref[TOKENS // WINDOW + tile])
    carry = lax.fori_loop(low, clear, functools.partial(step, masked=True), carry)
    carry = lax.fori_loop(clear, tile, functools.partial(step, masked=False), carry)
    top, mixed = step(tile, carry, True)
    over = 1.0 / mixed[HD : HD + 1]
    top_ref[...] = top
    over_ref[...] = over
    mixed = jnp.concatenate([jnp.zeros((HD, WINDOW), f32), mixed[:HD] * over], axis=0)
    mixed = jnp.transpose(mixed)
    wide_ref[...] = mixed
    o_ref[...] = mixed.astype(bf16)


def attend(info, query, starts, own, other):
    rows = lambda width: pl.BlockSpec((WINDOW, width), lambda i, info: (i, 0))
    line = pl.BlockSpec((1, WINDOW), lambda i, info: (0, i))
    whole = pl.BlockSpec((TOKENS, BLOCK), lambda i, info: (0, 0))
    return pl.pallas_call(
        attend_kernel,
        grid_spec=pltpu.PrefetchScalarGridSpec(
            num_scalar_prefetch=1,
            grid=(TOKENS // WINDOW,),
            in_specs=[rows(BLOCK), line, whole, whole],
            out_specs=[rows(BLOCK), rows(BLOCK), line, line],
            scratch_shapes=[pltpu.VMEM((2, HD + 16, TOKENS), bf16)],
        ),
        out_shape=[
            jax.ShapeDtypeStruct((TOKENS, BLOCK), bf16),
            jax.ShapeDtypeStruct((TOKENS, BLOCK), f32),
            jax.ShapeDtypeStruct((1, TOKENS), f32),
            jax.ShapeDtypeStruct((1, TOKENS), f32),
        ],
        compiler_params=pltpu.CompilerParams(vmem_limit_bytes=32 * MIB),
        cost_estimate=pl.CostEstimate(
            flops=8 * TOKENS * TOKENS * BLOCK, bytes_accessed=4 * MIB, transcendentals=2 * TOKENS * TOKENS
        ),
        name="attend",
    )(info, query, starts, own, other)


def attend_back_kernel(
    info_ref, q_ref, do_ref, o_ref, top_ref, over_ref, start_ref, c_ref, s_ref, own_ref, other_ref,
    dq_ref, down_ref, dother_ref, kt_ref,
):
    tile = pl.program_id(0)
    core = info_ref[2 * (TOKENS // WINDOW)]

    @pl.when(tile == 0)
    def _():
        for part in range(TOKENS // BLOCK):
            rows = pl.ds(part * BLOCK, BLOCK)
            kt_ref[0, :, rows] = turned(own_ref[rows, :])[:HD]
            kt_ref[1, :, rows] = turned(other_ref[rows, :])[:HD]
        down_ref[...] = jnp.zeros_like(down_ref)
        dother_ref[...] = jnp.zeros_like(dother_ref)

    query = q_ref[...]
    top = top_ref[...]
    starts = start_ref[...]
    places = query_places(tile, core)
    turned_grad = (jnp.transpose(do_ref[...]) * over_ref[...]).astype(bf16).astype(f32)
    inner = jnp.sum(turned_grad * jnp.transpose(o_ref[...]), axis=0, keepdims=True)
    grad = jnp.transpose(turned_grad).astype(bf16)

    def step(index, carry, masked):
        rows = pl.ds(pl.multiple_of(index * WINDOW, WINDOW), WINDOW)
        for which, (ref, dref) in enumerate(((own_ref, down_ref), (other_ref, dother_ref))):
            pair = ref[rows, :]
            parts = jnp.exp2(dot(pair, query, LAST) * LOG2E - top)
            if masked:
                keys = key_places(index, core if which == 0 else 1 - core)
                allowed = (keys >= starts) & (keys <= places)
                parts = jnp.where(allowed, parts, 0.0)
            parts = parts.astype(bf16)
            changes = (parts.astype(f32) * (dot(pair, grad, LAST) - inner)).astype(bf16)
            dref[rows, :] += dot(changes, query) + dot(parts, grad)
            carry = carry + dot(kt_ref[which, :, rows], changes)
        return carry

    low, clear = (info_ref[tile], info_ref[TOKENS // WINDOW + tile])
    carry = jnp.zeros((HD, WINDOW), f32)
    carry = lax.fori_loop(low, clear, functools.partial(step, masked=True), carry)
    carry = lax.fori_loop(clear, tile, functools.partial(step, masked=False), carry)
    carry = step(tile, carry, True) * SCALE
    change = jnp.transpose(jnp.concatenate([carry, jnp.zeros((HD, WINDOW), f32)], axis=0))
    dq_ref[...] = (change * c_ref[...] - half_turn(change) * s_ref[...]).astype(bf16)


def attend_back(info, query, grad, mixed, top, over, starts, cosine, sine, own, other):
    rows = pl.BlockSpec((WINDOW, BLOCK), lambda i, info: (i, 0))
    line = pl.BlockSpec((1, WINDOW), lambda i, info: (0, i))
    whole = pl.BlockSpec((TOKENS, BLOCK), lambda i, info: (0, 0))
    return pl.pallas_call(
        attend_back_kernel,
        grid_spec=pltpu.PrefetchScalarGridSpec(
            num_scalar_prefetch=1,
            grid=(TOKENS // WINDOW,),
            in_specs=[rows, rows, rows, line, line, line, rows, rows, whole, whole],
            out_specs=[rows, whole, whole],
            scratch_shapes=[pltpu.VMEM((2, HD, TOKENS), bf16)],
        ),
        out_shape=[
            jax.ShapeDtypeStruct((TOKENS, BLOCK), bf16),
            jax.ShapeDtypeStruct((TOKENS, BLOCK), f32),
            jax.ShapeDtypeStruct((TOKENS, BLOCK), f32),
        ],
        compiler_params=pltpu.CompilerParams(vmem_limit_bytes=40 * MIB),
        cost_estimate=pl.CostEstimate(
            flops=20 * TOKENS * TOKENS * BLOCK, bytes_accessed=6 * MIB, transcendentals=2 * TOKENS * TOKENS
        ),
        name="attend_back",
    )(info, query, grad, mixed, top, over, starts, cosine, sine, own, other)


def join_kernel(mine_ref, theirs_ref, c_ref, s_ref, out_ref):
    pair = mine_ref[...] + theirs_ref[...].astype(f32)
    out_ref[...] = (pair * c_ref[...] - half_turn(pair) * s_ref[...]).astype(bf16)


def join_pairs(mine, theirs, cosine, sine):
    rows = pl.BlockSpec((2 * TILE, BLOCK), lambda i: (i, 0))
    return pl.pallas_call(
        join_kernel,
        grid=(TOKENS // (2 * TILE),),
        in_specs=[rows] * 4,
        out_specs=rows,
        out_shape=jax.ShapeDtypeStruct((TOKENS, BLOCK), bf16),
        name="join_pairs",
    )(mine, theirs, cosine, sine)


def on_device(
    inputs,
    segments,
    cotangent,
    qkv_weight,
    qkv_bias,
    dense_weight,
    dense_bias,
    fc_in_weight,
    fc_in_bias,
    fc_out_weight,
    fc_out_bias,
    norm1_gain,
    norm1_bias,
    norm2_gain,
    norm2_bias,
):
    section = lax.axis_index("section")
    place = lax.axis_index("shard")
    chip, core = (place // 2, place % 2)
    first_layer = section == 0
    x0 = lax.dynamic_index_in_dim(inputs, section, 0, keepdims=False)[0]
    out_grad = lax.dynamic_index_in_dim(cotangent, section, 0, keepdims=False)[0]
    my_segs = lax.dynamic_index_in_dim(segments, section, 0, keepdims=False)[0]

    x0_all = plane_gather(x0)
    grad1_all = plane_gather(out_grad)

    pieces = lambda vector: vector.astype(bf16).reshape(-1, 32)
    vectors = jnp.concatenate(
        [
            pieces(v[0])
            for v in (
                norm1_gain, norm1_bias, norm2_gain, norm2_bias, qkv_bias, fc_in_bias, dense_bias, fc_out_bias,
            )
        ]
    )
    vectors_away = section_swap(vectors)
    spare = jnp.concatenate([pieces(my_segs), vectors, vectors_away, jnp.zeros((2, 32), bf16)])
    spare = jnp.concatenate([spare[:16], spare[16:]], axis=1).reshape(1, 1, 16, HD)
    heads = qkv_weight[0].reshape(2, 16, 3, CHIPS, HD).transpose(3, 0, 1, 2, 4)
    units = fc_in_weight[0].reshape(2, 16, CHIPS, UNITS).transpose(2, 0, 1, 3)
    cut = jnp.concatenate(
        [
            heads[..., 0, :],
            jnp.broadcast_to(spare, (CHIPS, 2, 16, HD)),
            heads[..., 1, :],
            heads[..., 2, :],
            units,
        ],
        axis=-1,
    ).reshape(2 * CHIPS, 16, WIDE)
    got = lax.all_to_all(cut, "shard", 0, 0, tiled=True)
    notes = got[:, :, HD:BLOCK]
    notes = jnp.concatenate([notes[..., :32], notes[..., 32:]], axis=1)
    rows_own = jnp.concatenate([dense_weight[0], fc_out_weight[0]], axis=0)
    rows_away = section_swap(rows_own)
    got_away = section_swap(got)
    got_pair = jnp.stack([got, got_away])
    rows_pair = jnp.stack([rows_own, rows_away])
    got_other = core_swap(got_pair)
    rows_other = core_swap(rows_pair)

    def by_core(mine, theirs, axis):
        return jnp.where(
            core == 0, jnp.stack([mine, theirs], axis), jnp.stack([theirs, mine], axis)
        )

    columns_both = by_core(got_pair, got_other, 2).reshape(2, D, WIDE)
    head_rows = by_core(rows_pair[:, :32], rows_other[:, :32], 1).reshape(2, HD, D)
    unit_rows = by_core(rows_pair[:, 32:], rows_other[:, 32:], 1).reshape(2, UNITS, D)
    out_both = jnp.concatenate([unit_rows, jnp.zeros((2, HD, D), bf16), head_rows], axis=1)
    notes_both = (notes[:, 4:17], notes[:, 17:30])

    def layer_weights(layer):
        mine = first_layer == (layer == 0)
        pick = lambda both: jnp.where(mine, both[0], both[1])
        columns, note = (pick(columns_both).astype(f32), pick(notes_both))
        vector = lambda at, count: note[:, at : at + count].reshape(-1).astype(f32)
        gain1, shift1, gain2, shift2 = (vector(k, 1) for k in range(4))
        attn_bias = vector(4, 3).reshape(3, CHIPS, HD)
        attn_bias = lax.dynamic_index_in_dim(attn_bias, chip, 1, keepdims=False)
        up_bias = lax.dynamic_slice_in_dim(vector(7, 4), chip * UNITS, UNITS, 0)
        out_bias = vector(11, 1) + vector(12, 1)
        lane = jnp.arange(WIDE)
        gains = jnp.where(lane[None, :] < 2 * BLOCK, gain1[:, None], gain2[:, None])
        used = (lane < HD) | (lane >= BLOCK)
        bias = jnp.concatenate(
            [attn_bias[0], jnp.zeros((HD,), f32), attn_bias[1], attn_bias[2], up_bias]
        )
        shift = bias[None, :]
        plain = jnp.where(used[None, :], columns, 0.0).astype(bf16)
        scaled = jnp.where(used[None, :], columns * gains, 0.0).astype(bf16)
        lines = jnp.stack([gain1, shift1, gain2, shift2])
        return (plain, scaled, shift, lines, pick(out_both), out_bias)

    segs = notes[:, :4].astype(jnp.int32)
    numbers = jnp.arange(DOCS, dtype=jnp.int32)
    before = jnp.sum((segs.reshape(1, -1) < numbers[:, None]).astype(jnp.int32), axis=1)
    steps = before - jnp.concatenate([jnp.zeros((1,), jnp.int32), before[:-1]])
    my_rows = lax.dynamic_index_in_dim(
        segs.reshape(CHIPS, 2, BLOCK), core, 1, keepdims=False
    ).reshape(TOKENS)
    starts = jnp.sum(jnp.where(my_rows[None, :] >= numbers[:, None], steps[:, None], 0), axis=0)
    token = jnp.arange(TOKENS, dtype=jnp.int32)
    token = (token // BLOCK) * (2 * BLOCK) + core * BLOCK + token % BLOCK
    half_rot = ROT // 2
    frequency = jnp.exp(jnp.arange(half_rot, dtype=f32) * (-2.0 * math.log(10000.0) / ROT))
    angles = frequency[:, None] * (token - starts).astype(f32)[None, :]
    cos_rows, sin_rows = (jnp.cos(angles), jnp.sin(angles))
    ones = lambda count: jnp.ones((count, TOKENS), f32)
    zeros = lambda count: jnp.zeros((count, TOKENS), f32)
    cosine = jnp.concatenate([cos_rows, cos_rows, ones(BLOCK - ROT)], axis=0).T
    sine = jnp.concatenate([-sin_rows, sin_rows, zeros(BLOCK - ROT)], axis=0).T
    tiles = starts.reshape(TOKENS // WINDOW, WINDOW)
    low_tile = tiles[:, 0] // (2 * WINDOW)
    clear_tile = jnp.minimum(
        (tiles[:, -1] + 2 * WINDOW - 1) // (2 * WINDOW),
        jnp.arange(TOKENS // WINDOW, dtype=jnp.int32),
    )
    info = jnp.concatenate([low_tile, clear_tile, core[None], jnp.zeros((7,), jnp.int32)])
    start_line = starts[None, :]

    order = block_order(chip, core)
    straight = jnp.arange(CHIPS, dtype=jnp.int32)

    def forward(pieces, arranged, weights):
        plain, _, shift, lines, _, _ = weights
        normed, query, own, act, slope = project(
            arranged, pieces, plain, shift, lines, cosine, sine
        )
        other = core_swap(own)
        mixed, wide, top, over = attend(info, query, start_line, own, other)
        return (normed, query, own, other, act, slope, mixed, wide, top, over)

    def pulled(pieces, arranged, weights, kept):
        act, slope, mixed = kept[4:7]
        grad_mixed, changed, grad_all = pull_back(arranged, pieces, weights[4], slope)
        unit_grads = dot(act, grad_all, FIRST).reshape(2, BLOCK, D)
        head_grads = dot(mixed, grad_all, FIRST)[HD:].reshape(2, 32, D)
        up_grads = dot(kept[0], changed, FIRST).reshape(2 * CHIPS, 2, 16, UNITS)
        up_sum = jnp.sum(changed.astype(f32), axis=0)
        grad_sum = jnp.sum(grad_all.astype(f32), axis=0).reshape(2 * CHIPS, 1, 1, 32)
        extra = jnp.concatenate(
            [
                jnp.broadcast_to(up_sum, (2 * CHIPS, 2, 1, UNITS)),
                jnp.pad(
                    jnp.broadcast_to(grad_sum, (2 * CHIPS, 2, 1, 32)),
                    ((0, 0), (0, 0), (0, 6), (0, UNITS - 32)),
                ),
            ],
            axis=2,
        )
        early = jnp.concatenate([up_grads, extra], axis=2)
        rows = jnp.concatenate([head_grads, unit_grads], axis=1)
        return (grad_mixed, changed, (over_cores(early, 1), over_cores(rows, 0)))

    def over_cores(parts, axis):
        keep, send = (
            lax.dynamic_index_in_dim(parts, which, axis, keepdims=False) for which in (core, 1 - core)
        )
        return keep + core_swap(send.astype(bf16)).astype(f32)

    def attended(grad_mixed, kept):
        _, query, own, other, _, _, _, wide, top, over = kept
        dq, d_own, d_other = attend_back(
            info, query, grad_mixed, wide, top, over, start_line, cosine, sine, own, other
        )
        return (dq, join_pairs(d_own, core_swap(d_other.astype(bf16)), cosine, sine))

    def late_grads(normed, dq, d_pair):
        made = jnp.concatenate([dq, d_pair], axis=1)
        grads = dot(normed, made, FIRST).reshape(2 * CHIPS, 2, 16, 2 * BLOCK)
        sums = jnp.sum(made.astype(f32), axis=0).reshape(1, 1, 4, HD)
        extra = jnp.pad(
            jnp.broadcast_to(sums, (2 * CHIPS, 2, 4, HD)), ((0, 0), (0, 0), (0, 12), (0, 0))
        )
        grads = jnp.concatenate([grads[..., :HD], extra, grads[..., BLOCK:]], axis=-1)
        return over_cores(grads, 1)

    def norm_back(rows, grad, summed):
        here, inverse = norm_rows(rows)
        inner_part = (
            summed
            - jnp.mean(summed, axis=-1, keepdims=True)
            - here * jnp.mean(summed * here, axis=-1, keepdims=True)
        )
        return (grad.astype(f32) + inverse * inner_part).astype(bf16)

    def over_planes(part0, part1):
        mine = jnp.where(first_layer, part0, part1)
        mine = mine + section_swap(jnp.where(first_layer, part1, part0).astype(bf16)).astype(f32)
        return mine + rep_swap(mine.astype(bf16)).astype(f32)

    def to_owners(parts):
        got = lax.all_to_all(parts.astype(bf16), "shard", 0, 0, tiled=True).astype(f32)
        return got.reshape(CHIPS, 2, *parts.shape[1:])

    weights0, weights1 = (layer_weights(0), layer_weights(1))
    kept0 = forward((x0_all,), straight, weights0)
    summed = scatter_rows((kept0[4], kept0[6]), weights0[4], order, False)
    x1 = (add(x0, summed) + weights0[5][None, :]).astype(bf16)
    x1, grad1_all = lax.optimization_barrier((x1, grad1_all))
    kept1 = forward(gather_rows(x1), order, weights1)
    inner = jnp.concatenate([kept1[4], kept1[6]], axis=1)
    summed = plane_scatter(dot(inner, weights1[4]).astype(bf16))
    x2 = (add(x1, summed) + weights1[5][None, :]).astype(bf16)

    grad_mixed, changed1, early1 = pulled((grad1_all,), straight, weights1, kept1)
    dq1, d_pair1 = attended(grad_mixed, kept1)
    summed = scatter_rows((dq1, d_pair1, changed1), weights1[1], order, True)
    grad1 = norm_back(x1, out_grad, summed)
    late1 = late_grads(kept1[0], dq1, d_pair1)

    grad_mixed, changed0, early0 = pulled(gather_rows(grad1), order, weights0, kept0)
    dq0, d_pair0 = attended(grad_mixed, kept0)
    late0 = late_grads(kept0[0], dq0, d_pair0)
    summed = scatter_rows((dq0, d_pair0, changed0), weights0[1], order, True)
    grad0 = norm_back(x0, grad1, summed)

    def placed(layer0, layer1):
        mine = jnp.where(first_layer, layer0, layer1)
        theirs = section_swap(jnp.where(first_layer, layer1, layer0))
        return jnp.where(
            first_layer, jnp.stack([mine, theirs]), jnp.stack([theirs, mine])
        )[None, :, None]

    section_outputs = placed(x1, x2)
    input_grads = placed(grad0, grad1)

    row_sum = over_planes(early0[1], early1[1])
    early = to_owners(over_planes(early0[0], early1[0]))
    late = to_owners(over_planes(late0, late1))
    shift_grad = early[0, 0, 17, :32]
    join = lambda parts: parts.transpose(1, 2, 0, 3).reshape(32, -1)
    up_core = join(early[:, :, :16])
    up_sum = early[:, 0, 16].reshape(-1)
    spans = ((0, HD), (BLOCK, BLOCK + HD), (BLOCK + HD, 2 * BLOCK))
    qkv_core = jnp.concatenate([join(late[..., a:b]) for a, b in spans], axis=1)
    sums = late[:, 0, :4, HD:BLOCK].reshape(CHIPS, 2 * BLOCK)
    qkv_sum = jnp.concatenate([sums[:, a:b].reshape(-1) for a, b in spans])
    column = lambda vector: vector[0].astype(f32)[:, None]
    qkv_grad = column(norm1_gain) * qkv_core + column(norm1_bias) * qkv_sum[None, :]
    up_grad = column(norm2_gain) * up_core + column(norm2_bias) * up_sum[None, :]
    wide_qkv, wide_up = (qkv_weight[0].astype(f32), fc_in_weight[0].astype(f32))
    mine_of = lambda vector, width: lax.dynamic_slice_in_dim(vector, place * width, width, 0)
    return (
        section_outputs,
        input_grads,
        qkv_grad[None],
        mine_of(qkv_sum[: 2 * D], 64)[None],
        mine_of(qkv_sum[2 * D :], 32)[None],
        row_sum[None, :32],
        shift_grad[None],
        up_grad[None],
        mine_of(up_sum, 128)[None],
        row_sum[None, 32:],
        shift_grad[None],
        jnp.sum(wide_qkv * qkv_core, axis=1)[None],
        jnp.sum(wide_qkv * qkv_sum[None, :], axis=1)[None],
        jnp.sum(wide_up * up_core, axis=1)[None],
        jnp.sum(wide_up * up_sum[None, :], axis=1)[None],
    )


def solution(mesh):
    rows = P(None, "rep", "shard", None)
    outs = P("section", None, "rep", "shard", None)
    matrix = P("section", "shard", None)
    vector = P("section", "shard")
    return jax.shard_map(
        on_device,
        mesh=mesh,
        in_specs=(
            rows, P(None, "rep", "shard"), rows, matrix, vector, matrix, vector, matrix, vector, matrix,
            vector, vector, vector, vector, vector,
        ),
        out_specs=(
            outs, outs, matrix, vector, vector, matrix, vector, matrix, vector, matrix, vector, vector,
            vector, vector, vector,
        ),
        check_vma=False,
    )
```

```python
import functools
import math

import jax
import jax.numpy as jnp
from jax import lax
from jax.experimental import pallas as pl
from jax.experimental.pallas import tpu as pltpu
from jax.sharding import PartitionSpec as P

D = 1024
HEADS = 16
HD = 64
FF = 4096
ROT = 16
epsilon = 1e-05

CHIPS = 16
UNITS = FF // CHIPS
WIDE = 512
TOKENS = 2048
TILE = 256
WINDOW = 512
BLOCK = 128
SIDE = 4
OFFSETS = (0, 1, -1, 2)
DOCS = 24
LOG2E = math.log2(math.e)
SCALE = 1.0 / math.sqrt(HD)
MIB = 1024 * 1024

f32 = jnp.float32
bf16 = jnp.bfloat16

SAME_CORE = [[2 * chip + core for chip in range(CHIPS)] for core in range(2)]
LAST = (((1,), (1,)), ((), ()))
FIRST = (((0,), (0,)), ((), ()))


def core_swap(value):
    return lax.ppermute(value, "shard", [(i, i ^ 1) for i in range(2 * CHIPS)])


def section_swap(value):
    return lax.ppermute(value, "section", [(0, 1), (1, 0)])


def cross(value, section):
    pairs = [(2 * (1 - section) + rep, 2 * section + 1 - rep) for rep in range(2)]
    return lax.ppermute(value, ("section", "rep"), pairs)


def plane_gather(rows):
    return lax.all_gather(rows, "shard", axis=0, tiled=True, axis_index_groups=SAME_CORE)


def plane_scatter(partial):
    return lax.psum_scatter(
        partial, "shard", scatter_dimension=0, tiled=True, axis_index_groups=SAME_CORE
    )


def hop(value, second, step):
    pairs = []
    for y in range(SIDE):
        for x in range(SIDE):
            for core in range(2):
                along_x = (core == 0) != second
                to_y, to_x = ((y, (x + step) % SIDE) if along_x else ((y + step) % SIDE, x))
                pairs.append(((y * SIDE + x) * 2 + core, (to_y * SIDE + to_x) * 2 + core))
    return lax.ppermute(value, "shard", pairs)


def row_gather(own):
    return (own, hop(own, False, -1), hop(own, False, 1), hop(own, False, 2))


def ring_gather(own):
    half = own.shape[0] // 2
    after = hop(own, True, -1)
    prior = hop(own, True, 1)
    far_first = hop(prior[:half], True, 1)
    far_last = hop(after[half:], True, -1)
    return (own, after, prior, far_first, far_last)


def block_order(chip, core):
    y, x = (chip // SIDE, chip % SIDE)
    order = []
    for second in OFFSETS:
        for first in OFFSETS:
            step_y, step_x = (jnp.where(core == 0, second, first), jnp.where(core == 0, first, second))
            order.append(((y + step_y) % SIDE) * SIDE + (x + step_x) % SIDE)
    return jnp.stack(order).astype(jnp.int32)


def gather_rows(own):
    return ring_gather(jnp.concatenate(row_gather(own), axis=0))


def add(*terms):
    return sum(term.astype(f32) for term in terms)


def after(value, *others):
    zero = sum(jnp.minimum(jnp.abs(lax.slice(o, (0,) * o.ndim, (1,) * o.ndim).reshape(())), 0) for o in others)
    return value + zero.astype(value.dtype)


def scatter_rows(parts, weight, order, flipped, first=(), ready=()):
    quarter = SIDE * BLOCK
    half = quarter // 2
    far = blocks_product(parts, weight, order[3 * SIDE :], flipped, bf16, first)
    far_first = hop(far[:half], True, 1)
    far_last = hop(far[half:], True, -1)
    near = blocks_product(parts, weight, order[SIDE : 3 * SIDE], flipped, bf16)
    ahead = jnp.concatenate([add(near[:half], far_first).astype(bf16), near[half:quarter]])
    back = jnp.concatenate(
        [near[quarter : quarter + half], add(near[quarter + half :], far_last).astype(bf16)]
    )
    ahead_first = ahead
    from_back = hop(ahead, True, 1)
    from_ahead = hop(back, True, -1)
    home = blocks_product(parts, weight, order[:SIDE], flipped, f32, ready)
    rows = lambda at, count: add(*(v[at : at + count] for v in (home, from_back, from_ahead)))
    ahead, back, far = (rows(k * BLOCK, BLOCK).astype(bf16) for k in (1, 2, 3))
    summed = add(rows(0, BLOCK), hop(far, False, 2), hop(ahead, False, 1), hop(back, False, -1))
    return (summed, ahead_first, far)


def dot(left, right, dims=None):
    if dims is None:
        return jnp.dot(left, right, preferred_element_type=f32)
    return lax.dot_general(left, right, dims, preferred_element_type=f32)


def norm_rows(rows):
    values = rows.astype(f32)
    centred = values - jnp.mean(values, axis=-1, keepdims=True)
    inverse = lax.rsqrt(jnp.mean(centred * centred, axis=-1, keepdims=True) + epsilon)
    return (centred * inverse, inverse)


def half_turn(rows):
    lane = lax.broadcasted_iota(jnp.int32, rows.shape, 1) % HD
    ahead = pltpu.roll(rows, BLOCK - ROT // 2, 1)
    behind = pltpu.roll(rows, ROT // 2, 1)
    return jnp.where(lane < ROT // 2, ahead, behind)


def fetch_blocks(order_ref, pieces, rows_ref, sems):
    copies = []
    for piece in pieces:
        for block in range(piece.shape[0] // BLOCK):
            slot = len(copies)
            place = pl.multiple_of(order_ref[slot] * BLOCK, BLOCK)
            copy = pltpu.make_async_copy(
                piece.at[pl.ds(block * BLOCK, BLOCK)], rows_ref.at[pl.ds(place, BLOCK)], sems.at[slot]
            )
            copy.start()
            copies.append(copy)
    for copy in copies:
        copy.wait()


def project_kernel(count, order_ref, *refs):
    pieces, refs = (refs[:count], refs[count:])
    w_ref, b_ref, g_ref, c_ref, s_ref, n_ref, q_ref, kv_ref, act_ref, slope_ref, rows_ref, sems = refs

    @pl.when(pl.program_id(0) == 0)
    def _():
        fetch_blocks(order_ref, pieces, rows_ref, sems)

    here = pl.ds(pl.multiple_of(pl.program_id(0) * TILE, TILE), TILE)
    normed, _ = norm_rows(rows_ref[here, :])
    n_ref[...] = normed.astype(bf16)
    first = (normed * g_ref[0:1] + g_ref[1:2]).astype(bf16)
    second = (normed * g_ref[2:3] + g_ref[3:4]).astype(bf16)
    made = dot(first, w_ref[:, : 2 * BLOCK]) + b_ref[:, : 2 * BLOCK]
    cosine, sine = (c_ref[...], s_ref[...])
    query = made[:, :BLOCK]
    query = query * cosine + half_turn(query) * sine
    q_ref[...] = (query * SCALE).astype(bf16)
    pair = made[:, BLOCK:]
    pair = pair * cosine + half_turn(pair) * sine
    kv_ref[...] = pair.astype(bf16)
    up = dot(second, w_ref[:, 2 * BLOCK :]) + b_ref[:, 2 * BLOCK :]
    normal_cdf = 0.5 * (1.0 + lax.erf(up * (1.0 / math.sqrt(2.0))))
    act_ref[...] = (up * normal_cdf).astype(bf16)
    bell = jnp.exp(-0.5 * up * up) * (1.0 / math.sqrt(2.0 * math.pi))
    slope_ref[...] = (normal_cdf + up * bell).astype(bf16)


def tile_rows(width):
    return pl.BlockSpec((TILE, width), lambda i, order: (i, 0))


def whole_of(height, width):
    return pl.BlockSpec((height, width), lambda i, order: (0, 0))


def out_rows(width):
    return jax.ShapeDtypeStruct((TOKENS, width), bf16)


def unused(ties):
    return [pl.BlockSpec(memory_space=pl.ANY)] * len(ties)


def project(order, pieces, weight, shift, gains, cosine, sine):
    return pl.pallas_call(
        functools.partial(project_kernel, len(pieces)),
        grid_spec=pltpu.PrefetchScalarGridSpec(
            num_scalar_prefetch=1,
            grid=(TOKENS // TILE,),
            in_specs=[pl.BlockSpec(memory_space=pltpu.HBM)] * len(pieces)
            + [whole_of(D, WIDE), whole_of(1, WIDE), whole_of(4, D), tile_rows(BLOCK), tile_rows(BLOCK)],
            out_specs=[tile_rows(w) for w in (D, BLOCK, BLOCK, UNITS, UNITS)],
            scratch_shapes=[pltpu.VMEM((TOKENS, D), bf16), pltpu.SemaphoreType.DMA((CHIPS,))],
        ),
        out_shape=[pltpu.HBM((TOKENS, D), bf16)] + [out_rows(w) for w in (BLOCK, BLOCK, UNITS, UNITS)],
        compiler_params=pltpu.CompilerParams(vmem_limit_bytes=14 * MIB),
        cost_estimate=pl.CostEstimate(
            flops=2 * TOKENS * D * WIDE, bytes_accessed=12 * MIB, transcendentals=2 * TOKENS * UNITS
        ),
        name="project",
    )(order, *pieces, weight, shift, gains, cosine, sine)


def pull_back_kernel(count, order_ref, *refs):
    pieces, refs = (refs[:count], refs[count:])
    w_ref, slope_ref = refs[:2]
    do_ref, e_ref, g_ref, rows_ref, sems = refs[-5:]

    @pl.when(pl.program_id(0) == 0)
    def _():
        fetch_blocks(order_ref, pieces, rows_ref, sems)

    here = pl.ds(pl.multiple_of(pl.program_id(0) * TILE, TILE), TILE)
    grad = rows_ref[here, :]
    g_ref[...] = grad
    back = dot(grad, w_ref[...], LAST)
    e_ref[...] = (back[:, :UNITS] * slope_ref[...].astype(f32)).astype(bf16)
    do_ref[...] = back[:, UNITS:]


def pull_back(order, pieces, weight, slope, ties=()):
    return pl.pallas_call(
        functools.partial(pull_back_kernel, len(pieces)),
        grid_spec=pltpu.PrefetchScalarGridSpec(
            num_scalar_prefetch=1,
            grid=(TOKENS // TILE,),
            in_specs=[pl.BlockSpec(memory_space=pltpu.HBM)] * len(pieces)
            + [whole_of(UNITS + BLOCK, D), tile_rows(UNITS)]
            + unused(ties),
            out_specs=[tile_rows(w) for w in (BLOCK, UNITS, D)],
            scratch_shapes=[pltpu.VMEM((TOKENS, D), bf16), pltpu.SemaphoreType.DMA((CHIPS,))],
        ),
        out_shape=[jax.ShapeDtypeStruct((TOKENS, BLOCK), f32), out_rows(UNITS), pltpu.HBM((TOKENS, D), bf16)],
        compiler_params=pltpu.CompilerParams(vmem_limit_bytes=14 * MIB),
        cost_estimate=pl.CostEstimate(
            flops=2 * TOKENS * D * (UNITS + BLOCK), bytes_accessed=12 * MIB, transcendentals=0
        ),
        name="pull_back",
    )(order, *pieces, weight, slope, *ties)


def blocks_product_kernel(count, flipped, order_ref, *refs):
    w_ref, out_ref = (refs[count * SIDE], refs[-1])
    columns = [
        jnp.concatenate([refs[part * SIDE + block][...] for block in range(SIDE)], axis=0)
        for part in range(count)
    ]
    left = jnp.concatenate(columns, axis=1)
    out_ref[...] = dot(left, w_ref[...], LAST if flipped else None).astype(out_ref.dtype)


def blocks_product(parts, weight, order, flipped, dtype, ties=()):
    def block(width, which):
        return pl.BlockSpec((BLOCK, width), lambda i, order: (order[i * SIDE + which], 0))

    groups = order.shape[0] // SIDE
    depth = sum(part.shape[1] for part in parts)
    return pl.pallas_call(
        functools.partial(blocks_product_kernel, len(parts), flipped),
        grid_spec=pltpu.PrefetchScalarGridSpec(
            num_scalar_prefetch=1,
            grid=(groups,),
            in_specs=[block(part.shape[1], which) for part in parts for which in range(SIDE)]
            + [whole_of(*weight.shape)]
            + unused(ties),
            out_specs=pl.BlockSpec((SIDE * BLOCK, D), lambda i, order: (i, 0)),
        ),
        out_shape=jax.ShapeDtypeStruct((groups * SIDE * BLOCK, D), dtype),
        compiler_params=pltpu.CompilerParams(vmem_limit_bytes=10 * MIB),
        cost_estimate=pl.CostEstimate(
            flops=2 * groups * SIDE * BLOCK * depth * D, bytes_accessed=2 * MIB + groups * MIB, transcendentals=0
        ),
        name="blocks_product",
    )(order, *[part for part in parts for _ in range(SIDE)], weight, *ties)


def key_places(tile, core):
    row = lax.broadcasted_iota(jnp.int32, (WINDOW, 1), 0)
    return tile * (2 * WINDOW) + (row // BLOCK) * (2 * BLOCK) + core * BLOCK + row % BLOCK


def query_places(tile, core):
    row = lax.broadcasted_iota(jnp.int32, (1, WINDOW), 1)
    return tile * (2 * WINDOW) + (row // BLOCK) * (2 * BLOCK) + core * BLOCK + row % BLOCK


def turned(rows):
    return jnp.transpose(rows.astype(f32)).astype(bf16)


def attend_kernel(
    info_ref, q_ref, start_ref, own_ref, other_ref, o_ref, wide_ref, top_ref, over_ref, vt_ref
):
    tile = pl.program_id(0)
    core = info_ref[2 * (TOKENS // WINDOW)]

    @pl.when(tile == 0)
    def _():
        for part in range(TOKENS // BLOCK):
            rows = pl.ds(part * BLOCK, BLOCK)
            for which, ref in enumerate((own_ref, other_ref)):
                pair = turned(ref[rows, :])
                vt_ref[which, :, rows] = jnp.concatenate([pair[HD:], jnp.ones((16, BLOCK), bf16)], axis=0)

    query = q_ref[...]
    starts = start_ref[...]
    places = query_places(tile, core)

    def step(index, carry, masked):
        top, mixed = carry
        rows = pl.ds(pl.multiple_of(index * WINDOW, WINDOW), WINDOW)
        scores = [dot(ref[rows, :], query, LAST) * LOG2E for ref in (own_ref, other_ref)]
        if masked:
            allowed = []
            for which in range(2):
                keys = key_places(index, core if which == 0 else 1 - core)
                allowed.append((keys >= starts) & (keys <= places))
            scores = [jnp.where(a, s, -1e30) for a, s in zip(allowed, scores)]
        highest = jnp.max(jnp.maximum(scores[0], scores[1]), axis=0, keepdims=True)
        raised = jnp.maximum(top, jnp.ceil(highest))
        parts = [jnp.exp2(s - raised) for s in scores]
        if masked:
            parts = [jnp.where(a, p, 0.0) for a, p in zip(allowed, parts)]
        mixed = mixed * jnp.exp2(top - raised)
        for which in range(2):
            mixed = mixed + dot(vt_ref[which, :, rows], parts[which].astype(bf16))
        return (raised, mixed)

    carry = (jnp.full((1, WINDOW), -1e30, f32), jnp.zeros((HD + 16, WINDOW), f32))
    low, clear = (info_ref[tile], info_ref[TOKENS // WINDOW + tile])
    carry = lax.fori_loop(low, clear, functools.partial(step, masked=True), carry)
    carry = lax.fori_loop(clear, tile, functools.partial(step, masked=False), carry)
    top, mixed = step(tile, carry, True)
    over = 1.0 / mixed[HD : HD + 1]
    top_ref[...] = top
    over_ref[...] = over
    spare = (lax.broadcasted_iota(jnp.int32, (HD, WINDOW), 0) == 0).astype(f32)
    mixed = jnp.concatenate([spare, mixed[:HD] * over], axis=0)
    mixed = jnp.transpose(mixed)
    wide_ref[...] = mixed
    o_ref[...] = mixed.astype(bf16)


def attend(info, query, starts, own, other):
    rows = lambda width: pl.BlockSpec((WINDOW, width), lambda i, info: (i, 0))
    line = pl.BlockSpec((1, WINDOW), lambda i, info: (0, i))
    whole = pl.BlockSpec((TOKENS, BLOCK), lambda i, info: (0, 0))
    return pl.pallas_call(
        attend_kernel,
        grid_spec=pltpu.PrefetchScalarGridSpec(
            num_scalar_prefetch=1,
            grid=(TOKENS // WINDOW,),
            in_specs=[rows(BLOCK), line, whole, whole],
            out_specs=[rows(BLOCK), rows(BLOCK), line, line],
            scratch_shapes=[pltpu.VMEM((2, HD + 16, TOKENS), bf16)],
        ),
        out_shape=[
            jax.ShapeDtypeStruct((TOKENS, BLOCK), bf16),
            jax.ShapeDtypeStruct((TOKENS, BLOCK), f32),
            jax.ShapeDtypeStruct((1, TOKENS), f32),
            jax.ShapeDtypeStruct((1, TOKENS), f32),
        ],
        compiler_params=pltpu.CompilerParams(vmem_limit_bytes=32 * MIB),
        cost_estimate=pl.CostEstimate(
            flops=8 * TOKENS * TOKENS * BLOCK, bytes_accessed=4 * MIB, transcendentals=2 * TOKENS * TOKENS
        ),
        name="attend",
    )(info, query, starts, own, other)


def attend_back_kernel(
    info_ref, q_ref, do_ref, o_ref, top_ref, over_ref, start_ref, c_ref, s_ref, own_ref, other_ref, *refs
):
    dq_ref, down_ref, dother_low_ref, kt_ref, dother_ref = refs[-5:]
    tile = pl.program_id(0)
    core = info_ref[2 * (TOKENS // WINDOW)]

    @pl.when(tile == 0)
    def _():
        for part in range(TOKENS // BLOCK):
            rows = pl.ds(part * BLOCK, BLOCK)
            kt_ref[0, :, rows] = turned(own_ref[rows, :])[:HD]
            kt_ref[1, :, rows] = turned(other_ref[rows, :])[:HD]
        down_ref[...] = jnp.zeros_like(down_ref)
        dother_ref[...] = jnp.zeros_like(dother_ref)

    query = q_ref[...]
    top = top_ref[...]
    starts = start_ref[...]
    places = query_places(tile, core)
    turned_grad = (jnp.transpose(do_ref[...]) * over_ref[...]).astype(bf16).astype(f32)
    inner = jnp.sum(turned_grad * jnp.transpose(o_ref[...]), axis=0, keepdims=True)
    grad = jnp.transpose(turned_grad).astype(bf16)

    def step(index, carry, masked):
        rows = pl.ds(pl.multiple_of(index * WINDOW, WINDOW), WINDOW)
        for which, (ref, dref) in enumerate(((own_ref, down_ref), (other_ref, dother_ref))):
            pair = ref[rows, :]
            parts = jnp.exp2(dot(pair, query, LAST) * LOG2E - top)
            if masked:
                keys = key_places(index, core if which == 0 else 1 - core)
                allowed = (keys >= starts) & (keys <= places)
                parts = jnp.where(allowed, parts, 0.0)
            parts = parts.astype(bf16)
            changes = (parts.astype(f32) * (dot(pair, grad, LAST) - inner)).astype(bf16)
            dref[rows, :] += dot(changes, query) + dot(parts, grad)
            carry = carry + dot(kt_ref[which, :, rows], changes)
        return carry

    low, clear = (info_ref[tile], info_ref[TOKENS // WINDOW + tile])
    carry = jnp.zeros((HD, WINDOW), f32)
    carry = lax.fori_loop(low, clear, functools.partial(step, masked=True), carry)
    carry = lax.fori_loop(clear, tile, functools.partial(step, masked=False), carry)
    carry = step(tile, carry, True) * SCALE
    change = jnp.transpose(jnp.concatenate([carry, jnp.zeros((HD, WINDOW), f32)], axis=0))
    dq_ref[...] = (change * c_ref[...] - half_turn(change) * s_ref[...]).astype(bf16)

    @pl.when(tile == TOKENS // WINDOW - 1)
    def _():
        dother_low_ref[...] = dother_ref[...].astype(bf16)


def attend_back(info, query, grad, mixed, top, over, starts, cosine, sine, own, other, ties=()):
    rows = pl.BlockSpec((WINDOW, BLOCK), lambda i, info: (i, 0))
    line = pl.BlockSpec((1, WINDOW), lambda i, info: (0, i))
    whole = pl.BlockSpec((TOKENS, BLOCK), lambda i, info: (0, 0))
    return pl.pallas_call(
        attend_back_kernel,
        grid_spec=pltpu.PrefetchScalarGridSpec(
            num_scalar_prefetch=1,
            grid=(TOKENS // WINDOW,),
            in_specs=[rows, rows, rows, line, line, line, rows, rows, whole, whole] + unused(ties),
            out_specs=[rows, whole, whole],
            scratch_shapes=[pltpu.VMEM((2, HD, TOKENS), bf16), pltpu.VMEM((TOKENS, BLOCK), f32)],
        ),
        out_shape=[
            jax.ShapeDtypeStruct((TOKENS, BLOCK), bf16),
            jax.ShapeDtypeStruct((TOKENS, BLOCK), f32),
            jax.ShapeDtypeStruct((TOKENS, BLOCK), bf16),
        ],
        compiler_params=pltpu.CompilerParams(vmem_limit_bytes=40 * MIB),
        cost_estimate=pl.CostEstimate(
            flops=20 * TOKENS * TOKENS * BLOCK, bytes_accessed=6 * MIB, transcendentals=2 * TOKENS * TOKENS
        ),
        name="attend_back",
    )(info, query, grad, mixed, top, over, starts, cosine, sine, own, other, *ties)


def join_kernel(mine_ref, theirs_ref, c_ref, s_ref, out_ref):
    pair = mine_ref[...] + theirs_ref[...].astype(f32)
    out_ref[...] = (pair * c_ref[...] - half_turn(pair) * s_ref[...]).astype(bf16)


def join_pairs(mine, theirs, cosine, sine):
    rows = pl.BlockSpec((2 * TILE, BLOCK), lambda i: (i, 0))
    return pl.pallas_call(
        join_kernel,
        grid=(TOKENS // (2 * TILE),),
        in_specs=[rows] * 4,
        out_specs=rows,
        out_shape=jax.ShapeDtypeStruct((TOKENS, BLOCK), bf16),
        name="join_pairs",
    )(mine, theirs, cosine, sine)


def finish_kernel(got_ref, qkv_ref, up_ref, norm_ref, qkv_out, up_out, qkv_sum_ref, up_sum_ref, norm_out):
    gain1, shift1, gain2, shift2 = (norm_ref[:, k : k + 1] for k in range(4))
    first = lax.broadcasted_iota(jnp.int32, (32, BLOCK), 1) < HD
    total = [jnp.zeros((32, 1), f32) for _ in range(4)]
    across = lambda values: jnp.sum(values, axis=1, keepdims=True)
    for chip in range(0, CHIPS, 2):
        tiles = [got_ref[chip + k, 40:, :].astype(f32) for k in range(2)]
        (low0, high0), (low1, high1) = ((t[:, :BLOCK], t[:, BLOCK:]) for t in tiles)
        turn = lambda values: pltpu.roll(values, HD, 1)
        cores = (
            jnp.where(first, low0, turn(low1)),
            jnp.where(first, high0, turn(high1)),
            jnp.where(first, turn(high0), high1),
        )
        notes = jnp.where(first, turn(low0), low1)
        for part, (core, row) in enumerate(zip(cores, (0, 2, 3))):
            at = pl.ds(part * D + chip * HD, BLOCK)
            sums = notes[row : row + 1]
            weight = qkv_ref[:, at].astype(f32)
            qkv_out[:, at] = gain1 * core + shift1 * sums
            qkv_sum_ref[:, at] = sums
            total[0] += across(weight * core)
            total[1] += across(weight * sums)
    for chip in range(CHIPS):
        at = pl.ds(chip * UNITS, UNITS)
        core = got_ref[chip, :32, :].astype(f32)
        sums = got_ref[chip, 32:40, :].astype(f32)[:1]
        weight = up_ref[:, at].astype(f32)
        up_out[:, at] = gain2 * core + shift2 * sums
        up_sum_ref[:, at] = sums
        total[2] += across(weight * core)
        total[3] += across(weight * sums)
    lane = lax.broadcasted_iota(jnp.int32, (32, BLOCK), 1)
    out = jnp.zeros((32, BLOCK), f32)
    for k in range(4):
        out = jnp.where(lane == k, total[k], out)
    norm_out[...] = out


def finish(got, qkv_weight, up_weight, norms):
    shape = lambda *dims: jax.ShapeDtypeStruct(dims, f32)
    return pl.pallas_call(
        finish_kernel,
        out_shape=[shape(32, 3 * D), shape(32, FF), shape(1, 3 * D), shape(1, FF), shape(32, BLOCK)],
        compiler_params=pltpu.CompilerParams(vmem_limit_bytes=10 * MIB),
        cost_estimate=pl.CostEstimate(flops=8 * 32 * 7 * D, bytes_accessed=3 * MIB, transcendentals=0),
        name="finish",
    )(got, qkv_weight, up_weight, norms)


def on_device(
    inputs,
    segments,
    cotangent,
    qkv_weight,
    qkv_bias,
    dense_weight,
    dense_bias,
    fc_in_weight,
    fc_in_bias,
    fc_out_weight,
    fc_out_bias,
    norm1_gain,
    norm1_bias,
    norm2_gain,
    norm2_bias,
):
    section = lax.axis_index("section")
    place = lax.axis_index("shard")
    chip, core = (place // 2, place % 2)
    first_layer = section == 0
    x0 = lax.dynamic_index_in_dim(inputs, section, 0, keepdims=False)[0]
    out_grad = lax.dynamic_index_in_dim(cotangent, section, 0, keepdims=False)[0]
    my_segs = lax.dynamic_index_in_dim(segments, section, 0, keepdims=False)[0]

    x0_all = plane_gather(x0)
    grad1_all = plane_gather(out_grad)

    pieces = lambda vector: vector.astype(bf16).reshape(-1, 32)
    vectors = jnp.concatenate(
        [
            pieces(v[0])
            for v in (
                norm1_gain, norm1_bias, norm2_gain, norm2_bias, qkv_bias, fc_in_bias, dense_bias, fc_out_bias,
            )
        ]
    )
    vectors_away = section_swap(vectors)
    spare = jnp.concatenate([pieces(my_segs), vectors, vectors_away, jnp.zeros((2, 32), bf16)])
    spare = jnp.concatenate([spare[:16], spare[16:]], axis=1).reshape(1, 1, 16, HD)
    heads = qkv_weight[0].reshape(2, 16, 3, CHIPS, HD).transpose(3, 0, 1, 2, 4)
    units = fc_in_weight[0].reshape(2, 16, CHIPS, UNITS).transpose(2, 0, 1, 3)
    cut = jnp.concatenate(
        [
            heads[..., 0, :],
            jnp.broadcast_to(spare, (CHIPS, 2, 16, HD)),
            heads[..., 1, :],
            heads[..., 2, :],
            units,
        ],
        axis=-1,
    ).reshape(2 * CHIPS, 16, WIDE)
    got = lax.all_to_all(cut, "shard", 0, 0, tiled=True)
    notes = got[:, :, HD:BLOCK]
    notes = jnp.concatenate([notes[..., :32], notes[..., 32:]], axis=1)
    rows_own = jnp.concatenate([dense_weight[0], fc_out_weight[0]], axis=0)
    rows_away = section_swap(rows_own)
    got_away = section_swap(got)
    got_pair = jnp.stack([got, got_away])
    rows_pair = jnp.stack([rows_own, rows_away])
    got_other = core_swap(got_pair)
    rows_other = core_swap(rows_pair)

    def by_core(mine, theirs, axis):
        return jnp.where(
            core == 0, jnp.stack([mine, theirs], axis), jnp.stack([theirs, mine], axis)
        )

    columns_both = by_core(got_pair, got_other, 2).reshape(2, D, WIDE)
    head_rows = by_core(rows_pair[:, :32], rows_other[:, :32], 1).reshape(2, HD, D)
    unit_rows = by_core(rows_pair[:, 32:], rows_other[:, 32:], 1).reshape(2, UNITS, D)
    out_both = jnp.concatenate([unit_rows, jnp.zeros((2, HD, D), bf16), head_rows], axis=1)
    notes_both = (notes[:, 4:17], notes[:, 17:30])

    def layer_weights(layer):
        mine = first_layer == (layer == 0)
        pick = lambda both: jnp.where(mine, both[0], both[1])
        columns, note = (pick(columns_both).astype(f32), pick(notes_both))
        vector = lambda at, count: note[:, at : at + count].reshape(-1).astype(f32)
        gain1, shift1, gain2, shift2 = (vector(k, 1) for k in range(4))
        attn_bias = vector(4, 3).reshape(3, CHIPS, HD)
        attn_bias = lax.dynamic_index_in_dim(attn_bias, chip, 1, keepdims=False)
        up_bias = lax.dynamic_slice_in_dim(vector(7, 4), chip * UNITS, UNITS, 0)
        out_bias = vector(11, 1) + vector(12, 1)
        lane = jnp.arange(WIDE)
        gains = jnp.where(lane[None, :] < 2 * BLOCK, gain1[:, None], gain2[:, None])
        used = (lane < HD) | (lane >= BLOCK)
        bias = jnp.concatenate(
            [attn_bias[0], jnp.zeros((HD,), f32), attn_bias[1], attn_bias[2], up_bias]
        )
        shift = bias[None, :]
        plain = jnp.where(used[None, :], columns, 0.0).astype(bf16)
        scaled = jnp.where(used[None, :], columns * gains, 0.0).astype(bf16)
        lines = jnp.stack([gain1, shift1, gain2, shift2])
        return (plain, scaled, shift, lines, pick(out_both), out_bias)

    segs = notes[:, :4].astype(jnp.int32)
    numbers = jnp.arange(DOCS, dtype=jnp.int32)
    before = jnp.sum((segs.reshape(1, -1) < numbers[:, None]).astype(jnp.int32), axis=1)
    steps = before - jnp.concatenate([jnp.zeros((1,), jnp.int32), before[:-1]])
    my_rows = lax.dynamic_index_in_dim(
        segs.reshape(CHIPS, 2, BLOCK), core, 1, keepdims=False
    ).reshape(TOKENS)
    starts = jnp.sum(jnp.where(my_rows[None, :] >= numbers[:, None], steps[:, None], 0), axis=0)
    token = jnp.arange(TOKENS, dtype=jnp.int32)
    token = (token // BLOCK) * (2 * BLOCK) + core * BLOCK + token % BLOCK
    half_rot = ROT // 2
    frequency = jnp.exp(jnp.arange(half_rot, dtype=f32) * (-2.0 * math.log(10000.0) / ROT))
    angles = frequency[:, None] * (token - starts).astype(f32)[None, :]
    cos_rows, sin_rows = (jnp.cos(angles), jnp.sin(angles))
    ones = lambda count: jnp.ones((count, TOKENS), f32)
    zeros = lambda count: jnp.zeros((count, TOKENS), f32)
    cosine = jnp.concatenate([cos_rows, cos_rows, ones(BLOCK - ROT)], axis=0).T
    sine = jnp.concatenate([-sin_rows, sin_rows, zeros(BLOCK - ROT)], axis=0).T
    tiles = starts.reshape(TOKENS // WINDOW, WINDOW)
    low_tile = tiles[:, 0] // (2 * WINDOW)
    clear_tile = jnp.minimum(
        (tiles[:, -1] + 2 * WINDOW - 1) // (2 * WINDOW),
        jnp.arange(TOKENS // WINDOW, dtype=jnp.int32),
    )
    info = jnp.concatenate([low_tile, clear_tile, core[None], jnp.zeros((7,), jnp.int32)])
    start_line = starts[None, :]

    order = block_order(chip, core)
    straight = jnp.arange(CHIPS, dtype=jnp.int32)

    def forward(pieces, arranged, weights):
        plain, _, shift, lines, _, _ = weights
        normed, query, own, act, slope = project(
            arranged, pieces, plain, shift, lines, cosine, sine
        )
        other = core_swap(own)
        mixed, wide, top, over = attend(info, query, start_line, own, other)
        return (normed, query, own, other, act, slope, mixed, wide, top, over)

    def pulled(pieces, arranged, weights, kept, ties=()):
        return pull_back(arranged, pieces, weights[4], kept[5], ties)

    def by_owner(parts):
        return parts.reshape(CHIPS, 2, 32, parts.shape[-1])

    def early_grads(kept, changed, grad_all):
        up_grads = by_owner(dot(kept[0], changed, FIRST))
        grads = dot(jnp.concatenate([kept[4], kept[6]], axis=1), grad_all, FIRST)
        up_sum = jnp.sum(changed.astype(f32), axis=0)
        grad_sum = jnp.pad(grads[UNITS].reshape(CHIPS, 2, 1, 32), ((0, 0),) * 3 + ((0, UNITS - 32),))
        extra = [jnp.broadcast_to(up_sum, (CHIPS, 2, 1, UNITS)), grad_sum]
        extra.append(jnp.zeros((CHIPS, 2, 6, UNITS), f32))
        blocks = jnp.concatenate([up_grads, *extra], axis=2).transpose(1, 0, 2, 3)
        heads, units = (grads[UNITS + HD :].reshape(2, 32, D), grads[:UNITS].reshape(2, BLOCK, D))
        rows = jnp.concatenate([heads, units], axis=1)
        rows = [rows[..., at : at + UNITS] for at in range(0, D, UNITS)]
        return [blocks.reshape(2, CHIPS * 40, UNITS), *rows]

    def over_cores(parts):
        keep, send = (
            jnp.concatenate(
                [lax.dynamic_index_in_dim(part, which, 0, keepdims=False) for part in parts]
            )
            for which in (core, 1 - core)
        )
        send = send.astype(bf16)
        return (add(keep, core_swap(send)), send)

    def attended(grad_mixed, kept, ties=()):
        _, query, own, other, _, _, _, wide, top, over = kept
        dq, d_own, d_other = attend_back(
            info, query, grad_mixed, wide, top, over, start_line, cosine, sine, own, other, ties
        )
        return (dq, join_pairs(d_own, core_swap(d_other), cosine, sine))

    def late_grads(normed, dq, d_pair):
        made = jnp.concatenate([dq, d_pair], axis=1)
        grads = by_owner(dot(normed, made, FIRST))
        sums = jnp.sum(made.astype(f32), axis=0).reshape(1, 1, 4, HD)
        extra = jnp.pad(jnp.broadcast_to(sums, (CHIPS, 2, 4, HD)), ((0, 0), (0, 0), (0, 28), (0, 0)))
        grads = jnp.concatenate([grads[..., :HD], extra, grads[..., BLOCK:]], axis=-1)
        return grads.transpose(1, 0, 2, 3).reshape(2, CHIPS * 32, 2 * BLOCK)

    def norm_back(rows, grad, summed):
        here, inverse = norm_rows(rows)
        inner_part = (
            summed
            - jnp.mean(summed, axis=-1, keepdims=True)
            - here * jnp.mean(summed * here, axis=-1, keepdims=True)
        )
        return (grad.astype(f32) + inverse * inner_part).astype(bf16)

    weights0, weights1 = (layer_weights(0), layer_weights(1))
    kept0 = forward((x0_all,), straight, weights0)
    ready = (weights0[1], weights1[0], weights1[1], weights1[2])
    summed, _, _ = scatter_rows((kept0[4], kept0[6]), weights0[4], order, False, (), ready)
    x1 = (add(x0, summed) + weights0[5][None, :]).astype(bf16)
    x1, grad1_all = lax.optimization_barrier((x1, grad1_all))
    kept1 = forward(gather_rows(x1), order, weights1)
    grad_mixed, changed1, grad1_all = pulled((grad1_all,), straight, weights1, kept1)
    dq1, d_pair1 = attended(grad_mixed, kept1)
    inner = jnp.concatenate([kept1[4], after(kept1[6], dq1)], axis=1)
    summed = plane_scatter(dot(inner, weights1[4]).astype(bf16))
    x2 = (add(x1, summed) + weights1[5][None, :]).astype(bf16)
    summed, held, _ = scatter_rows((dq1, d_pair1, changed1), weights1[1], order, True)
    grad1 = norm_back(x1, out_grad, summed)
    early1 = early_grads(kept1, after(changed1, held), after(grad1_all, held))
    layer1, _ = over_cores([late_grads(kept1[0], after(dq1, held), d_pair1), *early1])
    layer1 = layer1.astype(bf16)
    half1 = add(layer1, section_swap(layer1)).astype(bf16)
    layer1 = add(half1, cross(half1, 1)).astype(bf16)

    grad_mixed, changed0, grad0_all = pulled(
        gather_rows(grad1), order, weights0, kept0, (half1,)
    )
    early0, _ = over_cores(early_grads(kept0, changed0, grad0_all))
    early0 = early0.astype(bf16)
    dq0, d_pair0 = attended(grad_mixed, kept0, (x2, layer1))
    late0, send = over_cores([late_grads(kept0[0], dq0, d_pair0)])
    summed, held, step = scatter_rows(
        (dq0, d_pair0, changed0), weights0[1], order, True, (send,)
    )
    half0 = add(after(early0, held), section_swap(early0)).astype(bf16)
    early0 = add(half0, cross(half0, 0)).astype(bf16)
    grad0 = norm_back(x0, grad1, summed)

    def placed(layer0, layer1):
        mine = jnp.where(first_layer, layer0, layer1)
        theirs = section_swap(jnp.where(first_layer, layer1, layer0))
        return jnp.where(
            first_layer, jnp.stack([mine, theirs]), jnp.stack([theirs, mine])
        )[None, :, None]

    section_outputs = placed(x1, x2)
    input_grads = placed(grad0, grad1)

    late0 = late0.astype(bf16)
    half0 = add(late0, section_swap(late0)).astype(bf16)
    late0 = add(half0, cross(half0, 0))
    late0 = after(late0, step).astype(bf16)
    parts = jnp.where(first_layer, jnp.concatenate([late0, early0]), layer1)
    late, early, rows = jnp.split(parts, [CHIPS * 32, CHIPS * 72])
    row_sum = jnp.concatenate(jnp.split(rows, D // UNITS), axis=1).astype(f32)
    parts = jnp.concatenate([part.reshape(CHIPS, -1, UNITS) for part in (early, late)], axis=1)
    got = lax.all_to_all(parts, "shard", 0, 0, tiled=True, axis_index_groups=SAME_CORE)
    column = lambda vector: vector[0].astype(f32)[:, None]
    norms = jnp.concatenate([column(v) for v in (norm1_gain, norm1_bias, norm2_gain, norm2_bias)], axis=1)
    qkv_grad, up_grad, qkv_sum, up_sum, norm_grads = finish(got, qkv_weight[0], fc_in_weight[0], norms)
    shift_grad = got[0, 33, :32].astype(f32)
    mine_of = lambda vector, at, width: lax.dynamic_slice_in_dim(
        vector, at + place * width, width, 1
    )
    return (
        section_outputs,
        input_grads,
        qkv_grad[None],
        mine_of(qkv_sum[:, : 2 * D], 0, 64),
        mine_of(qkv_sum[:, 2 * D :], 0, 32),
        row_sum[None, :32],
        shift_grad[None],
        up_grad[None],
        mine_of(up_sum, 0, 128),
        row_sum[None, 32:],
        shift_grad[None],
        *(norm_grads[:, k][None] for k in range(4)),
    )


def solution(mesh):
    rows = P(None, "rep", "shard", None)
    outs = P("section", None, "rep", "shard", None)
    matrix = P("section", "shard", None)
    vector = P("section", "shard")
    return jax.shard_map(
        on_device,
        mesh=mesh,
        in_specs=(
            rows, P(None, "rep", "shard"), rows, matrix, vector, matrix, vector, matrix, vector, matrix,
            vector, vector, vector, vector, vector,
        ),
        out_specs=(
            outs, outs, matrix, vector, vector, matrix, vector, matrix, vector, matrix, vector, vector,
            vector, vector, vector,
        ),
        check_vma=False,
    )
```

```python
import functools
import math

import jax
import jax.numpy as jnp
from jax import lax
from jax.experimental import pallas as pl
from jax.experimental.pallas import tpu as pltpu
from jax.sharding import PartitionSpec as P

D = 1024
HEADS = 16
HD = 64
FF = 4096
ROT = 16
epsilon = 1e-05

CHIPS = 16
UNITS = FF // CHIPS
WIDE = 512
TOKENS = 2048
TILE = 256
WINDOW = 512
EARLY = 48
BLOCK = 128
SIDE = 4
OFFSETS = (0, 1, -1, 2)
DOCS = 24
LOG2E = math.log2(math.e)
SCALE = 1.0 / math.sqrt(HD)
MIB = 1024 * 1024

f32 = jnp.float32
bf16 = jnp.bfloat16

SAME_CORE = [[2 * chip + core for chip in range(CHIPS)] for core in range(2)]
LAST = (((1,), (1,)), ((), ()))
FIRST = (((0,), (0,)), ((), ()))


def core_swap(value):
    return lax.ppermute(value, "shard", [(i, i ^ 1) for i in range(2 * CHIPS)])


def section_swap(value):
    return lax.ppermute(value, "section", [(0, 1), (1, 0)])


def cross(value, section):
    pairs = [(2 * (1 - section) + rep, 2 * section + 1 - rep) for rep in range(2)]
    return lax.ppermute(value, ("section", "rep"), pairs)


def plane_gather(rows):
    return lax.all_gather(rows, "shard", axis=0, tiled=True, axis_index_groups=SAME_CORE)


def plane_scatter(partial):
    return lax.psum_scatter(
        partial, "shard", scatter_dimension=0, tiled=True, axis_index_groups=SAME_CORE
    )


def hop(value, second, step):
    pairs = []
    for y in range(SIDE):
        for x in range(SIDE):
            for core in range(2):
                along_x = (core == 0) != second
                to_y, to_x = ((y, (x + step) % SIDE) if along_x else ((y + step) % SIDE, x))
                pairs.append(((y * SIDE + x) * 2 + core, (to_y * SIDE + to_x) * 2 + core))
    return lax.ppermute(value, "shard", pairs)


def row_gather(own):
    return (own, hop(own, False, -1), hop(own, False, 1), hop(own, False, 2))


def ring_gather(own):
    half = own.shape[0] // 2
    after = hop(own, True, -1)
    prior = hop(own, True, 1)
    far_first = hop(prior[:half], True, 1)
    far_last = hop(after[half:], True, -1)
    return (own, after, prior, far_first, far_last)


def block_order(chip, core):
    y, x = (chip // SIDE, chip % SIDE)
    order = []
    for second in OFFSETS:
        for first in OFFSETS:
            step_y, step_x = (jnp.where(core == 0, second, first), jnp.where(core == 0, first, second))
            order.append(((y + step_y) % SIDE) * SIDE + (x + step_x) % SIDE)
    return jnp.stack(order).astype(jnp.int32)


def gather_rows(own):
    return ring_gather(jnp.concatenate(row_gather(own), axis=0))


def add(*terms):
    return sum(term.astype(f32) for term in terms)


def after(value, *others):
    zero = sum(jnp.minimum(jnp.abs(lax.slice(o, (0,) * o.ndim, (1,) * o.ndim).reshape(())), 0) for o in others)
    return value + zero.astype(value.dtype)


def scatter_rows(parts, weight, order, flipped, first=(), ready=()):
    quarter = SIDE * BLOCK
    half = quarter // 2
    far = blocks_product(parts, weight, order[3 * SIDE :], flipped, bf16, first)
    far_first = hop(far[:half], True, 1)
    far_last = hop(far[half:], True, -1)
    near = blocks_product(parts, weight, order[SIDE : 3 * SIDE], flipped, bf16)
    ahead = jnp.concatenate([add(near[:half], far_first).astype(bf16), near[half:quarter]])
    back = jnp.concatenate(
        [near[quarter : quarter + half], add(near[quarter + half :], far_last).astype(bf16)]
    )
    ahead_first = ahead
    from_back = hop(ahead, True, 1)
    from_ahead = hop(back, True, -1)
    home = blocks_product(parts, weight, order[:SIDE], flipped, f32, ready)
    rows = lambda at, count: add(*(v[at : at + count] for v in (home, from_back, from_ahead)))
    ahead, back, far = (rows(k * BLOCK, BLOCK).astype(bf16) for k in (1, 2, 3))
    summed = add(rows(0, BLOCK), hop(far, False, 2), hop(ahead, False, 1), hop(back, False, -1))
    return (summed, ahead_first, far)


def dot(left, right, dims=None):
    if dims is None:
        return jnp.dot(left, right, preferred_element_type=f32)
    return lax.dot_general(left, right, dims, preferred_element_type=f32)


def norm_rows(rows):
    values = rows.astype(f32)
    centred = values - jnp.mean(values, axis=-1, keepdims=True)
    inverse = lax.rsqrt(jnp.mean(centred * centred, axis=-1, keepdims=True) + epsilon)
    return (centred * inverse, inverse)


def half_turn(rows):
    lane = lax.broadcasted_iota(jnp.int32, rows.shape, 1) % HD
    ahead = pltpu.roll(rows, BLOCK - ROT // 2, 1)
    behind = pltpu.roll(rows, ROT // 2, 1)
    return jnp.where(lane < ROT // 2, ahead, behind)


def fetch_blocks(order_ref, pieces, rows_ref, sems):
    copies = []
    for piece in pieces:
        for block in range(piece.shape[0] // BLOCK):
            slot = len(copies)
            place = pl.multiple_of(order_ref[slot] * BLOCK, BLOCK)
            copy = pltpu.make_async_copy(
                piece.at[pl.ds(block * BLOCK, BLOCK)], rows_ref.at[pl.ds(place, BLOCK)], sems.at[slot]
            )
            copy.start()
            copies.append(copy)
    for copy in copies:
        copy.wait()


def project_kernel(count, order_ref, *refs):
    pieces, refs = (refs[:count], refs[count:])
    w_ref, b_ref, g_ref, c_ref, s_ref, n_ref, q_ref, kv_ref, act_ref, slope_ref, rows_ref, sems = refs

    @pl.when(pl.program_id(0) == 0)
    def _():
        fetch_blocks(order_ref, pieces, rows_ref, sems)

    here = pl.ds(pl.multiple_of(pl.program_id(0) * TILE, TILE), TILE)
    normed, _ = norm_rows(rows_ref[here, :])
    n_ref[...] = normed.astype(bf16)
    first = (normed * g_ref[0:1] + g_ref[1:2]).astype(bf16)
    second = (normed * g_ref[2:3] + g_ref[3:4]).astype(bf16)
    made = dot(first, w_ref[:, : 2 * BLOCK]) + b_ref[:, : 2 * BLOCK]
    cosine, sine = (c_ref[...], s_ref[...])
    query = made[:, :BLOCK]
    query = query * cosine + half_turn(query) * sine
    q_ref[...] = (query * SCALE).astype(bf16)
    pair = made[:, BLOCK:]
    pair = pair * cosine + half_turn(pair) * sine
    kv_ref[...] = pair.astype(bf16)
    up = dot(second, w_ref[:, 2 * BLOCK :]) + b_ref[:, 2 * BLOCK :]
    normal_cdf = 0.5 * (1.0 + lax.erf(up * (1.0 / math.sqrt(2.0))))
    act_ref[...] = (up * normal_cdf).astype(bf16)
    bell = jnp.exp(-0.5 * up * up) * (1.0 / math.sqrt(2.0 * math.pi))
    slope_ref[...] = (normal_cdf + up * bell).astype(bf16)


def tile_rows(width):
    return pl.BlockSpec((TILE, width), lambda i, order: (i, 0))


def whole_of(height, width):
    return pl.BlockSpec((height, width), lambda i, order: (0, 0))


def out_rows(width):
    return jax.ShapeDtypeStruct((TOKENS, width), bf16)


def unused(ties):
    return [pl.BlockSpec(memory_space=pl.ANY)] * len(ties)


def project(order, pieces, weight, shift, gains, cosine, sine):
    return pl.pallas_call(
        functools.partial(project_kernel, len(pieces)),
        grid_spec=pltpu.PrefetchScalarGridSpec(
            num_scalar_prefetch=1,
            grid=(TOKENS // TILE,),
            in_specs=[pl.BlockSpec(memory_space=pltpu.HBM)] * len(pieces)
            + [whole_of(D, WIDE), whole_of(1, WIDE), whole_of(4, D), tile_rows(BLOCK), tile_rows(BLOCK)],
            out_specs=[tile_rows(w) for w in (D, BLOCK, BLOCK, UNITS, UNITS)],
            scratch_shapes=[pltpu.VMEM((TOKENS, D), bf16), pltpu.SemaphoreType.DMA((CHIPS,))],
        ),
        out_shape=[pltpu.HBM((TOKENS, D), bf16)] + [out_rows(w) for w in (BLOCK, BLOCK, UNITS, UNITS)],
        compiler_params=pltpu.CompilerParams(vmem_limit_bytes=14 * MIB),
        cost_estimate=pl.CostEstimate(
            flops=2 * TOKENS * D * WIDE, bytes_accessed=12 * MIB, transcendentals=2 * TOKENS * UNITS
        ),
        name="project",
    )(order, *pieces, weight, shift, gains, cosine, sine)


def pull_back_kernel(count, order_ref, *refs):
    pieces, refs = (refs[:count], refs[count:])
    w_ref, slope_ref = refs[:2]
    do_ref, e_ref, g_ref, rows_ref, sems = refs[-5:]

    @pl.when(pl.program_id(0) == 0)
    def _():
        fetch_blocks(order_ref, pieces, rows_ref, sems)

    here = pl.ds(pl.multiple_of(pl.program_id(0) * TILE, TILE), TILE)
    grad = rows_ref[here, :]
    g_ref[...] = grad
    back = dot(grad, w_ref[...], LAST)
    e_ref[...] = (back[:, :UNITS] * slope_ref[...].astype(f32)).astype(bf16)
    do_ref[...] = back[:, UNITS:]


def pull_back(order, pieces, weight, slope, ties=()):
    return pl.pallas_call(
        functools.partial(pull_back_kernel, len(pieces)),
        grid_spec=pltpu.PrefetchScalarGridSpec(
            num_scalar_prefetch=1,
            grid=(TOKENS // TILE,),
            in_specs=[pl.BlockSpec(memory_space=pltpu.HBM)] * len(pieces)
            + [whole_of(UNITS + BLOCK, D), tile_rows(UNITS)]
            + unused(ties),
            out_specs=[tile_rows(w) for w in (BLOCK, UNITS, D)],
            scratch_shapes=[pltpu.VMEM((TOKENS, D), bf16), pltpu.SemaphoreType.DMA((CHIPS,))],
        ),
        out_shape=[jax.ShapeDtypeStruct((TOKENS, BLOCK), f32), out_rows(UNITS), pltpu.HBM((TOKENS, D), bf16)],
        compiler_params=pltpu.CompilerParams(vmem_limit_bytes=14 * MIB),
        cost_estimate=pl.CostEstimate(
            flops=2 * TOKENS * D * (UNITS + BLOCK), bytes_accessed=12 * MIB, transcendentals=0
        ),
        name="pull_back",
    )(order, *pieces, weight, slope, *ties)


def blocks_product_kernel(count, flipped, order_ref, *refs):
    w_ref, out_ref = (refs[count * SIDE], refs[-1])
    columns = [
        jnp.concatenate([refs[part * SIDE + block][...] for block in range(SIDE)], axis=0)
        for part in range(count)
    ]
    left = jnp.concatenate(columns, axis=1)
    out_ref[...] = dot(left, w_ref[...], LAST if flipped else None).astype(out_ref.dtype)


def blocks_product(parts, weight, order, flipped, dtype, ties=()):
    def block(width, which):
        return pl.BlockSpec((BLOCK, width), lambda i, order: (order[i * SIDE + which], 0))

    groups = order.shape[0] // SIDE
    depth = sum(part.shape[1] for part in parts)
    return pl.pallas_call(
        functools.partial(blocks_product_kernel, len(parts), flipped),
        grid_spec=pltpu.PrefetchScalarGridSpec(
            num_scalar_prefetch=1,
            grid=(groups,),
            in_specs=[block(part.shape[1], which) for part in parts for which in range(SIDE)]
            + [whole_of(*weight.shape)]
            + unused(ties),
            out_specs=pl.BlockSpec((SIDE * BLOCK, D), lambda i, order: (i, 0)),
        ),
        out_shape=jax.ShapeDtypeStruct((groups * SIDE * BLOCK, D), dtype),
        compiler_params=pltpu.CompilerParams(vmem_limit_bytes=10 * MIB),
        cost_estimate=pl.CostEstimate(
            flops=2 * groups * SIDE * BLOCK * depth * D, bytes_accessed=2 * MIB + groups * MIB, transcendentals=0
        ),
        name="blocks_product",
    )(order, *[part for part in parts for _ in range(SIDE)], weight, *ties)


def key_places(tile, core):
    row = lax.broadcasted_iota(jnp.int32, (WINDOW, 1), 0)
    return tile * (2 * WINDOW) + (row // BLOCK) * (2 * BLOCK) + core * BLOCK + row % BLOCK


def query_places(tile, core):
    row = lax.broadcasted_iota(jnp.int32, (1, WINDOW), 1)
    return tile * (2 * WINDOW) + (row // BLOCK) * (2 * BLOCK) + core * BLOCK + row % BLOCK


def turned(rows):
    return jnp.transpose(rows.astype(f32)).astype(bf16)


def attend_kernel(
    info_ref, q_ref, start_ref, own_ref, other_ref, o_ref, wide_ref, top_ref, over_ref, vt_ref
):
    tile = pl.program_id(0)
    core = info_ref[2 * (TOKENS // WINDOW)]

    @pl.when(tile == 0)
    def _():
        for part in range(TOKENS // BLOCK):
            rows = pl.ds(part * BLOCK, BLOCK)
            for which, ref in enumerate((own_ref, other_ref)):
                pair = turned(ref[rows, :])
                vt_ref[which, :, rows] = jnp.concatenate([pair[HD:], jnp.ones((16, BLOCK), bf16)], axis=0)

    query = q_ref[...]
    starts = start_ref[...]
    places = query_places(tile, core)

    def step(index, carry, masked):
        top, mixed = carry
        rows = pl.ds(pl.multiple_of(index * WINDOW, WINDOW), WINDOW)
        scores = [dot(ref[rows, :], query, LAST) * LOG2E for ref in (own_ref, other_ref)]
        if masked:
            allowed = []
            for which in range(2):
                keys = key_places(index, core if which == 0 else 1 - core)
                allowed.append((keys >= starts) & (keys <= places))
            scores = [jnp.where(a, s, -1e30) for a, s in zip(allowed, scores)]
        highest = jnp.max(jnp.maximum(scores[0], scores[1]), axis=0, keepdims=True)
        raised = jnp.maximum(top, jnp.ceil(highest))
        parts = [jnp.exp2(s - raised) for s in scores]
        if masked:
            parts = [jnp.where(a, p, 0.0) for a, p in zip(allowed, parts)]
        mixed = mixed * jnp.exp2(top - raised)
        for which in range(2):
            mixed = mixed + dot(vt_ref[which, :, rows], parts[which].astype(bf16))
        return (raised, mixed)

    carry = (jnp.full((1, WINDOW), -1e30, f32), jnp.zeros((HD + 16, WINDOW), f32))
    low, clear = (info_ref[tile], info_ref[TOKENS // WINDOW + tile])
    carry = lax.fori_loop(low, clear, functools.partial(step, masked=True), carry)
    carry = lax.fori_loop(clear, tile, functools.partial(step, masked=False), carry)
    top, mixed = step(tile, carry, True)
    over = 1.0 / mixed[HD : HD + 1]
    top_ref[...] = top
    over_ref[...] = over
    spare = (lax.broadcasted_iota(jnp.int32, (HD, WINDOW), 0) == 0).astype(f32)
    mixed = jnp.concatenate([spare, mixed[:HD] * over], axis=0)
    mixed = jnp.transpose(mixed)
    wide_ref[...] = mixed
    o_ref[...] = mixed.astype(bf16)


def attend(info, query, starts, own, other):
    rows = lambda width: pl.BlockSpec((WINDOW, width), lambda i, info: (i, 0))
    line = pl.BlockSpec((1, WINDOW), lambda i, info: (0, i))
    whole = pl.BlockSpec((TOKENS, BLOCK), lambda i, info: (0, 0))
    return pl.pallas_call(
        attend_kernel,
        grid_spec=pltpu.PrefetchScalarGridSpec(
            num_scalar_prefetch=1,
            grid=(TOKENS // WINDOW,),
            in_specs=[rows(BLOCK), line, whole, whole],
            out_specs=[rows(BLOCK), rows(BLOCK), line, line],
            scratch_shapes=[pltpu.VMEM((2, HD + 16, TOKENS), bf16)],
        ),
        out_shape=[
            jax.ShapeDtypeStruct((TOKENS, BLOCK), bf16),
            jax.ShapeDtypeStruct((TOKENS, BLOCK), f32),
            jax.ShapeDtypeStruct((1, TOKENS), f32),
            jax.ShapeDtypeStruct((1, TOKENS), f32),
        ],
        compiler_params=pltpu.CompilerParams(vmem_limit_bytes=32 * MIB),
        cost_estimate=pl.CostEstimate(
            flops=8 * TOKENS * TOKENS * BLOCK, bytes_accessed=4 * MIB, transcendentals=2 * TOKENS * TOKENS
        ),
        name="attend",
    )(info, query, starts, own, other)


def attend_back_kernel(
    info_ref, q_ref, do_ref, o_ref, top_ref, over_ref, start_ref, c_ref, s_ref, own_ref, other_ref, *refs
):
    dq_ref, down_ref, dother_low_ref, kt_ref, dother_ref = refs[-5:]
    tile = pl.program_id(0)
    core = info_ref[2 * (TOKENS // WINDOW)]

    @pl.when(tile == 0)
    def _():
        for part in range(TOKENS // BLOCK):
            rows = pl.ds(part * BLOCK, BLOCK)
            kt_ref[0, :, rows] = turned(own_ref[rows, :])[:HD]
            kt_ref[1, :, rows] = turned(other_ref[rows, :])[:HD]
        down_ref[...] = jnp.zeros_like(down_ref)
        dother_ref[...] = jnp.zeros_like(dother_ref)

    query = q_ref[...]
    top = top_ref[...]
    starts = start_ref[...]
    places = query_places(tile, core)
    turned_grad = (jnp.transpose(do_ref[...]) * over_ref[...]).astype(bf16).astype(f32)
    inner = jnp.sum(turned_grad * jnp.transpose(o_ref[...]), axis=0, keepdims=True)
    grad = jnp.transpose(turned_grad).astype(bf16)

    def step(index, carry, masked):
        rows = pl.ds(pl.multiple_of(index * WINDOW, WINDOW), WINDOW)
        for which, (ref, dref) in enumerate(((own_ref, down_ref), (other_ref, dother_ref))):
            pair = ref[rows, :]
            parts = jnp.exp2(dot(pair, query, LAST) * LOG2E - top)
            if masked:
                keys = key_places(index, core if which == 0 else 1 - core)
                allowed = (keys >= starts) & (keys <= places)
                parts = jnp.where(allowed, parts, 0.0)
            parts = parts.astype(bf16)
            changes = (parts.astype(f32) * (dot(pair, grad, LAST) - inner)).astype(bf16)
            dref[rows, :] += dot(changes, query) + dot(parts, grad)
            carry = carry + dot(kt_ref[which, :, rows], changes)
        return carry

    low, clear = (info_ref[tile], info_ref[TOKENS // WINDOW + tile])
    carry = jnp.zeros((HD, WINDOW), f32)
    carry = lax.fori_loop(low, clear, functools.partial(step, masked=True), carry)
    carry = lax.fori_loop(clear, tile, functools.partial(step, masked=False), carry)
    carry = step(tile, carry, True) * SCALE
    change = jnp.transpose(jnp.concatenate([carry, jnp.zeros((HD, WINDOW), f32)], axis=0))
    dq_ref[...] = (change * c_ref[...] - half_turn(change) * s_ref[...]).astype(bf16)

    @pl.when(tile == TOKENS // WINDOW - 1)
    def _():
        dother_low_ref[...] = dother_ref[...].astype(bf16)


def attend_back(info, query, grad, mixed, top, over, starts, cosine, sine, own, other, ties=()):
    rows = pl.BlockSpec((WINDOW, BLOCK), lambda i, info: (i, 0))
    line = pl.BlockSpec((1, WINDOW), lambda i, info: (0, i))
    whole = pl.BlockSpec((TOKENS, BLOCK), lambda i, info: (0, 0))
    return pl.pallas_call(
        attend_back_kernel,
        grid_spec=pltpu.PrefetchScalarGridSpec(
            num_scalar_prefetch=1,
            grid=(TOKENS // WINDOW,),
            in_specs=[rows, rows, rows, line, line, line, rows, rows, whole, whole] + unused(ties),
            out_specs=[rows, whole, whole],
            scratch_shapes=[pltpu.VMEM((2, HD, TOKENS), bf16), pltpu.VMEM((TOKENS, BLOCK), f32)],
        ),
        out_shape=[
            jax.ShapeDtypeStruct((TOKENS, BLOCK), bf16),
            jax.ShapeDtypeStruct((TOKENS, BLOCK), f32),
            jax.ShapeDtypeStruct((TOKENS, BLOCK), bf16),
        ],
        compiler_params=pltpu.CompilerParams(vmem_limit_bytes=40 * MIB),
        cost_estimate=pl.CostEstimate(
            flops=20 * TOKENS * TOKENS * BLOCK, bytes_accessed=6 * MIB, transcendentals=2 * TOKENS * TOKENS
        ),
        name="attend_back",
    )(info, query, grad, mixed, top, over, starts, cosine, sine, own, other, *ties)


def join_kernel(mine_ref, theirs_ref, c_ref, s_ref, out_ref):
    pair = mine_ref[...] + theirs_ref[...].astype(f32)
    out_ref[...] = (pair * c_ref[...] - half_turn(pair) * s_ref[...]).astype(bf16)


def join_pairs(mine, theirs, cosine, sine):
    rows = pl.BlockSpec((2 * TILE, BLOCK), lambda i: (i, 0))
    return pl.pallas_call(
        join_kernel,
        grid=(TOKENS // (2 * TILE),),
        in_specs=[rows] * 4,
        out_specs=rows,
        out_shape=jax.ShapeDtypeStruct((TOKENS, BLOCK), bf16),
        name="join_pairs",
    )(mine, theirs, cosine, sine)


def pack_kernel(info_ref, up_ref, sum_ref, grads_ref, keep_ref, send_ref):
    core = info_ref[2 * (TOKENS // WINDOW)]
    lane = lax.broadcasted_iota(jnp.int32, (1, BLOCK), 1)
    row = lax.broadcasted_iota(jnp.int32, (16, UNITS), 0)
    for out_ref, which in ((keep_ref, core), (send_ref, 1 - core)):
        for chip in range(CHIPS):
            at = chip * EARLY
            rows = pl.ds(pl.multiple_of(chip * 64 + which * 32, 32), 32)
            out_ref[at : at + 32, :] = up_ref[rows, :].astype(out_ref.dtype)
            sums = grads_ref[UNITS : UNITS + 8, pl.ds(chip // 2 * BLOCK, BLOCK)][:1]
            here = chip % 2 * 64
            first = pltpu.roll(sums, (BLOCK - here) % BLOCK, 1) if here else sums
            mine = jnp.where(which == 0, first, pltpu.roll(sums, BLOCK - here - 32, 1))
            mine = jnp.concatenate([jnp.where(lane < 32, mine, 0.0), jnp.zeros((1, BLOCK), f32)], axis=1)
            extra = jnp.where(row == 0, sum_ref[...], jnp.where(row == 1, mine, 0.0))
            out_ref[at + 32 : at + EARLY, :] = extra.astype(out_ref.dtype)
        heads = pl.ds(pl.multiple_of(UNITS + HD + which * 32, 32), 32)
        units = pl.ds(pl.multiple_of(which * BLOCK, BLOCK), BLOCK)
        for part in range(D // UNITS):
            at = CHIPS * EARLY + part * 160
            columns = pl.ds(part * UNITS, UNITS)
            out_ref[at : at + 32, :] = grads_ref[heads, columns].astype(out_ref.dtype)
            out_ref[at + 32 : at + 160, :] = grads_ref[units, columns].astype(out_ref.dtype)


def pack(info, up_grads, up_sum, grads):
    rows = CHIPS * EARLY + 160 * (D // UNITS)
    return pl.pallas_call(
        pack_kernel,
        grid_spec=pltpu.PrefetchScalarGridSpec(
            num_scalar_prefetch=1,
            grid=(1,),
            in_specs=[whole_of(D, UNITS), whole_of(1, UNITS), whole_of(UNITS + BLOCK, D)],
            out_specs=[whole_of(rows, UNITS), whole_of(rows, UNITS)],
        ),
        out_shape=[
            jax.ShapeDtypeStruct((rows, UNITS), f32),
            jax.ShapeDtypeStruct((rows, UNITS), bf16),
        ],
        compiler_params=pltpu.CompilerParams(vmem_limit_bytes=16 * MIB),
        cost_estimate=pl.CostEstimate(flops=4 * MIB, bytes_accessed=5 * MIB, transcendentals=0),
        name="pack",
    )(info, up_grads, up_sum, grads)


def finish_kernel(got_ref, qkv_ref, up_ref, norm_ref, qkv_out, up_out, qkv_sum_ref, up_sum_ref, norm_out):
    gain1, shift1, gain2, shift2 = (norm_ref[:, k : k + 1] for k in range(4))
    first = lax.broadcasted_iota(jnp.int32, (32, BLOCK), 1) < HD
    total = [jnp.zeros((32, 1), f32) for _ in range(4)]
    across = lambda values: jnp.sum(values, axis=1, keepdims=True)
    for chip in range(0, CHIPS, 2):
        tiles = [got_ref[chip + k, EARLY:, :].astype(f32) for k in range(2)]
        (low0, high0), (low1, high1) = ((t[:, :BLOCK], t[:, BLOCK:]) for t in tiles)
        turn = lambda values: pltpu.roll(values, HD, 1)
        cores = (
            jnp.where(first, low0, turn(low1)),
            jnp.where(first, high0, turn(high1)),
            jnp.where(first, turn(high0), high1),
        )
        notes = jnp.where(first, turn(low0), low1)
        for part, (core, row) in enumerate(zip(cores, (0, 2, 3))):
            at = pl.ds(part * D + chip * HD, BLOCK)
            sums = notes[row : row + 1]
            weight = qkv_ref[:, at].astype(f32)
            qkv_out[:, at] = gain1 * core + shift1 * sums
            qkv_sum_ref[:, at] = sums
            total[0] += across(weight * core)
            total[1] += across(weight * sums)
    for chip in range(CHIPS):
        at = pl.ds(chip * UNITS, UNITS)
        core = got_ref[chip, :32, :].astype(f32)
        sums = got_ref[chip, 32:EARLY, :].astype(f32)[:1]
        weight = up_ref[:, at].astype(f32)
        up_out[:, at] = gain2 * core + shift2 * sums
        up_sum_ref[:, at] = sums
        total[2] += across(weight * core)
        total[3] += across(weight * sums)
    lane = lax.broadcasted_iota(jnp.int32, (32, BLOCK), 1)
    out = jnp.zeros((32, BLOCK), f32)
    for k in range(4):
        out = jnp.where(lane == k, total[k], out)
    norm_out[...] = out


def finish(got, qkv_weight, up_weight, norms):
    shape = lambda *dims: jax.ShapeDtypeStruct(dims, f32)
    return pl.pallas_call(
        finish_kernel,
        out_shape=[shape(32, 3 * D), shape(32, FF), shape(1, 3 * D), shape(1, FF), shape(32, BLOCK)],
        compiler_params=pltpu.CompilerParams(vmem_limit_bytes=10 * MIB),
        cost_estimate=pl.CostEstimate(flops=8 * 32 * 7 * D, bytes_accessed=3 * MIB, transcendentals=0),
        name="finish",
    )(got, qkv_weight, up_weight, norms)


def on_device(
    inputs,
    segments,
    cotangent,
    qkv_weight,
    qkv_bias,
    dense_weight,
    dense_bias,
    fc_in_weight,
    fc_in_bias,
    fc_out_weight,
    fc_out_bias,
    norm1_gain,
    norm1_bias,
    norm2_gain,
    norm2_bias,
):
    section = lax.axis_index("section")
    place = lax.axis_index("shard")
    chip, core = (place // 2, place % 2)
    first_layer = section == 0
    x0 = lax.dynamic_index_in_dim(inputs, section, 0, keepdims=False)[0]
    out_grad = lax.dynamic_index_in_dim(cotangent, section, 0, keepdims=False)[0]
    my_segs = lax.dynamic_index_in_dim(segments, section, 0, keepdims=False)[0]

    x0_all = plane_gather(x0)
    grad1_all = plane_gather(out_grad)

    pieces = lambda vector: vector.astype(bf16).reshape(-1, 32)
    vectors = jnp.concatenate(
        [
            pieces(v[0])
            for v in (
                norm1_gain, norm1_bias, norm2_gain, norm2_bias, qkv_bias, fc_in_bias, dense_bias, fc_out_bias,
            )
        ]
    )
    vectors_away = section_swap(vectors)
    spare = jnp.concatenate([pieces(my_segs), vectors, vectors_away, jnp.zeros((2, 32), bf16)])
    spare = jnp.concatenate([spare[:16], spare[16:]], axis=1).reshape(1, 1, 16, HD)
    heads = qkv_weight[0].reshape(2, 16, 3, CHIPS, HD).transpose(3, 0, 1, 2, 4)
    units = fc_in_weight[0].reshape(2, 16, CHIPS, UNITS).transpose(2, 0, 1, 3)
    cut = jnp.concatenate(
        [
            heads[..., 0, :],
            jnp.broadcast_to(spare, (CHIPS, 2, 16, HD)),
            heads[..., 1, :],
            heads[..., 2, :],
            units,
        ],
        axis=-1,
    ).reshape(2 * CHIPS, 16, WIDE)
    got = lax.all_to_all(cut, "shard", 0, 0, tiled=True)
    notes = got[:, :, HD:BLOCK]
    notes = jnp.concatenate([notes[..., :32], notes[..., 32:]], axis=1)
    rows_own = jnp.concatenate([dense_weight[0], fc_out_weight[0]], axis=0)
    rows_away = section_swap(rows_own)
    got_away = section_swap(got)
    got_pair = jnp.stack([got, got_away])
    rows_pair = jnp.stack([rows_own, rows_away])
    got_other = core_swap(got_pair)
    rows_other = core_swap(rows_pair)

    def by_core(mine, theirs, axis):
        return jnp.where(
            core == 0, jnp.stack([mine, theirs], axis), jnp.stack([theirs, mine], axis)
        )

    columns_both = by_core(got_pair, got_other, 2).reshape(2, D, WIDE)
    head_rows = by_core(rows_pair[:, :32], rows_other[:, :32], 1).reshape(2, HD, D)
    unit_rows = by_core(rows_pair[:, 32:], rows_other[:, 32:], 1).reshape(2, UNITS, D)
    out_both = jnp.concatenate([unit_rows, jnp.zeros((2, HD, D), bf16), head_rows], axis=1)
    notes_both = (notes[:, 4:17], notes[:, 17:30])

    def layer_weights(layer):
        mine = first_layer == (layer == 0)
        pick = lambda both: jnp.where(mine, both[0], both[1])
        columns, note = (pick(columns_both).astype(f32), pick(notes_both))
        vector = lambda at, count: note[:, at : at + count].reshape(-1).astype(f32)
        gain1, shift1, gain2, shift2 = (vector(k, 1) for k in range(4))
        attn_bias = vector(4, 3).reshape(3, CHIPS, HD)
        attn_bias = lax.dynamic_index_in_dim(attn_bias, chip, 1, keepdims=False)
        up_bias = lax.dynamic_slice_in_dim(vector(7, 4), chip * UNITS, UNITS, 0)
        out_bias = vector(11, 1) + vector(12, 1)
        lane = jnp.arange(WIDE)
        gains = jnp.where(lane[None, :] < 2 * BLOCK, gain1[:, None], gain2[:, None])
        used = (lane < HD) | (lane >= BLOCK)
        bias = jnp.concatenate(
            [attn_bias[0], jnp.zeros((HD,), f32), attn_bias[1], attn_bias[2], up_bias]
        )
        shift = bias[None, :]
        plain = jnp.where(used[None, :], columns, 0.0).astype(bf16)
        scaled = jnp.where(used[None, :], columns * gains, 0.0).astype(bf16)
        lines = jnp.stack([gain1, shift1, gain2, shift2])
        return (plain, scaled, shift, lines, pick(out_both), out_bias)

    segs = notes[:, :4].astype(jnp.int32)
    numbers = jnp.arange(DOCS, dtype=jnp.int32)
    before = jnp.sum((segs.reshape(1, -1) < numbers[:, None]).astype(jnp.int32), axis=1)
    steps = before - jnp.concatenate([jnp.zeros((1,), jnp.int32), before[:-1]])
    my_rows = lax.dynamic_index_in_dim(
        segs.reshape(CHIPS, 2, BLOCK), core, 1, keepdims=False
    ).reshape(TOKENS)
    starts = jnp.sum(jnp.where(my_rows[None, :] >= numbers[:, None], steps[:, None], 0), axis=0)
    token = jnp.arange(TOKENS, dtype=jnp.int32)
    token = (token // BLOCK) * (2 * BLOCK) + core * BLOCK + token % BLOCK
    half_rot = ROT // 2
    frequency = jnp.exp(jnp.arange(half_rot, dtype=f32) * (-2.0 * math.log(10000.0) / ROT))
    angles = frequency[:, None] * (token - starts).astype(f32)[None, :]
    cos_rows, sin_rows = (jnp.cos(angles), jnp.sin(angles))
    ones = lambda count: jnp.ones((count, TOKENS), f32)
    zeros = lambda count: jnp.zeros((count, TOKENS), f32)
    cosine = jnp.concatenate([cos_rows, cos_rows, ones(BLOCK - ROT)], axis=0).T
    sine = jnp.concatenate([-sin_rows, sin_rows, zeros(BLOCK - ROT)], axis=0).T
    tiles = starts.reshape(TOKENS // WINDOW, WINDOW)
    low_tile = tiles[:, 0] // (2 * WINDOW)
    clear_tile = jnp.minimum(
        (tiles[:, -1] + 2 * WINDOW - 1) // (2 * WINDOW),
        jnp.arange(TOKENS // WINDOW, dtype=jnp.int32),
    )
    info = jnp.concatenate([low_tile, clear_tile, core[None], jnp.zeros((7,), jnp.int32)])
    start_line = starts[None, :]

    order = block_order(chip, core)
    straight = jnp.arange(CHIPS, dtype=jnp.int32)

    def forward(pieces, arranged, weights):
        plain, _, shift, lines, _, _ = weights
        normed, query, own, act, slope = project(
            arranged, pieces, plain, shift, lines, cosine, sine
        )
        other = core_swap(own)
        mixed, wide, top, over = attend(info, query, start_line, own, other)
        return (normed, query, own, other, act, slope, mixed, wide, top, over)

    def pulled(pieces, arranged, weights, kept, ties=()):
        return pull_back(arranged, pieces, weights[4], kept[5], ties)

    def by_owner(parts):
        return parts.reshape(CHIPS, 2, 32, parts.shape[-1])

    def early_grads(kept, changed, grad_all):
        up_grads = dot(kept[0], changed, FIRST)
        grads = dot(jnp.concatenate([kept[4], kept[6]], axis=1), grad_all, FIRST)
        up_sum = jnp.sum(changed.astype(f32), axis=0, keepdims=True)
        keep, send = pack(info, up_grads, up_sum, grads)
        return add(keep, core_swap(send)).astype(bf16)

    def over_cores(parts):
        keep, send = (
            jnp.concatenate(
                [lax.dynamic_index_in_dim(part, which, 0, keepdims=False) for part in parts]
            )
            for which in (core, 1 - core)
        )
        send = send.astype(bf16)
        return (add(keep, core_swap(send)), send)

    def attended(grad_mixed, kept, ties=()):
        _, query, own, other, _, _, _, wide, top, over = kept
        dq, d_own, d_other = attend_back(
            info, query, grad_mixed, wide, top, over, start_line, cosine, sine, own, other, ties
        )
        return (dq, join_pairs(d_own, core_swap(d_other), cosine, sine))

    def late_grads(normed, dq, d_pair):
        made = jnp.concatenate([dq, d_pair], axis=1)
        grads = by_owner(dot(normed, made, FIRST))
        sums = jnp.sum(made.astype(f32), axis=0).reshape(1, 1, 4, HD)
        extra = jnp.pad(jnp.broadcast_to(sums, (CHIPS, 2, 4, HD)), ((0, 0), (0, 0), (0, 28), (0, 0)))
        grads = jnp.concatenate([grads[..., :HD], extra, grads[..., BLOCK:]], axis=-1)
        return grads.transpose(1, 0, 2, 3).reshape(2, CHIPS * 32, 2 * BLOCK)

    def norm_back(rows, grad, summed):
        here, inverse = norm_rows(rows)
        inner_part = (
            summed
            - jnp.mean(summed, axis=-1, keepdims=True)
            - here * jnp.mean(summed * here, axis=-1, keepdims=True)
        )
        return (grad.astype(f32) + inverse * inner_part).astype(bf16)

    weights0, weights1 = (layer_weights(0), layer_weights(1))
    kept0 = forward((x0_all,), straight, weights0)
    ready = (weights0[1], weights1[0], weights1[1], weights1[2])
    summed, _, _ = scatter_rows((kept0[4], kept0[6]), weights0[4], order, False, (), ready)
    x1 = (add(x0, summed) + weights0[5][None, :]).astype(bf16)
    x1, grad1_all = lax.optimization_barrier((x1, grad1_all))
    kept1 = forward(gather_rows(x1), order, weights1)
    grad_mixed, changed1, grad1_all = pulled((grad1_all,), straight, weights1, kept1)
    dq1, d_pair1 = attended(grad_mixed, kept1)
    inner = jnp.concatenate([kept1[4], after(kept1[6], dq1)], axis=1)
    summed = plane_scatter(dot(inner, weights1[4]).astype(bf16))
    x2 = (add(x1, summed) + weights1[5][None, :]).astype(bf16)
    summed, _, _ = scatter_rows((dq1, d_pair1, changed1), weights1[1], order, True)
    grad1 = norm_back(x1, out_grad, summed)
    early1 = early_grads(kept1, changed1, grad1_all)
    late1, _ = over_cores([late_grads(kept1[0], dq1, d_pair1)])
    layer1 = jnp.concatenate([late1.astype(bf16), early1])
    half1 = add(layer1, section_swap(layer1)).astype(bf16)
    layer1 = add(half1, cross(half1, 1)).astype(bf16)

    grad_mixed, changed0, grad0_all = pulled(
        gather_rows(grad1), order, weights0, kept0, (half1,)
    )
    early0 = early_grads(kept0, changed0, grad0_all)
    dq0, d_pair0 = attended(grad_mixed, kept0, (x2, layer1))
    late0, send = over_cores([late_grads(kept0[0], dq0, d_pair0)])
    summed, held, step = scatter_rows(
        (dq0, d_pair0, changed0), weights0[1], order, True, (send,)
    )
    half0 = add(after(early0, held), section_swap(early0)).astype(bf16)
    early0 = add(after(half0, step), cross(half0, 0)).astype(bf16)
    grad0 = norm_back(x0, grad1, summed)

    def placed(layer0, layer1):
        mine = jnp.where(first_layer, layer0, layer1)
        theirs = section_swap(jnp.where(first_layer, layer1, layer0))
        return jnp.where(
            first_layer, jnp.stack([mine, theirs]), jnp.stack([theirs, mine])
        )[None, :, None]

    section_outputs = placed(x1, x2)
    input_grads = placed(grad0, grad1)

    late0 = late0.astype(bf16)
    half0 = add(late0, section_swap(late0)).astype(bf16)
    late0 = add(half0, cross(half0, 0))
    late0 = after(late0, step).astype(bf16)
    parts = jnp.where(first_layer, jnp.concatenate([late0, early0]), layer1)
    late, early, rows = jnp.split(parts, [CHIPS * 32, CHIPS * (32 + EARLY)])
    row_sum = jnp.concatenate(jnp.split(rows, D // UNITS), axis=1).astype(f32)
    parts = jnp.concatenate([part.reshape(CHIPS, -1, UNITS) for part in (early, late)], axis=1)
    got = lax.all_to_all(parts, "shard", 0, 0, tiled=True, axis_index_groups=SAME_CORE)
    column = lambda vector: vector[0].astype(f32)[:, None]
    norms = jnp.concatenate([column(v) for v in (norm1_gain, norm1_bias, norm2_gain, norm2_bias)], axis=1)
    qkv_grad, up_grad, qkv_sum, up_sum, norm_grads = finish(got, qkv_weight[0], fc_in_weight[0], norms)
    shift_grad = got[0, 33, :32].astype(f32)
    mine_of = lambda vector, at, width: lax.dynamic_slice_in_dim(
        vector, at + place * width, width, 1
    )
    return (
        section_outputs,
        input_grads,
        qkv_grad[None],
        mine_of(qkv_sum[:, : 2 * D], 0, 64),
        mine_of(qkv_sum[:, 2 * D :], 0, 32),
        row_sum[None, :32],
        shift_grad[None],
        up_grad[None],
        mine_of(up_sum, 0, 128),
        row_sum[None, 32:],
        shift_grad[None],
        *(norm_grads[:, k][None] for k in range(4)),
    )


def solution(mesh):
    rows = P(None, "rep", "shard", None)
    outs = P("section", None, "rep", "shard", None)
    matrix = P("section", "shard", None)
    vector = P("section", "shard")
    return jax.shard_map(
        on_device,
        mesh=mesh,
        in_specs=(
            rows, P(None, "rep", "shard"), rows, matrix, vector, matrix, vector, matrix, vector, matrix,
            vector, vector, vector, vector, vector,
        ),
        out_specs=(
            outs, outs, matrix, vector, vector, matrix, vector, matrix, vector, matrix, vector, vector,
            vector, vector, vector,
        ),
        check_vma=False,
    )
```

```python
import functools
import math

import jax
import jax.numpy as jnp
from jax import lax
from jax.experimental import pallas as pl
from jax.experimental.pallas import tpu as pltpu
from jax.sharding import PartitionSpec as P

D = 1024
HEADS = 16
HD = 64
FF = 4096
ROT = 16
epsilon = 1e-05

CHIPS = 16
UNITS = FF // CHIPS
WIDE = 512
TOKENS = 2048
TILE = 256
WINDOW = 512
EARLY = 48
BLOCK = 128
SIDE = 4
OFFSETS = (0, 1, -1, 2)
DOCS = 24
LOG2E = math.log2(math.e)
SCALE = 1.0 / math.sqrt(HD)
MIB = 1024 * 1024

f32 = jnp.float32
bf16 = jnp.bfloat16

SAME_CORE = [[2 * chip + core for chip in range(CHIPS)] for core in range(2)]
LAST = (((1,), (1,)), ((), ()))
FIRST = (((0,), (0,)), ((), ()))


def core_swap(value):
    return lax.ppermute(value, "shard", [(i, i ^ 1) for i in range(2 * CHIPS)])


def section_swap(value):
    return lax.ppermute(value, "section", [(0, 1), (1, 0)])


def cross(value, section):
    pairs = [(2 * (1 - section) + rep, 2 * section + 1 - rep) for rep in range(2)]
    return lax.ppermute(value, ("section", "rep"), pairs)


def plane_gather(rows):
    return lax.all_gather(rows, "shard", axis=0, tiled=True, axis_index_groups=SAME_CORE)


def plane_scatter(partial):
    return lax.psum_scatter(
        partial, "shard", scatter_dimension=0, tiled=True, axis_index_groups=SAME_CORE
    )


def hop(value, second, step):
    pairs = []
    for y in range(SIDE):
        for x in range(SIDE):
            for core in range(2):
                along_x = (core == 0) != second
                to_y, to_x = ((y, (x + step) % SIDE) if along_x else ((y + step) % SIDE, x))
                pairs.append(((y * SIDE + x) * 2 + core, (to_y * SIDE + to_x) * 2 + core))
    return lax.ppermute(value, "shard", pairs)


def row_gather(own):
    return (own, hop(own, False, -1), hop(own, False, 1), hop(own, False, 2))


def ring_gather(own):
    half = own.shape[0] // 2
    after = hop(own, True, -1)
    prior = hop(own, True, 1)
    far_first = hop(prior[:half], True, 1)
    far_last = hop(after[half:], True, -1)
    return (own, after, prior, far_first, far_last)


def block_order(chip, core):
    y, x = (chip // SIDE, chip % SIDE)
    order = []
    for second in OFFSETS:
        for first in OFFSETS:
            step_y, step_x = (jnp.where(core == 0, second, first), jnp.where(core == 0, first, second))
            order.append(((y + step_y) % SIDE) * SIDE + (x + step_x) % SIDE)
    return jnp.stack(order).astype(jnp.int32)


def gather_rows(own):
    return ring_gather(jnp.concatenate(row_gather(own), axis=0))


def add(*terms):
    return sum(term.astype(f32) for term in terms)


def after(value, *others):
    zero = sum(jnp.minimum(jnp.abs(lax.slice(o, (0,) * o.ndim, (1,) * o.ndim).reshape(())), 0) for o in others)
    return value + zero.astype(value.dtype)


def scatter_rows(parts, weight, order, flipped, first=(), ready=()):
    quarter = SIDE * BLOCK
    half = quarter // 2
    far = blocks_product(parts, weight, order[3 * SIDE :], flipped, bf16, first)
    far_first = hop(far[:half], True, 1)
    far_last = hop(far[half:], True, -1)
    near = blocks_product(parts, weight, order[SIDE : 3 * SIDE], flipped, bf16)
    ahead = jnp.concatenate([add(near[:half], far_first).astype(bf16), near[half:quarter]])
    back = jnp.concatenate(
        [near[quarter : quarter + half], add(near[quarter + half :], far_last).astype(bf16)]
    )
    ahead_first = ahead
    from_back = hop(ahead, True, 1)
    from_ahead = hop(back, True, -1)
    home = blocks_product(parts, weight, order[:SIDE], flipped, f32, ready)
    rows = lambda at, count: add(*(v[at : at + count] for v in (home, from_back, from_ahead)))
    ahead, back, far = (rows(k * BLOCK, BLOCK).astype(bf16) for k in (1, 2, 3))
    summed = add(rows(0, BLOCK), hop(far, False, 2), hop(ahead, False, 1), hop(back, False, -1))
    return (summed, ahead_first, far)


def dot(left, right, dims=None):
    if dims is None:
        return jnp.dot(left, right, preferred_element_type=f32)
    return lax.dot_general(left, right, dims, preferred_element_type=f32)


def norm_rows(rows):
    values = rows.astype(f32)
    centred = values - jnp.mean(values, axis=-1, keepdims=True)
    inverse = lax.rsqrt(jnp.mean(centred * centred, axis=-1, keepdims=True) + epsilon)
    return (centred * inverse, inverse)


def half_turn(rows):
    lane = lax.broadcasted_iota(jnp.int32, rows.shape, 1) % HD
    ahead = pltpu.roll(rows, BLOCK - ROT // 2, 1)
    behind = pltpu.roll(rows, ROT // 2, 1)
    return jnp.where(lane < ROT // 2, ahead, behind)


def fetch_blocks(order_ref, pieces, rows_ref, sems):
    copies = []
    for piece in pieces:
        for block in range(piece.shape[0] // BLOCK):
            slot = len(copies)
            place = pl.multiple_of(order_ref[slot] * BLOCK, BLOCK)
            copy = pltpu.make_async_copy(
                piece.at[pl.ds(block * BLOCK, BLOCK)], rows_ref.at[pl.ds(place, BLOCK)], sems.at[slot]
            )
            copy.start()
            copies.append(copy)
    for copy in copies:
        copy.wait()


def project_kernel(count, order_ref, *refs):
    pieces, refs = (refs[:count], refs[count:])
    w_ref, b_ref, g_ref, c_ref, s_ref, n_ref, q_ref, kv_ref, act_ref, slope_ref, rows_ref, sems = refs

    @pl.when(pl.program_id(0) == 0)
    def _():
        fetch_blocks(order_ref, pieces, rows_ref, sems)

    here = pl.ds(pl.multiple_of(pl.program_id(0) * TILE, TILE), TILE)
    normed, _ = norm_rows(rows_ref[here, :])
    n_ref[...] = normed.astype(bf16)
    first = (normed * g_ref[0:1] + g_ref[1:2]).astype(bf16)
    second = (normed * g_ref[2:3] + g_ref[3:4]).astype(bf16)
    made = dot(first, w_ref[:, : 2 * BLOCK]) + b_ref[:, : 2 * BLOCK]
    cosine, sine = (c_ref[...], s_ref[...])
    query = made[:, :BLOCK]
    query = query * cosine + half_turn(query) * sine
    q_ref[...] = (query * SCALE).astype(bf16)
    pair = made[:, BLOCK:]
    pair = pair * cosine + half_turn(pair) * sine
    kv_ref[...] = pair.astype(bf16)
    up = dot(second, w_ref[:, 2 * BLOCK :]) + b_ref[:, 2 * BLOCK :]
    normal_cdf = 0.5 * (1.0 + lax.erf(up * (1.0 / math.sqrt(2.0))))
    act_ref[...] = (up * normal_cdf).astype(bf16)
    bell = jnp.exp(-0.5 * up * up) * (1.0 / math.sqrt(2.0 * math.pi))
    slope_ref[...] = (normal_cdf + up * bell).astype(bf16)


def tile_rows(width):
    return pl.BlockSpec((TILE, width), lambda i, order: (i, 0))


def whole_of(height, width):
    return pl.BlockSpec((height, width), lambda i, order: (0, 0))


def out_rows(width):
    return jax.ShapeDtypeStruct((TOKENS, width), bf16)


def unused(ties):
    return [pl.BlockSpec(memory_space=pl.ANY)] * len(ties)


def project(order, pieces, weight, shift, gains, cosine, sine):
    return pl.pallas_call(
        functools.partial(project_kernel, len(pieces)),
        grid_spec=pltpu.PrefetchScalarGridSpec(
            num_scalar_prefetch=1,
            grid=(TOKENS // TILE,),
            in_specs=[pl.BlockSpec(memory_space=pltpu.HBM)] * len(pieces)
            + [whole_of(D, WIDE), whole_of(1, WIDE), whole_of(4, D), tile_rows(BLOCK), tile_rows(BLOCK)],
            out_specs=[tile_rows(w) for w in (D, BLOCK, BLOCK, UNITS, UNITS)],
            scratch_shapes=[pltpu.VMEM((TOKENS, D), bf16), pltpu.SemaphoreType.DMA((CHIPS,))],
        ),
        out_shape=[pltpu.HBM((TOKENS, D), bf16)] + [out_rows(w) for w in (BLOCK, BLOCK, UNITS, UNITS)],
        compiler_params=pltpu.CompilerParams(vmem_limit_bytes=14 * MIB),
        cost_estimate=pl.CostEstimate(
            flops=2 * TOKENS * D * WIDE, bytes_accessed=12 * MIB, transcendentals=2 * TOKENS * UNITS
        ),
        name="project",
    )(order, *pieces, weight, shift, gains, cosine, sine)


def pull_back_kernel(count, order_ref, *refs):
    pieces, refs = (refs[:count], refs[count:])
    w_ref, slope_ref = refs[:2]
    do_ref, e_ref, g_ref, rows_ref, sems = refs[-5:]

    @pl.when(pl.program_id(0) == 0)
    def _():
        fetch_blocks(order_ref, pieces, rows_ref, sems)

    here = pl.ds(pl.multiple_of(pl.program_id(0) * TILE, TILE), TILE)
    grad = rows_ref[here, :]
    g_ref[...] = grad
    back = dot(grad, w_ref[...], LAST)
    e_ref[...] = (back[:, :UNITS] * slope_ref[...].astype(f32)).astype(bf16)
    do_ref[...] = back[:, UNITS:]


def pull_back(order, pieces, weight, slope, ties=()):
    return pl.pallas_call(
        functools.partial(pull_back_kernel, len(pieces)),
        grid_spec=pltpu.PrefetchScalarGridSpec(
            num_scalar_prefetch=1,
            grid=(TOKENS // TILE,),
            in_specs=[pl.BlockSpec(memory_space=pltpu.HBM)] * len(pieces)
            + [whole_of(UNITS + BLOCK, D), tile_rows(UNITS)]
            + unused(ties),
            out_specs=[tile_rows(w) for w in (BLOCK, UNITS, D)],
            scratch_shapes=[pltpu.VMEM((TOKENS, D), bf16), pltpu.SemaphoreType.DMA((CHIPS,))],
        ),
        out_shape=[jax.ShapeDtypeStruct((TOKENS, BLOCK), f32), out_rows(UNITS), pltpu.HBM((TOKENS, D), bf16)],
        compiler_params=pltpu.CompilerParams(vmem_limit_bytes=14 * MIB),
        cost_estimate=pl.CostEstimate(
            flops=2 * TOKENS * D * (UNITS + BLOCK), bytes_accessed=12 * MIB, transcendentals=0
        ),
        name="pull_back",
    )(order, *pieces, weight, slope, *ties)


def blocks_product_kernel(count, flipped, order_ref, *refs):
    w_ref, out_ref = (refs[count * SIDE], refs[-1])
    columns = [
        jnp.concatenate([refs[part * SIDE + block][...] for block in range(SIDE)], axis=0)
        for part in range(count)
    ]
    left = jnp.concatenate(columns, axis=1)
    out_ref[...] = dot(left, w_ref[...], LAST if flipped else None).astype(out_ref.dtype)


def blocks_product(parts, weight, order, flipped, dtype, ties=()):
    def block(width, which):
        return pl.BlockSpec((BLOCK, width), lambda i, order: (order[i * SIDE + which], 0))

    groups = order.shape[0] // SIDE
    depth = sum(part.shape[1] for part in parts)
    return pl.pallas_call(
        functools.partial(blocks_product_kernel, len(parts), flipped),
        grid_spec=pltpu.PrefetchScalarGridSpec(
            num_scalar_prefetch=1,
            grid=(groups,),
            in_specs=[block(part.shape[1], which) for part in parts for which in range(SIDE)]
            + [whole_of(*weight.shape)]
            + unused(ties),
            out_specs=pl.BlockSpec((SIDE * BLOCK, D), lambda i, order: (i, 0)),
        ),
        out_shape=jax.ShapeDtypeStruct((groups * SIDE * BLOCK, D), dtype),
        compiler_params=pltpu.CompilerParams(vmem_limit_bytes=10 * MIB),
        cost_estimate=pl.CostEstimate(
            flops=2 * groups * SIDE * BLOCK * depth * D, bytes_accessed=2 * MIB + groups * MIB, transcendentals=0
        ),
        name="blocks_product",
    )(order, *[part for part in parts for _ in range(SIDE)], weight, *ties)


def key_places(tile, core):
    row = lax.broadcasted_iota(jnp.int32, (WINDOW, 1), 0)
    return tile * (2 * WINDOW) + (row // BLOCK) * (2 * BLOCK) + core * BLOCK + row % BLOCK


def query_places(tile, core):
    row = lax.broadcasted_iota(jnp.int32, (1, WINDOW), 1)
    return tile * (2 * WINDOW) + (row // BLOCK) * (2 * BLOCK) + core * BLOCK + row % BLOCK


def turned(rows):
    return jnp.transpose(rows.astype(f32)).astype(bf16)


def attend_kernel(
    info_ref, q_ref, start_ref, own_ref, other_ref, o_ref, wide_ref, top_ref, over_ref, vt_ref
):
    tile = pl.program_id(0)
    core = info_ref[2 * (TOKENS // WINDOW)]

    @pl.when(tile == 0)
    def _():
        for part in range(TOKENS // BLOCK):
            rows = pl.ds(part * BLOCK, BLOCK)
            for which, ref in enumerate((own_ref, other_ref)):
                pair = turned(ref[rows, :])
                vt_ref[which, :, rows] = jnp.concatenate([pair[HD:], jnp.ones((16, BLOCK), bf16)], axis=0)

    query = q_ref[...]
    starts = start_ref[...]
    places = query_places(tile, core)

    def step(index, carry, masked):
        top, mixed = carry
        rows = pl.ds(pl.multiple_of(index * WINDOW, WINDOW), WINDOW)
        scores = [dot(ref[rows, :], query, LAST) * LOG2E for ref in (own_ref, other_ref)]
        if masked:
            allowed = []
            for which in range(2):
                keys = key_places(index, core if which == 0 else 1 - core)
                allowed.append((keys >= starts) & (keys <= places))
            scores = [jnp.where(a, s, -1e30) for a, s in zip(allowed, scores)]
        highest = jnp.max(jnp.maximum(scores[0], scores[1]), axis=0, keepdims=True)
        raised = jnp.maximum(top, jnp.ceil(highest))
        parts = [jnp.exp2(s - raised) for s in scores]
        if masked:
            parts = [jnp.where(a, p, 0.0) for a, p in zip(allowed, parts)]
        mixed = mixed * jnp.exp2(top - raised)
        for which in range(2):
            mixed = mixed + dot(vt_ref[which, :, rows], parts[which].astype(bf16))
        return (raised, mixed)

    carry = (jnp.full((1, WINDOW), -1e30, f32), jnp.zeros((HD + 16, WINDOW), f32))
    low, clear = (info_ref[tile], info_ref[TOKENS // WINDOW + tile])
    carry = lax.fori_loop(low, clear, functools.partial(step, masked=True), carry)
    carry = lax.fori_loop(clear, tile, functools.partial(step, masked=False), carry)
    top, mixed = step(tile, carry, True)
    over = 1.0 / mixed[HD : HD + 1]
    top_ref[...] = top
    over_ref[...] = over
    spare = (lax.broadcasted_iota(jnp.int32, (HD, WINDOW), 0) == 0).astype(f32)
    mixed = jnp.concatenate([spare, mixed[:HD] * over], axis=0)
    mixed = jnp.transpose(mixed)
    wide_ref[...] = mixed
    o_ref[...] = mixed.astype(bf16)


def attend(info, query, starts, own, other):
    rows = lambda width: pl.BlockSpec((WINDOW, width), lambda i, info: (i, 0))
    line = pl.BlockSpec((1, WINDOW), lambda i, info: (0, i))
    whole = pl.BlockSpec((TOKENS, BLOCK), lambda i, info: (0, 0))
    return pl.pallas_call(
        attend_kernel,
        grid_spec=pltpu.PrefetchScalarGridSpec(
            num_scalar_prefetch=1,
            grid=(TOKENS // WINDOW,),
            in_specs=[rows(BLOCK), line, whole, whole],
            out_specs=[rows(BLOCK), rows(BLOCK), line, line],
            scratch_shapes=[pltpu.VMEM((2, HD + 16, TOKENS), bf16)],
        ),
        out_shape=[
            jax.ShapeDtypeStruct((TOKENS, BLOCK), bf16),
            jax.ShapeDtypeStruct((TOKENS, BLOCK), f32),
            jax.ShapeDtypeStruct((1, TOKENS), f32),
            jax.ShapeDtypeStruct((1, TOKENS), f32),
        ],
        compiler_params=pltpu.CompilerParams(vmem_limit_bytes=32 * MIB),
        cost_estimate=pl.CostEstimate(
            flops=8 * TOKENS * TOKENS * BLOCK, bytes_accessed=4 * MIB, transcendentals=2 * TOKENS * TOKENS
        ),
        name="attend",
    )(info, query, starts, own, other)


def attend_back_kernel(
    info_ref, q_ref, do_ref, o_ref, top_ref, over_ref, start_ref, c_ref, s_ref, own_ref, other_ref, *refs
):
    dq_ref, down_ref, dother_low_ref, kt_ref, dother_ref = refs[-5:]
    tile = pl.program_id(0)
    core = info_ref[2 * (TOKENS // WINDOW)]

    @pl.when(tile == 0)
    def _():
        for part in range(TOKENS // BLOCK):
            rows = pl.ds(part * BLOCK, BLOCK)
            kt_ref[0, :, rows] = turned(own_ref[rows, :])[:HD]
            kt_ref[1, :, rows] = turned(other_ref[rows, :])[:HD]
        down_ref[...] = jnp.zeros_like(down_ref)
        dother_ref[...] = jnp.zeros_like(dother_ref)

    query = q_ref[...]
    top = top_ref[...]
    starts = start_ref[...]
    places = query_places(tile, core)
    turned_grad = (jnp.transpose(do_ref[...]) * over_ref[...]).astype(bf16).astype(f32)
    inner = jnp.sum(turned_grad * jnp.transpose(o_ref[...]), axis=0, keepdims=True)
    grad = jnp.transpose(turned_grad).astype(bf16)

    def step(index, carry, masked):
        rows = pl.ds(pl.multiple_of(index * WINDOW, WINDOW), WINDOW)
        for which, (ref, dref) in enumerate(((own_ref, down_ref), (other_ref, dother_ref))):
            pair = ref[rows, :]
            parts = jnp.exp2(dot(pair, query, LAST) * LOG2E - top)
            if masked:
                keys = key_places(index, core if which == 0 else 1 - core)
                allowed = (keys >= starts) & (keys <= places)
                parts = jnp.where(allowed, parts, 0.0)
            parts = parts.astype(bf16)
            changes = (parts.astype(f32) * (dot(pair, grad, LAST) - inner)).astype(bf16)
            dref[rows, :] += dot(changes, query) + dot(parts, grad)
            carry = carry + dot(kt_ref[which, :, rows], changes)
        return carry

    low, clear = (info_ref[tile], info_ref[TOKENS // WINDOW + tile])
    carry = jnp.zeros((HD, WINDOW), f32)
    carry = lax.fori_loop(low, clear, functools.partial(step, masked=True), carry)
    carry = lax.fori_loop(clear, tile, functools.partial(step, masked=False), carry)
    carry = step(tile, carry, True) * SCALE
    change = jnp.transpose(jnp.concatenate([carry, jnp.zeros((HD, WINDOW), f32)], axis=0))
    dq_ref[...] = (change * c_ref[...] - half_turn(change) * s_ref[...]).astype(bf16)

    @pl.when(tile == TOKENS // WINDOW - 1)
    def _():
        dother_low_ref[...] = dother_ref[...].astype(bf16)


def attend_back(info, query, grad, mixed, top, over, starts, cosine, sine, own, other, ties=()):
    rows = pl.BlockSpec((WINDOW, BLOCK), lambda i, info: (i, 0))
    line = pl.BlockSpec((1, WINDOW), lambda i, info: (0, i))
    whole = pl.BlockSpec((TOKENS, BLOCK), lambda i, info: (0, 0))
    return pl.pallas_call(
        attend_back_kernel,
        grid_spec=pltpu.PrefetchScalarGridSpec(
            num_scalar_prefetch=1,
            grid=(TOKENS // WINDOW,),
            in_specs=[rows, rows, rows, line, line, line, rows, rows, whole, whole] + unused(ties),
            out_specs=[rows, whole, whole],
            scratch_shapes=[pltpu.VMEM((2, HD, TOKENS), bf16), pltpu.VMEM((TOKENS, BLOCK), f32)],
        ),
        out_shape=[
            jax.ShapeDtypeStruct((TOKENS, BLOCK), bf16),
            jax.ShapeDtypeStruct((TOKENS, BLOCK), f32),
            jax.ShapeDtypeStruct((TOKENS, BLOCK), bf16),
        ],
        compiler_params=pltpu.CompilerParams(vmem_limit_bytes=40 * MIB),
        cost_estimate=pl.CostEstimate(
            flops=20 * TOKENS * TOKENS * BLOCK, bytes_accessed=6 * MIB, transcendentals=2 * TOKENS * TOKENS
        ),
        name="attend_back",
    )(info, query, grad, mixed, top, over, starts, cosine, sine, own, other, *ties)


def join_kernel(mine_ref, theirs_ref, c_ref, s_ref, out_ref):
    pair = mine_ref[...] + theirs_ref[...].astype(f32)
    out_ref[...] = (pair * c_ref[...] - half_turn(pair) * s_ref[...]).astype(bf16)


def join_pairs(mine, theirs, cosine, sine):
    rows = pl.BlockSpec((2 * TILE, BLOCK), lambda i: (i, 0))
    return pl.pallas_call(
        join_kernel,
        grid=(TOKENS // (2 * TILE),),
        in_specs=[rows] * 4,
        out_specs=rows,
        out_shape=jax.ShapeDtypeStruct((TOKENS, BLOCK), bf16),
        name="join_pairs",
    )(mine, theirs, cosine, sine)


def pack_kernel(info_ref, up_ref, sum_ref, grads_ref, keep_ref, send_ref):
    core = info_ref[2 * (TOKENS // WINDOW)]
    lane = lax.broadcasted_iota(jnp.int32, (1, BLOCK), 1)
    row = lax.broadcasted_iota(jnp.int32, (16, UNITS), 0)
    for out_ref, which in ((keep_ref, core), (send_ref, 1 - core)):
        for chip in range(CHIPS):
            at = chip * EARLY
            rows = pl.ds(pl.multiple_of(chip * 64 + which * 32, 32), 32)
            out_ref[at : at + 32, :] = up_ref[rows, :].astype(out_ref.dtype)
            sums = grads_ref[UNITS : UNITS + 8, pl.ds(chip // 2 * BLOCK, BLOCK)][:1]
            here = chip % 2 * 64
            first = pltpu.roll(sums, (BLOCK - here) % BLOCK, 1) if here else sums
            mine = jnp.where(which == 0, first, pltpu.roll(sums, BLOCK - here - 32, 1))
            mine = jnp.concatenate([jnp.where(lane < 32, mine, 0.0), jnp.zeros((1, BLOCK), f32)], axis=1)
            extra = jnp.where(row == 0, sum_ref[...], jnp.where(row == 1, mine, 0.0))
            out_ref[at + 32 : at + EARLY, :] = extra.astype(out_ref.dtype)
        heads = pl.ds(pl.multiple_of(UNITS + HD + which * 32, 32), 32)
        units = pl.ds(pl.multiple_of(which * BLOCK, BLOCK), BLOCK)
        for part in range(D // UNITS):
            at = CHIPS * EARLY + part * 160
            columns = pl.ds(part * UNITS, UNITS)
            out_ref[at : at + 32, :] = grads_ref[heads, columns].astype(out_ref.dtype)
            out_ref[at + 32 : at + 160, :] = grads_ref[units, columns].astype(out_ref.dtype)


def pack(info, up_grads, up_sum, grads):
    rows = CHIPS * EARLY + 160 * (D // UNITS)
    return pl.pallas_call(
        pack_kernel,
        grid_spec=pltpu.PrefetchScalarGridSpec(
            num_scalar_prefetch=1,
            grid=(1,),
            in_specs=[whole_of(D, UNITS), whole_of(1, UNITS), whole_of(UNITS + BLOCK, D)],
            out_specs=[whole_of(rows, UNITS), whole_of(rows, UNITS)],
        ),
        out_shape=[
            jax.ShapeDtypeStruct((rows, UNITS), f32),
            jax.ShapeDtypeStruct((rows, UNITS), bf16),
        ],
        compiler_params=pltpu.CompilerParams(vmem_limit_bytes=16 * MIB),
        cost_estimate=pl.CostEstimate(flops=4 * MIB, bytes_accessed=5 * MIB, transcendentals=0),
        name="pack",
    )(info, up_grads, up_sum, grads)


def finish_kernel(got_ref, qkv_ref, up_ref, norm_ref, qkv_out, up_out, qkv_sum_ref, up_sum_ref, norm_out):
    gain1, shift1, gain2, shift2 = (norm_ref[:, k : k + 1] for k in range(4))
    first = lax.broadcasted_iota(jnp.int32, (32, BLOCK), 1) < HD
    total = [jnp.zeros((32, 1), f32) for _ in range(4)]
    across = lambda values: jnp.sum(values, axis=1, keepdims=True)
    for chip in range(0, CHIPS, 2):
        tiles = [got_ref[chip + k, EARLY:, :].astype(f32) for k in range(2)]
        (low0, high0), (low1, high1) = ((t[:, :BLOCK], t[:, BLOCK:]) for t in tiles)
        turn = lambda values: pltpu.roll(values, HD, 1)
        cores = (
            jnp.where(first, low0, turn(low1)),
            jnp.where(first, high0, turn(high1)),
            jnp.where(first, turn(high0), high1),
        )
        notes = jnp.where(first, turn(low0), low1)
        for part, (core, row) in enumerate(zip(cores, (0, 2, 3))):
            at = pl.ds(part * D + chip * HD, BLOCK)
            sums = notes[row : row + 1]
            weight = qkv_ref[:, at].astype(f32)
            qkv_out[:, at] = gain1 * core + shift1 * sums
            qkv_sum_ref[:, at] = sums
            total[0] += across(weight * core)
            total[1] += across(weight * sums)
    for chip in range(CHIPS):
        at = pl.ds(chip * UNITS, UNITS)
        core = got_ref[chip, :32, :].astype(f32)
        sums = got_ref[chip, 32:EARLY, :].astype(f32)[:1]
        weight = up_ref[:, at].astype(f32)
        up_out[:, at] = gain2 * core + shift2 * sums
        up_sum_ref[:, at] = sums
        total[2] += across(weight * core)
        total[3] += across(weight * sums)
    lane = lax.broadcasted_iota(jnp.int32, (32, BLOCK), 1)
    out = jnp.zeros((32, BLOCK), f32)
    for k in range(4):
        out = jnp.where(lane == k, total[k], out)
    norm_out[...] = out


def finish(got, qkv_weight, up_weight, norms):
    shape = lambda *dims: jax.ShapeDtypeStruct(dims, f32)
    return pl.pallas_call(
        finish_kernel,
        out_shape=[shape(32, 3 * D), shape(32, FF), shape(1, 3 * D), shape(1, FF), shape(32, BLOCK)],
        compiler_params=pltpu.CompilerParams(vmem_limit_bytes=10 * MIB),
        cost_estimate=pl.CostEstimate(flops=8 * 32 * 7 * D, bytes_accessed=3 * MIB, transcendentals=0),
        name="finish",
    )(got, qkv_weight, up_weight, norms)


def on_device(
    inputs,
    segments,
    cotangent,
    qkv_weight,
    qkv_bias,
    dense_weight,
    dense_bias,
    fc_in_weight,
    fc_in_bias,
    fc_out_weight,
    fc_out_bias,
    norm1_gain,
    norm1_bias,
    norm2_gain,
    norm2_bias,
):
    section = lax.axis_index("section")
    place = lax.axis_index("shard")
    chip, core = (place // 2, place % 2)
    first_layer = section == 0
    x0 = lax.dynamic_index_in_dim(inputs, section, 0, keepdims=False)[0]
    out_grad = lax.dynamic_index_in_dim(cotangent, section, 0, keepdims=False)[0]
    my_segs = lax.dynamic_index_in_dim(segments, section, 0, keepdims=False)[0]

    x0_all = plane_gather(x0)
    grad1_all = plane_gather(out_grad)

    pieces = lambda vector: vector.astype(bf16).reshape(-1, 32)
    vectors = jnp.concatenate(
        [
            pieces(v[0])
            for v in (
                norm1_gain, norm1_bias, norm2_gain, norm2_bias, qkv_bias, fc_in_bias, dense_bias, fc_out_bias,
            )
        ]
    )
    vectors_away = section_swap(vectors)
    spare = jnp.concatenate([pieces(my_segs), vectors, vectors_away, jnp.zeros((2, 32), bf16)])
    spare = jnp.concatenate([spare[:16], spare[16:]], axis=1).reshape(1, 1, 16, HD)
    heads = qkv_weight[0].reshape(2, 16, 3, CHIPS, HD).transpose(3, 0, 1, 2, 4)
    units = fc_in_weight[0].reshape(2, 16, CHIPS, UNITS).transpose(2, 0, 1, 3)
    cut = jnp.concatenate(
        [
            heads[..., 0, :],
            jnp.broadcast_to(spare, (CHIPS, 2, 16, HD)),
            heads[..., 1, :],
            heads[..., 2, :],
            units,
        ],
        axis=-1,
    ).reshape(2 * CHIPS, 16, WIDE)
    got = lax.all_to_all(cut, "shard", 0, 0, tiled=True)
    notes = got[:, :, HD:BLOCK]
    notes = jnp.concatenate([notes[..., :32], notes[..., 32:]], axis=1)
    rows_own = jnp.concatenate([dense_weight[0], fc_out_weight[0]], axis=0)
    rows_away = section_swap(rows_own)
    got_away = section_swap(got)
    got_pair = jnp.stack([got, got_away])
    rows_pair = jnp.stack([rows_own, rows_away])
    got_other = core_swap(got_pair)
    rows_other = core_swap(rows_pair)

    def by_core(mine, theirs, axis):
        return jnp.where(
            core == 0, jnp.stack([mine, theirs], axis), jnp.stack([theirs, mine], axis)
        )

    columns_both = by_core(got_pair, got_other, 2).reshape(2, D, WIDE)
    head_rows = by_core(rows_pair[:, :32], rows_other[:, :32], 1).reshape(2, HD, D)
    unit_rows = by_core(rows_pair[:, 32:], rows_other[:, 32:], 1).reshape(2, UNITS, D)
    out_both = jnp.concatenate([unit_rows, jnp.zeros((2, HD, D), bf16), head_rows], axis=1)
    notes_both = (notes[:, 4:17], notes[:, 17:30])

    def layer_weights(layer):
        mine = first_layer == (layer == 0)
        pick = lambda both: jnp.where(mine, both[0], both[1])
        columns, note = (pick(columns_both).astype(f32), pick(notes_both))
        vector = lambda at, count: note[:, at : at + count].reshape(-1).astype(f32)
        gain1, shift1, gain2, shift2 = (vector(k, 1) for k in range(4))
        attn_bias = vector(4, 3).reshape(3, CHIPS, HD)
        attn_bias = lax.dynamic_index_in_dim(attn_bias, chip, 1, keepdims=False)
        up_bias = lax.dynamic_slice_in_dim(vector(7, 4), chip * UNITS, UNITS, 0)
        out_bias = vector(11, 1) + vector(12, 1)
        lane = jnp.arange(WIDE)
        gains = jnp.where(lane[None, :] < 2 * BLOCK, gain1[:, None], gain2[:, None])
        used = (lane < HD) | (lane >= BLOCK)
        bias = jnp.concatenate(
            [attn_bias[0], jnp.zeros((HD,), f32), attn_bias[1], attn_bias[2], up_bias]
        )
        shift = bias[None, :]
        plain = jnp.where(used[None, :], columns, 0.0).astype(bf16)
        scaled = jnp.where(used[None, :], columns * gains, 0.0).astype(bf16)
        lines = jnp.stack([gain1, shift1, gain2, shift2])
        return (plain, scaled, shift, lines, pick(out_both), out_bias)

    segs = notes[:, :4].astype(jnp.int32)
    numbers = jnp.arange(DOCS, dtype=jnp.int32)
    before = jnp.sum((segs.reshape(1, -1) < numbers[:, None]).astype(jnp.int32), axis=1)
    steps = before - jnp.concatenate([jnp.zeros((1,), jnp.int32), before[:-1]])
    my_rows = lax.dynamic_index_in_dim(
        segs.reshape(CHIPS, 2, BLOCK), core, 1, keepdims=False
    ).reshape(TOKENS)
    starts = jnp.sum(jnp.where(my_rows[None, :] >= numbers[:, None], steps[:, None], 0), axis=0)
    token = jnp.arange(TOKENS, dtype=jnp.int32)
    token = (token // BLOCK) * (2 * BLOCK) + core * BLOCK + token % BLOCK
    half_rot = ROT // 2
    frequency = jnp.exp(jnp.arange(half_rot, dtype=f32) * (-2.0 * math.log(10000.0) / ROT))
    angles = frequency[:, None] * (token - starts).astype(f32)[None, :]
    cos_rows, sin_rows = (jnp.cos(angles), jnp.sin(angles))
    ones = lambda count: jnp.ones((count, TOKENS), f32)
    zeros = lambda count: jnp.zeros((count, TOKENS), f32)
    cosine = jnp.concatenate([cos_rows, cos_rows, ones(BLOCK - ROT)], axis=0).T
    sine = jnp.concatenate([-sin_rows, sin_rows, zeros(BLOCK - ROT)], axis=0).T
    tiles = starts.reshape(TOKENS // WINDOW, WINDOW)
    low_tile = tiles[:, 0] // (2 * WINDOW)
    clear_tile = jnp.minimum(
        (tiles[:, -1] + 2 * WINDOW - 1) // (2 * WINDOW),
        jnp.arange(TOKENS // WINDOW, dtype=jnp.int32),
    )
    info = jnp.concatenate([low_tile, clear_tile, core[None], jnp.zeros((7,), jnp.int32)])
    start_line = starts[None, :]

    order = block_order(chip, core)
    straight = jnp.arange(CHIPS, dtype=jnp.int32)

    def forward(pieces, arranged, weights):
        plain, _, shift, lines, _, _ = weights
        normed, query, own, act, slope = project(
            arranged, pieces, plain, shift, lines, cosine, sine
        )
        other = core_swap(own)
        mixed, wide, top, over = attend(info, query, start_line, own, other)
        return (normed, query, own, other, act, slope, mixed, wide, top, over)

    def pulled(pieces, arranged, weights, kept, ties=()):
        return pull_back(arranged, pieces, weights[4], kept[5], ties)

    def by_owner(parts):
        return parts.reshape(CHIPS, 2, 32, parts.shape[-1])

    def early_grads(kept, changed, grad_all):
        up_grads = dot(kept[0], changed, FIRST)
        grads = dot(jnp.concatenate([kept[4], kept[6]], axis=1), grad_all, FIRST)
        up_sum = jnp.sum(changed.astype(f32), axis=0, keepdims=True)
        keep, send = pack(info, up_grads, up_sum, grads)
        return add(keep, core_swap(send)).astype(bf16)

    def over_cores(parts):
        keep, send = (
            jnp.concatenate(
                [lax.dynamic_index_in_dim(part, which, 0, keepdims=False) for part in parts]
            )
            for which in (core, 1 - core)
        )
        send = send.astype(bf16)
        return (add(keep, core_swap(send)), send)

    def attended(grad_mixed, kept, ties=()):
        _, query, own, other, _, _, _, wide, top, over = kept
        dq, d_own, d_other = attend_back(
            info, query, grad_mixed, wide, top, over, start_line, cosine, sine, own, other, ties
        )
        return (dq, join_pairs(d_own, core_swap(d_other), cosine, sine))

    def late_grads(normed, dq, d_pair):
        made = jnp.concatenate([dq, d_pair], axis=1)
        grads = by_owner(dot(normed, made, FIRST))
        sums = jnp.sum(made.astype(f32), axis=0).reshape(1, 1, 4, HD)
        extra = jnp.pad(jnp.broadcast_to(sums, (CHIPS, 2, 4, HD)), ((0, 0), (0, 0), (0, 28), (0, 0)))
        grads = jnp.concatenate([grads[..., :HD], extra, grads[..., BLOCK:]], axis=-1)
        return grads.transpose(1, 0, 2, 3).reshape(2, CHIPS * 32, 2 * BLOCK)

    def norm_back(rows, grad, summed):
        here, inverse = norm_rows(rows)
        inner_part = (
            summed
            - jnp.mean(summed, axis=-1, keepdims=True)
            - here * jnp.mean(summed * here, axis=-1, keepdims=True)
        )
        return (grad.astype(f32) + inverse * inner_part).astype(bf16)

    weights0, weights1 = (layer_weights(0), layer_weights(1))
    kept0 = forward((x0_all,), straight, weights0)
    ready = (weights0[1], weights1[0], weights1[1], weights1[2])
    summed, _, _ = scatter_rows((kept0[4], kept0[6]), weights0[4], order, False, (), ready)
    x1 = (add(x0, summed) + weights0[5][None, :]).astype(bf16)
    x1, grad1_all = lax.optimization_barrier((x1, grad1_all))
    kept1 = forward(gather_rows(x1), order, weights1)
    grad_mixed, changed1, grad1_all = pulled((grad1_all,), straight, weights1, kept1)
    dq1, d_pair1 = attended(grad_mixed, kept1)
    inner = jnp.concatenate([kept1[4], after(kept1[6], d_pair1)], axis=1)
    summed = plane_scatter(dot(inner, weights1[4]).astype(bf16))
    x2 = (add(x1, summed) + weights1[5][None, :]).astype(bf16)
    summed, _, _ = scatter_rows((dq1, d_pair1, changed1), weights1[1], order, True)
    grad1 = norm_back(x1, out_grad, summed)
    early1 = early_grads(kept1, changed1, after(grad1_all, d_pair1))
    late1, _ = over_cores([late_grads(kept1[0], dq1, d_pair1)])
    layer1 = jnp.concatenate([late1.astype(bf16), early1])
    half1 = add(layer1, section_swap(layer1)).astype(bf16)
    layer1 = add(half1, cross(half1, 1)).astype(bf16)

    grad_mixed, changed0, grad0_all = pulled(
        gather_rows(grad1), order, weights0, kept0, (half1,)
    )
    early0 = early_grads(kept0, changed0, grad0_all)
    dq0, d_pair0 = attended(grad_mixed, kept0, (x2, layer1))
    late0, send = over_cores([late_grads(kept0[0], dq0, d_pair0)])
    summed, held, step = scatter_rows(
        (dq0, d_pair0, changed0), weights0[1], order, True, (send,)
    )
    half0 = add(after(early0, held), section_swap(early0)).astype(bf16)
    early0 = add(after(half0, step), cross(half0, 0)).astype(bf16)
    grad0 = norm_back(x0, grad1, summed)

    def placed(layer0, layer1):
        mine = jnp.where(first_layer, layer0, layer1)
        theirs = section_swap(jnp.where(first_layer, layer1, layer0))
        return jnp.where(
            first_layer, jnp.stack([mine, theirs]), jnp.stack([theirs, mine])
        )[None, :, None]

    section_outputs = placed(x1, x2)
    input_grads = placed(grad0, grad1)

    late0 = late0.astype(bf16)
    half0 = add(late0, section_swap(late0)).astype(bf16)
    late0 = add(half0, cross(half0, 0))
    late0 = after(late0, step).astype(bf16)
    parts = jnp.where(first_layer, jnp.concatenate([late0, early0]), layer1)
    late, early, rows = jnp.split(parts, [CHIPS * 32, CHIPS * (32 + EARLY)])
    row_sum = jnp.concatenate(jnp.split(rows, D // UNITS), axis=1).astype(f32)
    parts = jnp.concatenate([part.reshape(CHIPS, -1, UNITS) for part in (early, late)], axis=1)
    got = lax.all_to_all(parts, "shard", 0, 0, tiled=True, axis_index_groups=SAME_CORE)
    column = lambda vector: vector[0].astype(f32)[:, None]
    norms = jnp.concatenate([column(v) for v in (norm1_gain, norm1_bias, norm2_gain, norm2_bias)], axis=1)
    qkv_grad, up_grad, qkv_sum, up_sum, norm_grads = finish(got, qkv_weight[0], fc_in_weight[0], norms)
    shift_grad = got[0, 33, :32].astype(f32)
    mine_of = lambda vector, at, width: lax.dynamic_slice_in_dim(
        vector, at + place * width, width, 1
    )
    return (
        section_outputs,
        input_grads,
        qkv_grad[None],
        mine_of(qkv_sum[:, : 2 * D], 0, 64),
        mine_of(qkv_sum[:, 2 * D :], 0, 32),
        row_sum[None, :32],
        shift_grad[None],
        up_grad[None],
        mine_of(up_sum, 0, 128),
        row_sum[None, 32:],
        shift_grad[None],
        *(norm_grads[:, k][None] for k in range(4)),
    )


def solution(mesh):
    rows = P(None, "rep", "shard", None)
    outs = P("section", None, "rep", "shard", None)
    matrix = P("section", "shard", None)
    vector = P("section", "shard")
    return jax.shard_map(
        on_device,
        mesh=mesh,
        in_specs=(
            rows, P(None, "rep", "shard"), rows, matrix, vector, matrix, vector, matrix, vector, matrix,
            vector, vector, vector, vector, vector,
        ),
        out_specs=(
            outs, outs, matrix, vector, vector, matrix, vector, matrix, vector, matrix, vector, vector,
            vector, vector, vector,
        ),
        check_vma=False,
    )
```

```python
import functools
import math

import jax
import jax.numpy as jnp
from jax import lax
from jax.experimental import pallas as pl
from jax.experimental.pallas import tpu as pltpu
from jax.sharding import PartitionSpec as P

D = 1024
HEADS = 16
HD = 64
FF = 4096
ROT = 16
epsilon = 1e-05

CHIPS = 16
UNITS = FF // CHIPS
WIDE = 512
TOKENS = 2048
TILE = 256
WINDOW = 512
EARLY = 48
BLOCK = 128
SIDE = 4
OFFSETS = (0, 1, -1, 2)
DOCS = 24
LOG2E = math.log2(math.e)
SCALE = 1.0 / math.sqrt(HD)
MIB = 1024 * 1024

f32 = jnp.float32
bf16 = jnp.bfloat16

SAME_CORE = [[2 * chip + core for chip in range(CHIPS)] for core in range(2)]
LAST = (((1,), (1,)), ((), ()))
FIRST = (((0,), (0,)), ((), ()))


def core_swap(value):
    return lax.ppermute(value, "shard", [(i, i ^ 1) for i in range(2 * CHIPS)])


def section_swap(value):
    return lax.ppermute(value, "section", [(0, 1), (1, 0)])


def cross(value, section):
    pairs = [(2 * (1 - section) + rep, 2 * section + 1 - rep) for rep in range(2)]
    return lax.ppermute(value, ("section", "rep"), pairs)


def plane_gather(rows):
    return lax.all_gather(rows, "shard", axis=0, tiled=True, axis_index_groups=SAME_CORE)


def plane_scatter(partial):
    return lax.psum_scatter(
        partial, "shard", scatter_dimension=0, tiled=True, axis_index_groups=SAME_CORE
    )


def hop(value, second, step):
    pairs = []
    for y in range(SIDE):
        for x in range(SIDE):
            for core in range(2):
                along_x = (core == 0) != second
                to_y, to_x = ((y, (x + step) % SIDE) if along_x else ((y + step) % SIDE, x))
                pairs.append(((y * SIDE + x) * 2 + core, (to_y * SIDE + to_x) * 2 + core))
    return lax.ppermute(value, "shard", pairs)


def row_gather(own):
    return (own, hop(own, False, -1), hop(own, False, 1), hop(own, False, 2))


def ring_gather(own):
    half = own.shape[0] // 2
    after = hop(own, True, -1)
    prior = hop(own, True, 1)
    far_first = hop(prior[:half], True, 1)
    far_last = hop(after[half:], True, -1)
    return (own, after, prior, far_first, far_last)


def block_order(chip, core):
    y, x = (chip // SIDE, chip % SIDE)
    order = []
    for second in OFFSETS:
        for first in OFFSETS:
            step_y, step_x = (jnp.where(core == 0, second, first), jnp.where(core == 0, first, second))
            order.append(((y + step_y) % SIDE) * SIDE + (x + step_x) % SIDE)
    return jnp.stack(order).astype(jnp.int32)


def gather_rows(own):
    return ring_gather(jnp.concatenate(row_gather(own), axis=0))


def add(*terms):
    return sum(term.astype(f32) for term in terms)


def after(value, *others):
    zero = sum(jnp.minimum(jnp.abs(lax.slice(o, (0,) * o.ndim, (1,) * o.ndim).reshape(())), 0) for o in others)
    return value + zero.astype(value.dtype)


def scatter_rows(parts, weight, order, flipped, first=(), ready=()):
    quarter = SIDE * BLOCK
    half = quarter // 2
    far = blocks_product(parts, weight, order[3 * SIDE :], flipped, bf16, first)
    far_first = hop(far[:half], True, 1)
    far_last = hop(far[half:], True, -1)
    near = blocks_product(parts, weight, order[SIDE : 3 * SIDE], flipped, bf16)
    ahead = jnp.concatenate([add(near[:half], far_first).astype(bf16), near[half:quarter]])
    back = jnp.concatenate(
        [near[quarter : quarter + half], add(near[quarter + half :], far_last).astype(bf16)]
    )
    ahead_first = ahead
    from_back = hop(ahead, True, 1)
    from_ahead = hop(back, True, -1)
    home = blocks_product(parts, weight, order[:SIDE], flipped, f32, ready)
    rows = lambda at, count: add(*(v[at : at + count] for v in (home, from_back, from_ahead)))
    ahead, back, far = (rows(k * BLOCK, BLOCK).astype(bf16) for k in (1, 2, 3))
    summed = add(rows(0, BLOCK), hop(far, False, 2), hop(ahead, False, 1), hop(back, False, -1))
    return (summed, ahead_first, far)


def dot(left, right, dims=None):
    if dims is None:
        return jnp.dot(left, right, preferred_element_type=f32)
    return lax.dot_general(left, right, dims, preferred_element_type=f32)


def norm_rows(rows):
    values = rows.astype(f32)
    centred = values - jnp.mean(values, axis=-1, keepdims=True)
    inverse = lax.rsqrt(jnp.mean(centred * centred, axis=-1, keepdims=True) + epsilon)
    return (centred * inverse, inverse)


def half_turn(rows):
    lane = lax.broadcasted_iota(jnp.int32, rows.shape, 1) % HD
    ahead = pltpu.roll(rows, BLOCK - ROT // 2, 1)
    behind = pltpu.roll(rows, ROT // 2, 1)
    return jnp.where(lane < ROT // 2, ahead, behind)


def fetch_blocks(order_ref, pieces, rows_ref, sems):
    copies = []
    for piece in pieces:
        for block in range(piece.shape[0] // BLOCK):
            slot = len(copies)
            place = pl.multiple_of(order_ref[slot] * BLOCK, BLOCK)
            copy = pltpu.make_async_copy(
                piece.at[pl.ds(block * BLOCK, BLOCK)], rows_ref.at[pl.ds(place, BLOCK)], sems.at[slot]
            )
            copy.start()
            copies.append(copy)
    for copy in copies:
        copy.wait()


def project_kernel(count, order_ref, *refs):
    pieces, refs = (refs[:count], refs[count:])
    w_ref, b_ref, g_ref, c_ref, s_ref, n_ref, q_ref, kv_ref, act_ref, slope_ref, rows_ref, sems = refs

    @pl.when(pl.program_id(0) == 0)
    def _():
        fetch_blocks(order_ref, pieces, rows_ref, sems)

    here = pl.ds(pl.multiple_of(pl.program_id(0) * TILE, TILE), TILE)
    normed, _ = norm_rows(rows_ref[here, :])
    n_ref[...] = normed.astype(bf16)
    first = (normed * g_ref[0:1] + g_ref[1:2]).astype(bf16)
    second = (normed * g_ref[2:3] + g_ref[3:4]).astype(bf16)
    made = dot(first, w_ref[:, : 2 * BLOCK]) + b_ref[:, : 2 * BLOCK]
    cosine, sine = (c_ref[...], s_ref[...])
    query = made[:, :BLOCK]
    query = query * cosine + half_turn(query) * sine
    q_ref[...] = (query * SCALE).astype(bf16)
    pair = made[:, BLOCK:]
    pair = pair * cosine + half_turn(pair) * sine
    kv_ref[...] = pair.astype(bf16)
    up = dot(second, w_ref[:, 2 * BLOCK :]) + b_ref[:, 2 * BLOCK :]
    normal_cdf = 0.5 * (1.0 + lax.erf(up * (1.0 / math.sqrt(2.0))))
    act_ref[...] = (up * normal_cdf).astype(bf16)
    bell = jnp.exp(-0.5 * up * up) * (1.0 / math.sqrt(2.0 * math.pi))
    slope_ref[...] = (normal_cdf + up * bell).astype(bf16)


def tile_rows(width):
    return pl.BlockSpec((TILE, width), lambda i, order: (i, 0))


def whole_of(height, width):
    return pl.BlockSpec((height, width), lambda i, order: (0, 0))


def out_rows(width):
    return jax.ShapeDtypeStruct((TOKENS, width), bf16)


def unused(ties):
    return [pl.BlockSpec(memory_space=pl.ANY)] * len(ties)


def project(order, pieces, weight, shift, gains, cosine, sine):
    return pl.pallas_call(
        functools.partial(project_kernel, len(pieces)),
        grid_spec=pltpu.PrefetchScalarGridSpec(
            num_scalar_prefetch=1,
            grid=(TOKENS // TILE,),
            in_specs=[pl.BlockSpec(memory_space=pltpu.HBM)] * len(pieces)
            + [whole_of(D, WIDE), whole_of(1, WIDE), whole_of(4, D), tile_rows(BLOCK), tile_rows(BLOCK)],
            out_specs=[tile_rows(w) for w in (D, BLOCK, BLOCK, UNITS, UNITS)],
            scratch_shapes=[pltpu.VMEM((TOKENS, D), bf16), pltpu.SemaphoreType.DMA((CHIPS,))],
        ),
        out_shape=[pltpu.HBM((TOKENS, D), bf16)] + [out_rows(w) for w in (BLOCK, BLOCK, UNITS, UNITS)],
        compiler_params=pltpu.CompilerParams(vmem_limit_bytes=14 * MIB),
        cost_estimate=pl.CostEstimate(
            flops=2 * TOKENS * D * WIDE, bytes_accessed=12 * MIB, transcendentals=2 * TOKENS * UNITS
        ),
        name="project",
    )(order, *pieces, weight, shift, gains, cosine, sine)


def pull_back_kernel(count, order_ref, *refs):
    pieces, refs = (refs[:count], refs[count:])
    w_ref, slope_ref = refs[:2]
    do_ref, e_ref, g_ref, rows_ref, sems = refs[-5:]

    @pl.when(pl.program_id(0) == 0)
    def _():
        fetch_blocks(order_ref, pieces, rows_ref, sems)

    here = pl.ds(pl.multiple_of(pl.program_id(0) * TILE, TILE), TILE)
    grad = rows_ref[here, :]
    g_ref[...] = grad
    back = dot(grad, w_ref[...], LAST)
    e_ref[...] = (back[:, :UNITS] * slope_ref[...].astype(f32)).astype(bf16)
    do_ref[...] = back[:, UNITS:]


def pull_back(order, pieces, weight, slope, ties=()):
    return pl.pallas_call(
        functools.partial(pull_back_kernel, len(pieces)),
        grid_spec=pltpu.PrefetchScalarGridSpec(
            num_scalar_prefetch=1,
            grid=(TOKENS // TILE,),
            in_specs=[pl.BlockSpec(memory_space=pltpu.HBM)] * len(pieces)
            + [whole_of(UNITS + BLOCK, D), tile_rows(UNITS)]
            + unused(ties),
            out_specs=[tile_rows(w) for w in (BLOCK, UNITS, D)],
            scratch_shapes=[pltpu.VMEM((TOKENS, D), bf16), pltpu.SemaphoreType.DMA((CHIPS,))],
        ),
        out_shape=[jax.ShapeDtypeStruct((TOKENS, BLOCK), f32), out_rows(UNITS), pltpu.HBM((TOKENS, D), bf16)],
        compiler_params=pltpu.CompilerParams(vmem_limit_bytes=14 * MIB),
        cost_estimate=pl.CostEstimate(
            flops=2 * TOKENS * D * (UNITS + BLOCK), bytes_accessed=12 * MIB, transcendentals=0
        ),
        name="pull_back",
    )(order, *pieces, weight, slope, *ties)


def blocks_product_kernel(count, flipped, order_ref, *refs):
    w_ref, out_ref = (refs[count * SIDE], refs[-1])
    columns = [
        jnp.concatenate([refs[part * SIDE + block][...] for block in range(SIDE)], axis=0)
        for part in range(count)
    ]
    left = jnp.concatenate(columns, axis=1)
    out_ref[...] = dot(left, w_ref[...], LAST if flipped else None).astype(out_ref.dtype)


def blocks_product(parts, weight, order, flipped, dtype, ties=()):
    def block(width, which):
        return pl.BlockSpec((BLOCK, width), lambda i, order: (order[i * SIDE + which], 0))

    groups = order.shape[0] // SIDE
    depth = sum(part.shape[1] for part in parts)
    return pl.pallas_call(
        functools.partial(blocks_product_kernel, len(parts), flipped),
        grid_spec=pltpu.PrefetchScalarGridSpec(
            num_scalar_prefetch=1,
            grid=(groups,),
            in_specs=[block(part.shape[1], which) for part in parts for which in range(SIDE)]
            + [whole_of(*weight.shape)]
            + unused(ties),
            out_specs=pl.BlockSpec((SIDE * BLOCK, D), lambda i, order: (i, 0)),
        ),
        out_shape=jax.ShapeDtypeStruct((groups * SIDE * BLOCK, D), dtype),
        compiler_params=pltpu.CompilerParams(vmem_limit_bytes=10 * MIB),
        cost_estimate=pl.CostEstimate(
            flops=2 * groups * SIDE * BLOCK * depth * D, bytes_accessed=2 * MIB + groups * MIB, transcendentals=0
        ),
        name="blocks_product",
    )(order, *[part for part in parts for _ in range(SIDE)], weight, *ties)


def key_places(tile, core):
    row = lax.broadcasted_iota(jnp.int32, (WINDOW, 1), 0)
    return tile * (2 * WINDOW) + (row // BLOCK) * (2 * BLOCK) + core * BLOCK + row % BLOCK


def query_places(tile, core):
    row = lax.broadcasted_iota(jnp.int32, (1, WINDOW), 1)
    return tile * (2 * WINDOW) + (row // BLOCK) * (2 * BLOCK) + core * BLOCK + row % BLOCK


def turned(rows):
    return jnp.transpose(rows.astype(f32)).astype(bf16)


def attend_kernel(
    info_ref, q_ref, start_ref, own_ref, other_ref, o_ref, wide_ref, top_ref, over_ref, vt_ref
):
    tile = pl.program_id(0)
    core = info_ref[2 * (TOKENS // WINDOW)]

    @pl.when(tile == 0)
    def _():
        for part in range(TOKENS // BLOCK):
            rows = pl.ds(part * BLOCK, BLOCK)
            for which, ref in enumerate((own_ref, other_ref)):
                pair = turned(ref[rows, :])
                vt_ref[which, :, rows] = jnp.concatenate([pair[HD:], jnp.ones((16, BLOCK), bf16)], axis=0)

    query = q_ref[...]
    starts = start_ref[...]
    places = query_places(tile, core)

    def step(index, carry, masked):
        top, mixed = carry
        rows = pl.ds(pl.multiple_of(index * WINDOW, WINDOW), WINDOW)
        scores = [dot(ref[rows, :], query, LAST) * LOG2E for ref in (own_ref, other_ref)]
        if masked:
            allowed = []
            for which in range(2):
                keys = key_places(index, core if which == 0 else 1 - core)
                allowed.append((keys >= starts) & (keys <= places))
            scores = [jnp.where(a, s, -1e30) for a, s in zip(allowed, scores)]
        highest = jnp.max(jnp.maximum(scores[0], scores[1]), axis=0, keepdims=True)
        raised = jnp.maximum(top, jnp.ceil(highest))
        parts = [jnp.exp2(s - raised) for s in scores]
        if masked:
            parts = [jnp.where(a, p, 0.0) for a, p in zip(allowed, parts)]
        mixed = mixed * jnp.exp2(top - raised)
        for which in range(2):
            mixed = mixed + dot(vt_ref[which, :, rows], parts[which].astype(bf16))
        return (raised, mixed)

    carry = (jnp.full((1, WINDOW), -1e30, f32), jnp.zeros((HD + 16, WINDOW), f32))
    low, clear = (info_ref[tile], info_ref[TOKENS // WINDOW + tile])
    carry = lax.fori_loop(low, clear, functools.partial(step, masked=True), carry)
    carry = lax.fori_loop(clear, tile, functools.partial(step, masked=False), carry)
    top, mixed = step(tile, carry, True)
    over = 1.0 / mixed[HD : HD + 1]
    top_ref[...] = top
    over_ref[...] = over
    spare = (lax.broadcasted_iota(jnp.int32, (HD, WINDOW), 0) == 0).astype(f32)
    mixed = jnp.concatenate([spare, mixed[:HD] * over], axis=0)
    mixed = jnp.transpose(mixed)
    wide_ref[...] = mixed
    o_ref[...] = mixed.astype(bf16)


def attend(info, query, starts, own, other):
    rows = lambda width: pl.BlockSpec((WINDOW, width), lambda i, info: (i, 0))
    line = pl.BlockSpec((1, WINDOW), lambda i, info: (0, i))
    whole = pl.BlockSpec((TOKENS, BLOCK), lambda i, info: (0, 0))
    return pl.pallas_call(
        attend_kernel,
        grid_spec=pltpu.PrefetchScalarGridSpec(
            num_scalar_prefetch=1,
            grid=(TOKENS // WINDOW,),
            in_specs=[rows(BLOCK), line, whole, whole],
            out_specs=[rows(BLOCK), rows(BLOCK), line, line],
            scratch_shapes=[pltpu.VMEM((2, HD + 16, TOKENS), bf16)],
        ),
        out_shape=[
            jax.ShapeDtypeStruct((TOKENS, BLOCK), bf16),
            jax.ShapeDtypeStruct((TOKENS, BLOCK), f32),
            jax.ShapeDtypeStruct((1, TOKENS), f32),
            jax.ShapeDtypeStruct((1, TOKENS), f32),
        ],
        compiler_params=pltpu.CompilerParams(vmem_limit_bytes=24 * MIB),
        cost_estimate=pl.CostEstimate(
            flops=8 * TOKENS * TOKENS * BLOCK, bytes_accessed=4 * MIB, transcendentals=2 * TOKENS * TOKENS
        ),
        name="attend",
    )(info, query, starts, own, other)


def attend_back_kernel(
    info_ref, q_ref, do_ref, o_ref, top_ref, over_ref, start_ref, c_ref, s_ref, own_ref, other_ref, *refs
):
    dq_ref, down_ref, dother_low_ref, kt_ref, dother_ref = refs[-5:]
    tile = pl.program_id(0)
    core = info_ref[2 * (TOKENS // WINDOW)]

    @pl.when(tile == 0)
    def _():
        for part in range(TOKENS // BLOCK):
            rows = pl.ds(part * BLOCK, BLOCK)
            kt_ref[0, :, rows] = turned(own_ref[rows, :])[:HD]
            kt_ref[1, :, rows] = turned(other_ref[rows, :])[:HD]
        down_ref[...] = jnp.zeros_like(down_ref)
        dother_ref[...] = jnp.zeros_like(dother_ref)

    query = q_ref[...]
    top = top_ref[...]
    starts = start_ref[...]
    places = query_places(tile, core)
    turned_grad = (jnp.transpose(do_ref[...]) * over_ref[...]).astype(bf16).astype(f32)
    inner = jnp.sum(turned_grad * jnp.transpose(o_ref[...]), axis=0, keepdims=True)
    grad = jnp.transpose(turned_grad).astype(bf16)

    def step(index, carry, masked):
        rows = pl.ds(pl.multiple_of(index * WINDOW, WINDOW), WINDOW)
        for which, (ref, dref) in enumerate(((own_ref, down_ref), (other_ref, dother_ref))):
            pair = ref[rows, :]
            parts = jnp.exp2(dot(pair, query, LAST) * LOG2E - top)
            if masked:
                keys = key_places(index, core if which == 0 else 1 - core)
                allowed = (keys >= starts) & (keys <= places)
                parts = jnp.where(allowed, parts, 0.0)
            parts = parts.astype(bf16)
            changes = (parts.astype(f32) * (dot(pair, grad, LAST) - inner)).astype(bf16)
            dref[rows, :] += dot(changes, query) + dot(parts, grad)
            carry = carry + dot(kt_ref[which, :, rows], changes)
        return carry

    low, clear = (info_ref[tile], info_ref[TOKENS // WINDOW + tile])
    carry = jnp.zeros((HD, WINDOW), f32)
    carry = lax.fori_loop(low, clear, functools.partial(step, masked=True), carry)
    carry = lax.fori_loop(clear, tile, functools.partial(step, masked=False), carry)
    carry = step(tile, carry, True) * SCALE
    change = jnp.transpose(jnp.concatenate([carry, jnp.zeros((HD, WINDOW), f32)], axis=0))
    dq_ref[...] = (change * c_ref[...] - half_turn(change) * s_ref[...]).astype(bf16)

    @pl.when(tile == TOKENS // WINDOW - 1)
    def _():
        dother_low_ref[...] = dother_ref[...].astype(bf16)


def attend_back(info, query, grad, mixed, top, over, starts, cosine, sine, own, other, ties=()):
    rows = pl.BlockSpec((WINDOW, BLOCK), lambda i, info: (i, 0))
    line = pl.BlockSpec((1, WINDOW), lambda i, info: (0, i))
    whole = pl.BlockSpec((TOKENS, BLOCK), lambda i, info: (0, 0))
    return pl.pallas_call(
        attend_back_kernel,
        grid_spec=pltpu.PrefetchScalarGridSpec(
            num_scalar_prefetch=1,
            grid=(TOKENS // WINDOW,),
            in_specs=[rows, rows, rows, line, line, line, rows, rows, whole, whole] + unused(ties),
            out_specs=[rows, whole, whole],
            scratch_shapes=[pltpu.VMEM((2, HD, TOKENS), bf16), pltpu.VMEM((TOKENS, BLOCK), f32)],
        ),
        out_shape=[
            jax.ShapeDtypeStruct((TOKENS, BLOCK), bf16),
            jax.ShapeDtypeStruct((TOKENS, BLOCK), f32),
            jax.ShapeDtypeStruct((TOKENS, BLOCK), bf16),
        ],
        compiler_params=pltpu.CompilerParams(vmem_limit_bytes=28 * MIB),
        cost_estimate=pl.CostEstimate(
            flops=20 * TOKENS * TOKENS * BLOCK, bytes_accessed=6 * MIB, transcendentals=2 * TOKENS * TOKENS
        ),
        name="attend_back",
    )(info, query, grad, mixed, top, over, starts, cosine, sine, own, other, *ties)


def join_kernel(mine_ref, theirs_ref, c_ref, s_ref, out_ref):
    pair = mine_ref[...] + theirs_ref[...].astype(f32)
    out_ref[...] = (pair * c_ref[...] - half_turn(pair) * s_ref[...]).astype(bf16)


def join_pairs(mine, theirs, cosine, sine):
    rows = pl.BlockSpec((TOKENS // 2, BLOCK), lambda i: (i, 0))
    return pl.pallas_call(
        join_kernel,
        grid=(2,),
        in_specs=[rows] * 4,
        out_specs=rows,
        out_shape=jax.ShapeDtypeStruct((TOKENS, BLOCK), bf16),
        name="join_pairs",
    )(mine, theirs, cosine, sine)


def pack_kernel(info_ref, up_ref, sum_ref, grads_ref, keep_ref, send_ref):
    core = info_ref[2 * (TOKENS // WINDOW)]
    lane = lax.broadcasted_iota(jnp.int32, (1, BLOCK), 1)
    row = lax.broadcasted_iota(jnp.int32, (16, UNITS), 0)
    for out_ref, which in ((keep_ref, core), (send_ref, 1 - core)):
        for chip in range(CHIPS):
            at = chip * EARLY
            rows = pl.ds(pl.multiple_of(chip * 64 + which * 32, 32), 32)
            out_ref[at : at + 32, :] = up_ref[rows, :].astype(out_ref.dtype)
            sums = grads_ref[UNITS : UNITS + 8, pl.ds(chip // 2 * BLOCK, BLOCK)][:1]
            here = chip % 2 * 64
            first = pltpu.roll(sums, (BLOCK - here) % BLOCK, 1) if here else sums
            mine = jnp.where(which == 0, first, pltpu.roll(sums, BLOCK - here - 32, 1))
            mine = jnp.concatenate([jnp.where(lane < 32, mine, 0.0), jnp.zeros((1, BLOCK), f32)], axis=1)
            extra = jnp.where(row == 0, sum_ref[...], jnp.where(row == 1, mine, 0.0))
            out_ref[at + 32 : at + EARLY, :] = extra.astype(out_ref.dtype)
        heads = pl.ds(pl.multiple_of(UNITS + HD + which * 32, 32), 32)
        units = pl.ds(pl.multiple_of(which * BLOCK, BLOCK), BLOCK)
        for part in range(D // UNITS):
            at = CHIPS * EARLY + part * 160
            columns = pl.ds(part * UNITS, UNITS)
            out_ref[at : at + 32, :] = grads_ref[heads, columns].astype(out_ref.dtype)
            out_ref[at + 32 : at + 160, :] = grads_ref[units, columns].astype(out_ref.dtype)


def pack(info, up_grads, up_sum, grads):
    rows = CHIPS * EARLY + 160 * (D // UNITS)
    return pl.pallas_call(
        pack_kernel,
        grid_spec=pltpu.PrefetchScalarGridSpec(
            num_scalar_prefetch=1,
            grid=(1,),
            in_specs=[whole_of(D, UNITS), whole_of(1, UNITS), whole_of(UNITS + BLOCK, D)],
            out_specs=[whole_of(rows, UNITS), whole_of(rows, UNITS)],
        ),
        out_shape=[
            jax.ShapeDtypeStruct((rows, UNITS), f32),
            jax.ShapeDtypeStruct((rows, UNITS), bf16),
        ],
        compiler_params=pltpu.CompilerParams(vmem_limit_bytes=16 * MIB),
        cost_estimate=pl.CostEstimate(flops=4 * MIB, bytes_accessed=5 * MIB, transcendentals=0),
        name="pack",
    )(info, up_grads, up_sum, grads)


def finish_kernel(got_ref, qkv_ref, up_ref, norm_ref, qkv_out, up_out, qkv_sum_ref, up_sum_ref, norm_out):
    gain1, shift1, gain2, shift2 = (norm_ref[:, k : k + 1] for k in range(4))
    first = lax.broadcasted_iota(jnp.int32, (32, BLOCK), 1) < HD
    total = [jnp.zeros((32, 1), f32) for _ in range(4)]
    across = lambda values: jnp.sum(values, axis=1, keepdims=True)
    for chip in range(0, CHIPS, 2):
        tiles = [got_ref[chip + k, EARLY:, :].astype(f32) for k in range(2)]
        (low0, high0), (low1, high1) = ((t[:, :BLOCK], t[:, BLOCK:]) for t in tiles)
        turn = lambda values: pltpu.roll(values, HD, 1)
        cores = (
            jnp.where(first, low0, turn(low1)),
            jnp.where(first, high0, turn(high1)),
            jnp.where(first, turn(high0), high1),
        )
        notes = jnp.where(first, turn(low0), low1)
        for part, (core, row) in enumerate(zip(cores, (0, 2, 3))):
            at = pl.ds(part * D + chip * HD, BLOCK)
            sums = notes[row : row + 1]
            weight = qkv_ref[:, at].astype(f32)
            qkv_out[:, at] = gain1 * core + shift1 * sums
            qkv_sum_ref[:, at] = sums
            total[0] += across(weight * core)
            total[1] += across(weight * sums)
    for chip in range(CHIPS):
        at = pl.ds(chip * UNITS, UNITS)
        core = got_ref[chip, :32, :].astype(f32)
        sums = got_ref[chip, 32:EARLY, :].astype(f32)[:1]
        weight = up_ref[:, at].astype(f32)
        up_out[:, at] = gain2 * core + shift2 * sums
        up_sum_ref[:, at] = sums
        total[2] += across(weight * core)
        total[3] += across(weight * sums)
    lane = lax.broadcasted_iota(jnp.int32, (32, BLOCK), 1)
    out = jnp.zeros((32, BLOCK), f32)
    for k in range(4):
        out = jnp.where(lane == k, total[k], out)
    norm_out[...] = out


def finish(got, qkv_weight, up_weight, norms):
    shape = lambda *dims: jax.ShapeDtypeStruct(dims, f32)
    return pl.pallas_call(
        finish_kernel,
        out_shape=[shape(32, 3 * D), shape(32, FF), shape(1, 3 * D), shape(1, FF), shape(32, BLOCK)],
        compiler_params=pltpu.CompilerParams(vmem_limit_bytes=10 * MIB),
        cost_estimate=pl.CostEstimate(flops=8 * 32 * 7 * D, bytes_accessed=3 * MIB, transcendentals=0),
        name="finish",
    )(got, qkv_weight, up_weight, norms)


def on_device(
    inputs,
    segments,
    cotangent,
    qkv_weight,
    qkv_bias,
    dense_weight,
    dense_bias,
    fc_in_weight,
    fc_in_bias,
    fc_out_weight,
    fc_out_bias,
    norm1_gain,
    norm1_bias,
    norm2_gain,
    norm2_bias,
):
    section = lax.axis_index("section")
    place = lax.axis_index("shard")
    chip, core = (place // 2, place % 2)
    first_layer = section == 0
    x0 = lax.dynamic_index_in_dim(inputs, section, 0, keepdims=False)[0]
    out_grad = lax.dynamic_index_in_dim(cotangent, section, 0, keepdims=False)[0]
    my_segs = lax.dynamic_index_in_dim(segments, section, 0, keepdims=False)[0]

    x0_all = plane_gather(x0)
    grad1_all = plane_gather(out_grad)

    pieces = lambda vector: vector.astype(bf16).reshape(-1, 32)
    vectors = jnp.concatenate(
        [
            pieces(v[0])
            for v in (
                norm1_gain, norm1_bias, norm2_gain, norm2_bias, qkv_bias, fc_in_bias, dense_bias, fc_out_bias,
            )
        ]
    )
    vectors_away = section_swap(vectors)
    spare = jnp.concatenate([pieces(my_segs), vectors, vectors_away, jnp.zeros((2, 32), bf16)])
    spare = jnp.concatenate([spare[:16], spare[16:]], axis=1).reshape(1, 1, 16, HD)
    heads = qkv_weight[0].reshape(2, 16, 3, CHIPS, HD).transpose(3, 0, 1, 2, 4)
    units = fc_in_weight[0].reshape(2, 16, CHIPS, UNITS).transpose(2, 0, 1, 3)
    cut = jnp.concatenate(
        [
            heads[..., 0, :],
            jnp.broadcast_to(spare, (CHIPS, 2, 16, HD)),
            heads[..., 1, :],
            heads[..., 2, :],
            units,
        ],
        axis=-1,
    ).reshape(2 * CHIPS, 16, WIDE)
    got = lax.all_to_all(cut, "shard", 0, 0, tiled=True)
    notes = got[:, :, HD:BLOCK]
    notes = jnp.concatenate([notes[..., :32], notes[..., 32:]], axis=1)
    rows_own = jnp.concatenate([dense_weight[0], fc_out_weight[0]], axis=0)
    rows_away = section_swap(rows_own)
    got_away = section_swap(got)
    got_pair = jnp.stack([got, got_away])
    rows_pair = jnp.stack([rows_own, rows_away])
    got_other = core_swap(got_pair)
    rows_other = core_swap(rows_pair)

    def by_core(mine, theirs, axis):
        return jnp.where(
            core == 0, jnp.stack([mine, theirs], axis), jnp.stack([theirs, mine], axis)
        )

    columns_both = by_core(got_pair, got_other, 2).reshape(2, D, WIDE)
    head_rows = by_core(rows_pair[:, :32], rows_other[:, :32], 1).reshape(2, HD, D)
    unit_rows = by_core(rows_pair[:, 32:], rows_other[:, 32:], 1).reshape(2, UNITS, D)
    out_both = jnp.concatenate([unit_rows, jnp.zeros((2, HD, D), bf16), head_rows], axis=1)
    notes_both = (notes[:, 4:17], notes[:, 17:30])

    def layer_weights(layer):
        mine = first_layer == (layer == 0)
        pick = lambda both: jnp.where(mine, both[0], both[1])
        columns, note = (pick(columns_both).astype(f32), pick(notes_both))
        vector = lambda at, count: note[:, at : at + count].reshape(-1).astype(f32)
        gain1, shift1, gain2, shift2 = (vector(k, 1) for k in range(4))
        attn_bias = vector(4, 3).reshape(3, CHIPS, HD)
        attn_bias = lax.dynamic_index_in_dim(attn_bias, chip, 1, keepdims=False)
        up_bias = lax.dynamic_slice_in_dim(vector(7, 4), chip * UNITS, UNITS, 0)
        out_bias = vector(11, 1) + vector(12, 1)
        lane = jnp.arange(WIDE)
        gains = jnp.where(lane[None, :] < 2 * BLOCK, gain1[:, None], gain2[:, None])
        used = (lane < HD) | (lane >= BLOCK)
        bias = jnp.concatenate(
            [attn_bias[0], jnp.zeros((HD,), f32), attn_bias[1], attn_bias[2], up_bias]
        )
        shift = bias[None, :]
        plain = jnp.where(used[None, :], columns, 0.0).astype(bf16)
        scaled = jnp.where(used[None, :], columns * gains, 0.0).astype(bf16)
        lines = jnp.stack([gain1, shift1, gain2, shift2])
        return (plain, scaled, shift, lines, pick(out_both), out_bias)

    segs = notes[:, :4].astype(jnp.int32)
    numbers = jnp.arange(DOCS, dtype=jnp.int32)
    before = jnp.sum((segs.reshape(1, -1) < numbers[:, None]).astype(jnp.int32), axis=1)
    steps = before - jnp.concatenate([jnp.zeros((1,), jnp.int32), before[:-1]])
    my_rows = lax.dynamic_index_in_dim(
        segs.reshape(CHIPS, 2, BLOCK), core, 1, keepdims=False
    ).reshape(TOKENS)
    starts = jnp.sum(jnp.where(my_rows[None, :] >= numbers[:, None], steps[:, None], 0), axis=0)
    token = jnp.arange(TOKENS, dtype=jnp.int32)
    token = (token // BLOCK) * (2 * BLOCK) + core * BLOCK + token % BLOCK
    half_rot = ROT // 2
    frequency = jnp.exp(jnp.arange(half_rot, dtype=f32) * (-2.0 * math.log(10000.0) / ROT))
    angles = frequency[:, None] * (token - starts).astype(f32)[None, :]
    cos_rows, sin_rows = (jnp.cos(angles), jnp.sin(angles))
    ones = lambda count: jnp.ones((count, TOKENS), f32)
    zeros = lambda count: jnp.zeros((count, TOKENS), f32)
    cosine = jnp.concatenate([cos_rows, cos_rows, ones(BLOCK - ROT)], axis=0).T
    sine = jnp.concatenate([-sin_rows, sin_rows, zeros(BLOCK - ROT)], axis=0).T
    tiles = starts.reshape(TOKENS // WINDOW, WINDOW)
    low_tile = tiles[:, 0] // (2 * WINDOW)
    clear_tile = jnp.minimum(
        (tiles[:, -1] + 2 * WINDOW - 1) // (2 * WINDOW),
        jnp.arange(TOKENS // WINDOW, dtype=jnp.int32),
    )
    info = jnp.concatenate([low_tile, clear_tile, core[None], jnp.zeros((7,), jnp.int32)])
    start_line = starts[None, :]

    order = block_order(chip, core)
    straight = jnp.arange(CHIPS, dtype=jnp.int32)

    def forward(pieces, arranged, weights):
        plain, _, shift, lines, _, _ = weights
        normed, query, own, act, slope = project(
            arranged, pieces, plain, shift, lines, cosine, sine
        )
        other = core_swap(own)
        mixed, wide, top, over = attend(info, query, start_line, own, other)
        return (normed, query, own, other, act, slope, mixed, wide, top, over)

    def pulled(pieces, arranged, weights, kept, ties=()):
        return pull_back(arranged, pieces, weights[4], kept[5], ties)

    def by_owner(parts):
        return parts.reshape(CHIPS, 2, 32, parts.shape[-1])

    def early_grads(kept, changed, grad_all):
        up_grads = dot(kept[0], changed, FIRST)
        grads = dot(jnp.concatenate([kept[4], kept[6]], axis=1), grad_all, FIRST)
        up_sum = jnp.sum(changed.astype(f32), axis=0, keepdims=True)
        keep, send = pack(info, up_grads, up_sum, grads)
        return add(keep, core_swap(send)).astype(bf16)

    def over_cores(parts):
        keep, send = (
            jnp.concatenate(
                [lax.dynamic_index_in_dim(part, which, 0, keepdims=False) for part in parts]
            )
            for which in (core, 1 - core)
        )
        send = send.astype(bf16)
        return (add(keep, core_swap(send)), send)

    def attended(grad_mixed, kept, ties=()):
        _, query, own, other, _, _, _, wide, top, over = kept
        dq, d_own, d_other = attend_back(
            info, query, grad_mixed, wide, top, over, start_line, cosine, sine, own, other, ties
        )
        return (dq, join_pairs(d_own, core_swap(d_other), cosine, sine))

    def late_grads(normed, dq, d_pair):
        made = jnp.concatenate([dq, d_pair], axis=1)
        grads = by_owner(dot(normed, made, FIRST))
        sums = jnp.sum(made.astype(f32), axis=0).reshape(1, 1, 4, HD)
        extra = jnp.pad(jnp.broadcast_to(sums, (CHIPS, 2, 4, HD)), ((0, 0), (0, 0), (0, 28), (0, 0)))
        grads = jnp.concatenate([grads[..., :HD], extra, grads[..., BLOCK:]], axis=-1)
        return grads.transpose(1, 0, 2, 3).reshape(2, CHIPS * 32, 2 * BLOCK)

    def norm_back(rows, grad, summed):
        here, inverse = norm_rows(rows)
        inner_part = (
            summed
            - jnp.mean(summed, axis=-1, keepdims=True)
            - here * jnp.mean(summed * here, axis=-1, keepdims=True)
        )
        return (grad.astype(f32) + inverse * inner_part).astype(bf16)

    weights0, weights1 = (layer_weights(0), layer_weights(1))
    kept0 = forward((x0_all,), straight, weights0)
    ready = (weights0[1], weights1[0], weights1[1], weights1[2])
    summed, _, _ = scatter_rows((kept0[4], kept0[6]), weights0[4], order, False, (), ready)
    x1 = (add(x0, summed) + weights0[5][None, :]).astype(bf16)
    x1, grad1_all = lax.optimization_barrier((x1, grad1_all))
    kept1 = forward(gather_rows(x1), order, weights1)
    grad_mixed, changed1, grad1_all = pulled((grad1_all,), straight, weights1, kept1)
    dq1, d_pair1 = attended(grad_mixed, kept1)
    inner = jnp.concatenate([kept1[4], after(kept1[6], dq1)], axis=1)
    summed = plane_scatter(dot(inner, weights1[4]).astype(bf16))
    x2 = (add(x1, summed) + weights1[5][None, :]).astype(bf16)
    summed, _, _ = scatter_rows((dq1, d_pair1, changed1), weights1[1], order, True)
    grad1 = norm_back(x1, out_grad, summed)
    early1 = early_grads(kept1, changed1, grad1_all)
    late1, _ = over_cores([late_grads(kept1[0], dq1, d_pair1)])
    layer1 = jnp.concatenate([late1.astype(bf16), early1])
    half1 = add(layer1, section_swap(layer1)).astype(bf16)
    layer1 = add(half1, cross(half1, 1)).astype(bf16)

    grad_mixed, changed0, grad0_all = pulled(
        gather_rows(grad1), order, weights0, kept0, (half1,)
    )
    early0 = early_grads(kept0, changed0, grad0_all)
    dq0, d_pair0 = attended(grad_mixed, kept0, (x2, layer1))
    late0, send = over_cores([late_grads(kept0[0], dq0, d_pair0)])
    summed, held, step = scatter_rows(
        (dq0, d_pair0, changed0), weights0[1], order, True, (send,)
    )
    half0 = add(after(early0, held), section_swap(early0)).astype(bf16)
    early0 = add(after(half0, step), cross(half0, 0)).astype(bf16)
    grad0 = norm_back(x0, grad1, summed)

    def placed(layer0, layer1):
        mine = jnp.where(first_layer, layer0, layer1)
        theirs = section_swap(jnp.where(first_layer, layer1, layer0))
        return jnp.where(
            first_layer, jnp.stack([mine, theirs]), jnp.stack([theirs, mine])
        )[None, :, None]

    section_outputs = placed(x1, x2)
    input_grads = placed(grad0, grad1)

    late0 = late0.astype(bf16)
    half0 = add(late0, section_swap(late0)).astype(bf16)
    late0 = add(half0, cross(half0, 0))
    late0 = after(late0, step).astype(bf16)
    parts = jnp.where(first_layer, jnp.concatenate([late0, early0]), layer1)
    late, early, rows = jnp.split(parts, [CHIPS * 32, CHIPS * (32 + EARLY)])
    row_sum = jnp.concatenate(jnp.split(rows, D // UNITS), axis=1).astype(f32)
    parts = jnp.concatenate([part.reshape(CHIPS, -1, UNITS) for part in (early, late)], axis=1)
    got = lax.all_to_all(parts, "shard", 0, 0, tiled=True, axis_index_groups=SAME_CORE)
    column = lambda vector: vector[0].astype(f32)[:, None]
    norms = jnp.concatenate([column(v) for v in (norm1_gain, norm1_bias, norm2_gain, norm2_bias)], axis=1)
    qkv_grad, up_grad, qkv_sum, up_sum, norm_grads = finish(got, qkv_weight[0], fc_in_weight[0], norms)
    shift_grad = got[0, 33, :32].astype(f32)
    mine_of = lambda vector, at, width: lax.dynamic_slice_in_dim(
        vector, at + place * width, width, 1
    )
    return (
        section_outputs,
        input_grads,
        qkv_grad[None],
        mine_of(qkv_sum[:, : 2 * D], 0, 64),
        mine_of(qkv_sum[:, 2 * D :], 0, 32),
        row_sum[None, :32],
        shift_grad[None],
        up_grad[None],
        mine_of(up_sum, 0, 128),
        row_sum[None, 32:],
        shift_grad[None],
        *(norm_grads[:, k][None] for k in range(4)),
    )


def solution(mesh):
    rows = P(None, "rep", "shard", None)
    outs = P("section", None, "rep", "shard", None)
    matrix = P("section", "shard", None)
    vector = P("section", "shard")
    return jax.shard_map(
        on_device,
        mesh=mesh,
        in_specs=(
            rows, P(None, "rep", "shard"), rows, matrix, vector, matrix, vector, matrix, vector, matrix,
            vector, vector, vector, vector, vector,
        ),
        out_specs=(
            outs, outs, matrix, vector, vector, matrix, vector, matrix, vector, matrix, vector, vector,
            vector, vector, vector,
        ),
        check_vma=False,
    )
```
